32 devices in a mesh: segment: 2 (over core), dp: 16 (over z, y, x).
Axes of the slice: x: 2, y: 2, z: 4, core: 2. Of those that a mesh axis runs over, the one named last changes fastest.
Arguments:
- inputs: bfloat16 [2, 96, 197, 384], P(None, 'dp'), may hold values from -6 to 6
- image_count: int32 [2, 16], P(None, 'dp'), may hold values from 1 to 6, as said below
- cotangent: bfloat16 [2, 96, 197, 384], P(None, 'dp'), may hold values from -6 to 6
- ln1_gain: float32 [2, 384], P('segment'), may hold values from 0.1 to 1.9
- ln1_bias: float32 [2, 384], P('segment'), may hold values from -3 to 3
- w_qkv: bfloat16 [2, 384, 1152], P('segment'), may hold values from -0.4375 to 0.4375
- bias_qv: float32 [2, 768], P('segment'), may hold values from -3 to 3
- w_out: bfloat16 [2, 384, 384], P('segment'), may hold values from -0.625 to 0.625
- b_out: float32 [2, 384], P('segment'), may hold values from -3 to 3
- ln2_gain: float32 [2, 384], P('segment'), may hold values from 0.1 to 1.9
- ln2_bias: float32 [2, 384], P('segment'), may hold values from -3 to 3
- w_up: bfloat16 [2, 384, 1536], P('segment'), may hold values from -0.3125 to 0.3125
- b_up: float32 [2, 1536], P('segment'), may hold values from -4 to 4
- w_down: bfloat16 [2, 1536, 384], P('segment'), may hold values from -0.21875 to 0.21875
- b_down: float32 [2, 384], P('segment'), may hold values from -3 to 3
Outputs:
- activations: bfloat16 [2, 2, 96, 197, 384], P('segment', None, 'dp')
- input_grads: bfloat16 [2, 2, 96, 197, 384], P('segment', None, 'dp')
- ln1_gain_grad: float32 [2, 384], P('segment', 'dp')
- ln1_bias_grad: float32 [2, 384], P('segment', 'dp')
- w_qkv_grad: float32 [2, 384, 1152], P('segment', 'dp')
- bias_qv_grad: float32 [2, 768], P('segment', 'dp')
- w_out_grad: float32 [2, 384, 384], P('segment', 'dp')
- b_out_grad: float32 [2, 384], P('segment', 'dp')
- ln2_gain_grad: float32 [2, 384], P('segment', 'dp')
- ln2_bias_grad: float32 [2, 384], P('segment', 'dp')
- w_up_grad: float32 [2, 384, 1536], P('segment', 'dp')
- b_up_grad: float32 [2, 1536], P('segment', 'dp')
- w_down_grad: float32 [2, 1536, 384], P('segment', 'dp')
- b_down_grad: float32 [2, 384], P('segment', 'dp')
The draws below stay inside these ranges and needn't reach their ends.
Inputs may be any that keep to these rules, and one draw needn't show every extreme that they name: Images of micro-batch m held by data rank r fill its slots below image_count[m, r]; higher slots hold no image. In each micro-batch some rank holds 6.
All inputs are finite; a program needn't handle non-finite values.
Results may differ from the reference program's by a relative error of at most 0.02.
The reference program's roundings to bfloat16 on the way count: a program that leaves them out, or rounds other values in their place, can miss the bound.
Values may be sent and summed in bfloat16 or wider, within the bound.
No kernel may reach another device: no remote copies, remote signals or barrier semaphores. Data moves between devices by JAX's collectives and lax.ppermute only.
A program may use at most 192 MiB of HBM per device.

```python
import jax
import jax.numpy as jnp
from jax import lax

D = 384
HEAD = 64
FF = 1536
SEQ = 197
MICRO = 2
SLOTS = 6
IMG = 96
N_DP = 16


def draw_image_count(key, part):
    key = jax.random.fold_in(key, 7)
    counts_key, full_key = jax.random.split(key)
    counts = jax.random.randint(counts_key, (MICRO, N_DP), 1, SLOTS + 1)
    full_rank = jax.random.randint(full_key, (MICRO, 1), 0, N_DP)
    ranks = jnp.arange(N_DP)[None, :]
    return jnp.where(ranks == full_rank, SLOTS, counts).astype(jnp.int32)


def block_scale(key, dims, shards, low, top_value):
    loudness = 1.0
    for axis_at, blocks in shards:
        heights = jax.random.uniform(jax.random.fold_in(jax.random.fold_in(key, 6), axis_at), (blocks,), jnp.float32, low / len(shards), top_value / len(shards))
        loudness = loudness * jnp.repeat(jnp.exp(heights), dims[axis_at] // blocks).reshape((-1,) + (1,) * (len(dims) - 1 - axis_at))
    return loudness


def normal_values(stream_key, extent, scale, most, cuts=(), kind=jnp.bfloat16):
    values = scale * jax.random.normal(stream_key, extent, jnp.float32)
    if cuts:
        values = values * block_scale(stream_key, extent, cuts, -0.22, 0.18)
    return jnp.clip(values, -most, most).astype(kind)


def setup_inputs(seed: int = 0) -> dict:
    seeds = jax.random.split(jax.random.key(seed), 16)
    inputs = normal_values(seeds[0], (MICRO, IMG, SEQ, D), 1.0, 6.0, ((1, 16),))
    image_count = draw_image_count(jax.random.fold_in(seeds[15], 71), 0)
    cotangent = normal_values(seeds[2], (MICRO, IMG, SEQ, D), 1.0, 6.0, ((1, 16),))
    ln1_gain = jnp.clip(1.0 + 0.18 * jax.random.normal(seeds[3], (2, D), jnp.float32), 0.1, 1.9)
    ln1_bias = normal_values(seeds[4], (2, D), 0.3, 3.0, ((0, 2),), jnp.float32)
    w_qkv = normal_values(seeds[5], (2, D, 3 * D), (D // 2) ** -0.5, 0.4375, ((0, 2),))
    bias_qv = normal_values(seeds[6], (2, 2 * D), 0.3, 3.0, ((0, 2),), jnp.float32)
    w_out = normal_values(seeds[7], (2, D, D), (D // 4) ** -0.5, 0.625, ((0, 2),))
    b_out = normal_values(seeds[8], (2, D), 0.3, 3.0, ((0, 2),), jnp.float32)
    ln2_gain = jnp.clip(1.0 + 0.18 * jax.random.normal(seeds[9], (2, D), jnp.float32), 0.1, 1.9)
    ln2_bias = normal_values(seeds[10], (2, D), 0.3, 3.0, ((0, 2),), jnp.float32)
    w_up = normal_values(seeds[11], (2, D, FF), D ** -0.5, 0.3125, ((0, 2),))
    b_up = normal_values(seeds[12], (2, FF), 0.5, 4.0, ((0, 2),), jnp.float32)
    w_down = normal_values(seeds[13], (2, FF, D), (FF // 2) ** -0.5, 0.21875, ((0, 2),))
    b_down = normal_values(seeds[14], (2, D), 0.3, 3.0, ((0, 2),), jnp.float32)
    return dict(inputs=inputs, image_count=image_count, cotangent=cotangent, ln1_gain=ln1_gain, ln1_bias=ln1_bias, w_qkv=w_qkv, bias_qv=bias_qv, w_out=w_out, b_out=b_out, ln2_gain=ln2_gain, ln2_bias=ln2_bias, w_up=w_up, b_up=b_up, w_down=w_down, b_down=b_down)


@jax.custom_vjp
def low(v):
    return lax.optimization_barrier(v.astype(jnp.bfloat16)).astype(jnp.float32)

@jax.custom_vjp
def low_back(v):
    return v

def low_keep(v):
    return (low(v), None)

def low_pass(kept, grad):
    return (grad,)

def back_keep(v):
    return (v, None)

def back_low(kept, grad):
    return (low(grad),)
low.defvjp(low_keep, low_pass)
low_back.defvjp(back_keep, back_low)
highest = lax.Precision.HIGHEST
epsilon = 1e-06

def norm_rows(rows, gain, shift):
    centered = rows - lax.optimization_barrier(jnp.mean(rows, axis=-1, keepdims=True))
    spread = lax.optimization_barrier(jnp.mean(centered * centered, axis=-1, keepdims=True))
    return centered * lax.rsqrt(spread + epsilon) * gain + shift

def layer(params, hidden):
    ln1_gain, ln1_bias, w_qkv, bias_qv, w_out, b_out, ln2_gain, ln2_bias, w_up, b_up, w_down, b_down = params
    images, tokens, features = hidden.shape
    head_count = features // HEAD
    normed = low(norm_rows(hidden, ln1_gain, ln1_bias))
    bias_full = jnp.concatenate([bias_qv[:features], jnp.zeros((features,), jnp.float32), bias_qv[features:]])
    joined = jnp.einsum('nsd,de->nse', normed, w_qkv, precision=highest) + bias_full
    joined = low_back(low(joined)).reshape(images, tokens, 3, head_count, HEAD)
    scores = jnp.einsum('nqhc,nkhc->nhqk', joined[:, :, 0], joined[:, :, 1], precision=highest)
    scores = low_back(scores * HEAD ** (-0.5))
    weights = low(jax.nn.softmax(scores, axis=-1))
    attended = jnp.einsum('nhqk,nkhc->nqhc', weights, joined[:, :, 2], precision=highest)
    attended = low_back(low(attended.reshape(images, tokens, features)))
    branch = low_back(jnp.einsum('nsd,de->nse', attended, w_out, precision=highest) + b_out)
    middle = hidden + branch
    second_norm = low(norm_rows(middle, ln2_gain, ln2_bias))
    before = low_back(jnp.einsum('nsd,df->nsf', second_norm, w_up, precision=highest) + b_up)
    active = low(jax.nn.gelu(before, approximate=False))
    mlp_branch = low_back(jnp.einsum('nsf,fd->nsd', active, w_down, precision=highest) + b_down)
    return middle + mlp_branch

def apply_layer(params, stack):
    blocks = stack.reshape(N_DP, SLOTS, SEQ, D)
    result = lax.map(jax.checkpoint(lambda block: layer(params, block)), blocks)
    return result.reshape(stack.shape)

def reference(inputs, image_count, cotangent, ln1_gain, ln1_bias, w_qkv, bias_qv, w_out, b_out, ln2_gain, ln2_bias, w_up, b_up, w_down, b_down):
    stacked = [arg.astype(jnp.float32) for arg in (ln1_gain, ln1_bias, w_qkv, bias_qv, w_out, b_out, ln2_gain, ln2_bias, w_up, b_up, w_down, b_down)]
    first_params = [arg[0] for arg in stacked]
    second_params = [arg[1] for arg in stacked]
    slot_ids = jnp.arange(IMG, dtype=jnp.int32) % SLOTS
    valid = (slot_ids[None, :] < jnp.repeat(image_count, SLOTS, axis=1)).astype(jnp.float32)[:, :, None, None]
    start = inputs.astype(jnp.float32)
    probe = jnp.zeros(start.shape, jnp.float32)

    def whole(first_set, second_set, start_rows, probe_rows):
        middles = []
        finals = []
        for batch in range(MICRO):
            middle = apply_layer(first_set, start_rows[batch]) * valid[batch]
            passed = low_back(low(middle) + probe_rows[batch])
            finals.append(apply_layer(second_set, passed) * valid[batch])
            middles.append(middle)
        return (jnp.stack(finals), jnp.stack(middles))
    finals, pullback, middles = jax.vjp(whole, first_params, second_params, start, probe, has_aux=True)
    grad_first, grad_second, grad_start, grad_probe = pullback(cotangent.astype(jnp.float32))
    activations = jnp.stack([middles, finals]).astype(jnp.bfloat16)
    input_grads = jnp.stack([grad_start, grad_probe]).astype(jnp.bfloat16)
    grads = [jnp.stack([former, latter]) for former, latter in zip(grad_first, grad_second)]
    return (activations, input_grads, grads[0], grads[1], grads[2], grads[3], grads[4], grads[5], grads[6], grads[7], grads[8], grads[9], grads[10], grads[11])
```

```python
import jax
import jax.numpy as jnp
from jax import lax
from jax.experimental import pallas as pl
from jax.experimental.pallas import tpu as pltpu
from jax.sharding import PartitionSpec as P

HEAD = 64
EPSILON = 1e-06
BF16 = jnp.bfloat16
F32 = jnp.float32
GROUP = 2
VMEM_LIMIT = 58 * 1024 * 1024


def dot(a, b):
    return lax.dot_general(a, b, (((1,), (0,)), ((), ())), preferred_element_type=F32)


def dot_nt(a, b):
    return lax.dot_general(a, b, (((1,), (1,)), ((), ())), preferred_element_type=F32)


def dot_tn(a, b):
    return lax.dot_general(a, b, (((0,), (0,)), ((), ())), preferred_element_type=F32)


def normalized(rows):
    centered = rows - jnp.mean(rows, axis=-1, keepdims=True)
    spread = jnp.mean(centered * centered, axis=-1, keepdims=True)
    inverse = lax.rsqrt(spread + EPSILON)
    return centered * inverse, inverse


def norm_backward(rows, grad, gain):
    hat, inverse = normalized(rows)
    scaled = grad * gain
    inner = jnp.mean(scaled * hat, axis=-1, keepdims=True)
    dx = inverse * (scaled - jnp.mean(scaled, axis=-1, keepdims=True) - hat * inner)
    return dx, grad * hat


def gelu_and_slope(x):
    bell = jnp.exp(x * x * -0.5)
    t = 1.0 / (1.0 + jnp.abs(x) * (0.3275911 * 0.7071067811865476))
    poly = t * (
        0.5 * 0.254829592
        + t
        * (
            0.5 * -0.284496736
            + t * (0.5 * 1.421413741 + t * (0.5 * -1.453152027 + t * (0.5 * 1.061405429)))
        )
    )
    tail = poly * bell
    cdf = jnp.where(x >= 0.0, 1.0 - tail, tail)
    return x * cdf, cdf + x * (bell * 0.3989422804014327)


def fold(rows):
    total = rows[0:8]
    for at in range(8, rows.shape[0], 8):
        total = total + rows[at : at + 8]
    return total


def row_chunks(total, size=32):
    return [(at, min(size, total - at)) for at in range(0, total, size)]


def forward_kernel(
    padded,
    keys,
    meta,
    h_ref,
    gain1,
    bias1,
    w_qkv,
    b_qkv,
    w_out,
    b_out,
    gain2,
    bias2,
    w_up,
    b_up,
    w_down,
    b_down,
    act_ref,
    normed_ref,
    joined_ref,
    p_ref,
    attended_ref,
    middle_ref,
    second_ref,
    active_ref,
    slope_ref,
    hidden,
    before,
):
    step = pl.program_id(0)
    count = meta[0]
    tokens, features = h_ref.shape[2:]
    heads = features // HEAD
    rows = GROUP * padded
    hidden_units = w_up.shape[1]

    @pl.when(step * GROUP >= count)
    def _():
        act_ref[...] = jnp.zeros_like(act_ref)

    @pl.when(step * GROUP < count)
    def _():
        for j in range(GROUP):
            hidden[j * padded + padded - 16 : (j + 1) * padded] = jnp.zeros((16, features), F32)
            hidden[j * padded : j * padded + tokens] = h_ref[0, j].astype(F32)
        for at, size in row_chunks(rows):
            hat, _ = normalized(hidden[at : at + size])
            normed_ref[at : at + size] = (hat * gain1[...] + bias1[...]).astype(BF16)
        for j in range(GROUP):
            lines = normed_ref[j * padded : (j + 1) * padded]
            for part in range(3):
                columns = slice(part * features, (part + 1) * features)
                value = (dot(lines, w_qkv[:, columns]) + b_qkv[:, columns]).astype(BF16)
                if part == 0:
                    value = value * jnp.asarray(HEAD**-0.5, BF16)
                joined_ref[j * keys : j * keys + padded, columns] = value
            joined_ref[j * keys + padded : (j + 1) * keys] = jnp.zeros(
                (keys - padded, 3 * features), BF16
            )
        lane = lax.broadcasted_iota(jnp.int32, (padded, 2 * HEAD), 1)
        real = lax.broadcasted_iota(jnp.int32, (padded, keys), 1) < tokens
        for j in range(GROUP):
            for pair in range(heads // 2):
                at = pair * 2 * HEAD
                q = joined_ref[j * keys : j * keys + padded, at : at + 2 * HEAD]
                k = joined_ref[j * keys : (j + 1) * keys, features + at : features + at + 2 * HEAD]
                v = joined_ref[
                    j * keys : (j + 1) * keys, 2 * features + at : 2 * features + at + 2 * HEAD
                ]
                parts = []
                for half in range(2):
                    mine = (lane < HEAD) if half == 0 else (lane >= HEAD)
                    s = dot_nt(jnp.where(mine, q, jnp.zeros_like(q)), k)
                    s = jnp.where(real, s, -1e30)
                    e = jnp.exp(s - jnp.max(s, axis=-1, keepdims=True))
                    p = (e * (1.0 / jnp.sum(e, axis=-1, keepdims=True))).astype(BF16)
                    p_ref[j, 2 * pair + half] = p
                    parts.append(dot(p, v))
                attended_ref[j * padded : (j + 1) * padded, at : at + 2 * HEAD] = jnp.where(
                    lane < HEAD, parts[0], parts[1]
                ).astype(BF16)
        middle_ref[...] = dot(attended_ref[...], w_out[...])
        for at, size in row_chunks(rows):
            middle = middle_ref[at : at + size] + hidden[at : at + size] + b_out[...]
            middle_ref[at : at + size] = middle
            hat, _ = normalized(middle)
            second_ref[at : at + size] = (hat * gain2[...] + bias2[...]).astype(BF16)
        width = features
        for j in range(GROUP):
            lines = slice(j * padded, (j + 1) * padded)
            for c in range(hidden_units // width):
                columns = slice(c * width, (c + 1) * width)
                before[lines, columns] = dot(second_ref[lines], w_up[:, columns])
                for at, size in row_chunks(padded, 16):
                    piece = slice(j * padded + at, j * padded + at + size)
                    active, slope = gelu_and_slope(before[piece, columns] + b_up[:, columns])
                    active_ref[piece, columns] = active.astype(BF16)
                    slope_ref[piece, columns] = slope.astype(BF16)
            hidden[lines] = dot(active_ref[lines], w_down[...])
        for j in range(GROUP):
            keep = jnp.where(step * GROUP + j < count, 1.0, 0.0)
            lines = slice(j * padded, (j + 1) * padded)
            result = (hidden[lines] + middle_ref[lines] + b_down[...]) * keep
            act_ref[0, j] = result[:tokens].astype(BF16)


def mlp_backward_kernel(
    padded,
    meta,
    grad_ref,
    active_ref,
    slope_ref,
    second_ref,
    middle_ref,
    gain2,
    w_up,
    w_down,
    grad_middle_ref,
    up_ref,
    down_ref,
    vec_ref,
    grad_out,
    down_in,
    grad_before,
    grad_norm,
    sum_up,
    sum_down,
    vec_one,
    vec_up,
):
    step = pl.program_id(0)
    count = meta[0]
    tokens, features = grad_ref.shape[2:]
    rows = GROUP * padded
    hidden_units = w_up.shape[1]

    @pl.when(step == 0)
    def _():
        for ref in (sum_up, sum_down, vec_one, vec_up):
            ref[...] = jnp.zeros_like(ref)

    @pl.when(step * GROUP < count)
    def _():
        for j in range(GROUP):
            keep = jnp.where(step * GROUP + j < count, 1.0, 0.0)
            value = grad_ref[0, j].astype(F32) * keep
            grad_out[j * padded + padded - 16 : (j + 1) * padded] = jnp.zeros((16, features), F32)
            grad_out[j * padded : j * padded + tokens] = value
        for at, size in row_chunks(rows):
            value = grad_out[at : at + size]
            down_in[at : at + size] = value.astype(BF16)
            vec_one[0:8] += fold(value)
        width = features
        sum_down[...] += dot_tn(down_in[...], active_ref[...])
        for j in range(GROUP):
            lines = slice(j * padded, (j + 1) * padded)
            for c in range(hidden_units // width):
                columns = slice(c * width, (c + 1) * width)
                piece = dot_nt(down_in[lines], w_down[columns, :])
                piece = (piece * slope_ref[lines, columns].astype(F32)).astype(BF16)
                grad_before[lines, columns] = piece
                vec_up[:, columns] += fold(piece.astype(F32))
            grad_norm[lines] = dot_nt(grad_before[lines], w_up[...])
        sum_up[...] += dot_tn(second_ref[...], grad_before[...])
        for at, size in row_chunks(rows):
            grad = grad_norm[at : at + size]
            dx, by_hat = norm_backward(middle_ref[at : at + size], grad, gain2[...])
            vec_one[8:16] += fold(by_hat)
            vec_one[16:24] += fold(grad)
            grad_middle_ref[at : at + size] = grad_out[at : at + size] + dx

    @pl.when(step == pl.num_programs(0) - 1)
    def _():
        for c in range(hidden_units // features):
            columns = slice(c * features, (c + 1) * features)
            up_ref[c] = sum_up[:, columns].astype(BF16)
            down_ref[columns, :] = sum_down[:, columns].T.astype(BF16)
        vec_ref[...] = jnp.zeros_like(vec_ref)
        vec_ref[0:1, :hidden_units] = jnp.sum(vec_up[...], axis=0, keepdims=True)
        for n in range(3):
            vec_ref[n + 1 : n + 2, :features] = jnp.sum(
                vec_one[8 * n : 8 * n + 8], axis=0, keepdims=True
            )


def attention_backward_kernel(
    padded,
    keys,
    meta,
    grad_middle_ref,
    h_ref,
    normed_ref,
    joined_ref,
    p_ref,
    attended_ref,
    gain1,
    w_qkv,
    w_out,
    grad_ref,
    big_ref,
    vec_ref,
    hidden,
    out_in,
    grad_attended,
    grad_joined,
    grad_norm,
    sums,
    vec_one,
    vec_qkv,
):
    step = pl.program_id(0)
    count = meta[0]
    tokens, features = h_ref.shape[2:]
    heads = features // HEAD
    rows = GROUP * padded

    @pl.when(step == 0)
    def _():
        for ref in (sums, vec_one, vec_qkv):
            ref[...] = jnp.zeros_like(ref)

    @pl.when(step * GROUP >= count)
    def _():
        grad_ref[...] = jnp.zeros_like(grad_ref)

    @pl.when(step * GROUP < count)
    def _():
        for j in range(GROUP):
            hidden[j * padded + padded - 16 : (j + 1) * padded] = jnp.zeros((16, features), F32)
            hidden[j * padded : j * padded + tokens] = h_ref[0, j].astype(F32)
        for at, size in row_chunks(rows):
            value = grad_middle_ref[at : at + size].astype(BF16)
            out_in[at : at + size] = value
            vec_one[0:8] += fold(value.astype(F32))
        sums[:, 3 * features :] += dot_tn(attended_ref[...], out_in[...])
        grad_attended[...] = dot_nt(out_in[...], w_out[...]).astype(BF16)
        lane = lax.broadcasted_iota(jnp.int32, (padded, 2 * HEAD), 1)
        for j in range(GROUP):
            lines = slice(j * padded, (j + 1) * padded)
            for pair in range(heads // 2):
                at = pair * 2 * HEAD
                q = joined_ref[j * keys : j * keys + padded, at : at + 2 * HEAD]
                k = joined_ref[j * keys : (j + 1) * keys, features + at : features + at + 2 * HEAD]
                v = joined_ref[
                    j * keys : (j + 1) * keys, 2 * features + at : 2 * features + at + 2 * HEAD
                ]
                ga = grad_attended[lines, at : at + 2 * HEAD]
                gq, gk, gv = [], [], []
                for half in range(2):
                    mine = (lane < HEAD) if half == 0 else (lane >= HEAD)
                    gp = dot_nt(jnp.where(mine, ga, jnp.zeros_like(ga)), v)
                    p = p_ref[j, 2 * pair + half]
                    wide = p.astype(F32)
                    by = wide * gp
                    gs = (by - wide * jnp.sum(by, axis=-1, keepdims=True)).astype(BF16)
                    gq.append(dot(gs, k))
                    gk.append(dot_tn(gs, q)[:padded])
                    gv.append(dot_tn(p, ga)[:padded])
                left = lane < HEAD
                parts = (
                    jnp.where(left, gq[0], gq[1]) * HEAD**-0.5,
                    jnp.where(left, gk[0], gk[1]),
                    jnp.where(left, gv[0], gv[1]),
                )
                for n, part in enumerate(parts):
                    column = n * features + at
                    part = part.astype(BF16)
                    grad_joined[lines, column : column + 2 * HEAD] = part
                    vec_qkv[:, column : column + 2 * HEAD] += fold(part.astype(F32))
        sums[:, : 3 * features] += dot_tn(normed_ref[...], grad_joined[...])
        grad_norm[...] = dot_nt(grad_joined[...], w_qkv[...])
        for at, size in row_chunks(rows):
            grad = grad_norm[at : at + size]
            dx, by_hat = norm_backward(hidden[at : at + size], grad, gain1[...])
            vec_one[8:16] += fold(by_hat)
            vec_one[16:24] += fold(grad)
            hidden[at : at + size] = grad_middle_ref[at : at + size] + dx
        for j in range(GROUP):
            grad_ref[0, j] = hidden[j * padded : j * padded + tokens].astype(BF16)

    @pl.when(step == pl.num_programs(0) - 1)
    def _():
        big_ref[...] = sums[...].astype(BF16)
        vec_ref[...] = jnp.zeros_like(vec_ref)
        vec_ref[0:1, : 3 * features] = jnp.sum(vec_qkv[...], axis=0, keepdims=True)
        for n in range(3):
            vec_ref[n + 1 : n + 2, :features] = jnp.sum(
                vec_one[8 * n : 8 * n + 8], axis=0, keepdims=True
            )


def whole(shape):
    return pl.BlockSpec(shape, lambda i, meta: (0,) * len(shape))


def lines_of(shape):
    return pl.BlockSpec(shape, lambda i, meta: (i,) + (0,) * (len(shape) - 1))


def images_of(micro_shape):
    tokens, features = micro_shape[2:]
    return pl.BlockSpec((1, GROUP, tokens, features), lambda i, meta: (meta[1], i, 0, 0))


def call(body, meta, args, arg_specs, outs, out_specs, scratch, flops):
    return pl.pallas_call(
        body,
        grid_spec=pltpu.PrefetchScalarGridSpec(
            num_scalar_prefetch=1,
            grid=(args[0][1],),
            in_specs=arg_specs,
            out_specs=out_specs,
            scratch_shapes=scratch,
        ),
        out_shape=outs,
        compiler_params=pltpu.CompilerParams(
            vmem_limit_bytes=VMEM_LIMIT, dimension_semantics=("arbitrary",)
        ),
        cost_estimate=pl.CostEstimate(flops=flops, bytes_accessed=20_000_000, transcendentals=0),
    )(meta, *args[1:])


def struct(shape, kind):
    return jax.ShapeDtypeStruct(shape, kind)


def sizes(images):
    slots, tokens, features = images.shape[1:]
    padded = -(-tokens // 16) * 16
    keys = -(-tokens // 128) * 128
    return slots, tokens, features, padded, keys


def forward(meta, images, params):
    slots, tokens, features, padded, keys = sizes(images)
    heads = features // HEAD
    steps = slots // GROUP
    rows = slots * padded
    units = params[8].shape[1]
    outs = [
        (struct((1, slots, tokens, features), BF16), None),
        (struct((rows, features), BF16), (GROUP * padded, features)),
        (struct((slots * keys, 3 * features), BF16), (GROUP * keys, 3 * features)),
        (struct((slots, heads, padded, keys), BF16), (GROUP, heads, padded, keys)),
        (struct((rows, features), BF16), (GROUP * padded, features)),
        (struct((rows, features), F32), (GROUP * padded, features)),
        (struct((rows, features), BF16), (GROUP * padded, features)),
        (struct((rows, units), BF16), (GROUP * padded, units)),
        (struct((rows, units), BF16), (GROUP * padded, units)),
    ]
    act_spec = pl.BlockSpec((1, GROUP, tokens, features), lambda i, meta: (0, i, 0, 0))
    return call(
        lambda *refs: forward_kernel(padded, keys, *refs),
        meta,
        ((None, steps), images, *params),
        [images_of(images.shape)] + [whole(p.shape) for p in params],
        [o[0] for o in outs],
        [act_spec] + [lines_of(o[1]) for o in outs[1:]],
        [
            pltpu.VMEM((GROUP * padded, features), F32),
            pltpu.VMEM((GROUP * padded, units), F32),
        ],
        flops=steps * GROUP * padded * features * (features * 8 + units * 4),
    )


def mlp_backward(meta, grad, saved, params):
    slots, tokens, features, padded, keys = sizes(grad)
    steps = slots // GROUP
    units = params[1].shape[1]
    block = GROUP * padded
    active, slope, second, middle = saved
    return call(
        lambda *refs: mlp_backward_kernel(padded, *refs),
        meta,
        ((None, steps), grad, active, slope, second, middle, *params),
        [images_of(grad.shape)]
        + [lines_of((block, units))] * 2
        + [lines_of((block, features))] * 2
        + [whole(p.shape) for p in params],
        [
            struct((slots * padded, features), F32),
            struct((units // features, features, features), BF16),
            struct((units, features), BF16),
            struct((8, units), F32),
        ],
        [
            lines_of((block, features)),
            whole((units // features, features, features)),
            whole((units, features)),
            whole((8, units)),
        ],
        [
            pltpu.VMEM((block, features), F32),
            pltpu.VMEM((block, features), BF16),
            pltpu.VMEM((block, units), BF16),
            pltpu.VMEM((block, features), F32),
            pltpu.VMEM((features, units), F32),
            pltpu.VMEM((features, units), F32),
            pltpu.VMEM((24, features), F32),
            pltpu.VMEM((8, units), F32),
        ],
        flops=steps * block * features * units * 8,
    )


def attention_backward(meta, grad_middle, images, saved, params):
    slots, tokens, features, padded, keys = sizes(images)
    steps = slots // GROUP
    heads = features // HEAD
    block = GROUP * padded
    normed, joined, p, attended = saved
    return call(
        lambda *refs: attention_backward_kernel(padded, keys, *refs),
        meta,
        ((None, steps), grad_middle, images, normed, joined, p, attended, *params),
        [
            lines_of((block, features)),
            images_of(images.shape),
            lines_of((block, features)),
            lines_of((GROUP * keys, 3 * features)),
            lines_of((GROUP, heads, padded, keys)),
            lines_of((block, features)),
        ]
        + [whole(q.shape) for q in params],
        [
            struct((1, slots, tokens, features), BF16),
            struct((features, 4 * features), BF16),
            struct((8, 3 * features), F32),
        ],
        [
            pl.BlockSpec((1, GROUP, tokens, features), lambda i, meta: (0, i, 0, 0)),
            whole((features, 4 * features)),
            whole((8, 3 * features)),
        ],
        [
            pltpu.VMEM((block, features), F32),
            pltpu.VMEM((block, features), BF16),
            pltpu.VMEM((block, features), BF16),
            pltpu.VMEM((block, 3 * features), BF16),
            pltpu.VMEM((block, features), F32),
            pltpu.VMEM((features, 4 * features), F32),
            pltpu.VMEM((24, features), F32),
            pltpu.VMEM((8, 3 * features), F32),
        ],
        flops=steps * block * features * features * 24,
    )


def swap_cores(block):
    return lax.ppermute(block, "segment", [(0, 1), (1, 0)])


def halve(block, bit):
    dp = lax.axis_size("dp")
    mine = (lax.axis_index("dp") >> bit) & 1
    keep = lax.dynamic_index_in_dim(block, mine, 1, keepdims=False)
    send = lax.dynamic_index_in_dim(block, 1 - mine, 1, keepdims=False)
    got = lax.ppermute(send, "dp", [(i, i ^ (1 << bit)) for i in range(dp)])
    return (keep.astype(F32) + got.astype(F32)).astype(block.dtype)


def reduce_shards(block, order):
    dp = lax.axis_size("dp")
    rest = block.shape[1:]
    bits = dp.bit_length() - 1
    held = list(range(bits))
    for bit in order:
        below = held.index(bit)
        block = block.reshape((-1, 2, 1 << below) + rest)
        block = halve(block, bit)
        held.remove(bit)
        block = block.reshape((-1,) + rest)
    top = 1 << len(held)
    low = bits - len(held)
    me = lax.axis_index("dp") >> low
    total = lax.dynamic_index_in_dim(block, me, 0, keepdims=False).astype(F32)
    for other in range(1, top):
        route = [(i, i ^ (other << low)) for i in range(dp)]
        send = lax.dynamic_index_in_dim(block, me ^ other, 0, keepdims=False)
        total = total + lax.ppermute(send, "dp", route).astype(F32)
    return total


def reduce_both_ways(block, axis):
    dp = lax.axis_size("dp")
    low = list(range(max(dp.bit_length() - 3, 0)))
    first, second = jnp.split(block, 2, axis=axis)
    parts = [reduce_shards(first, low), reduce_shards(second, low[:2][::-1] + low[2:])]
    return jnp.concatenate(parts, axis=axis - 1)


def meet(keep, send):
    return (keep.astype(F32) + swap_cores(send).astype(F32)).astype(BF16)


def reduce_mlp(up, down, first):
    dp = lax.axis_size("dp")
    blocks, rows, features = up.shape
    up = up.reshape(blocks, dp, rows // dp, features).swapaxes(0, 1)
    up = up.reshape(dp, blocks * rows // dp, features)
    down = down.reshape(up.shape)
    return reduce_both_ways(meet(jnp.where(first, up, down), jnp.where(first, down, up)), 1)


def reduce_attention(block, first):
    dp = lax.axis_size("dp")
    low, high = jnp.split(block.reshape(dp, block.shape[0] // dp, -1), 2, axis=2)
    return reduce_both_ways(meet(jnp.where(first, low, high), jnp.where(first, high, low)), 2)


def on_device(inputs, image_count, cotangent, *params):
    dp = lax.axis_size("dp")
    core = lax.axis_index("segment")
    first = core == 0
    slots, tokens, features = inputs.shape[1:]
    own = [p[0] for p in params]
    received = [swap_cores(p) for p in own]
    layers = []
    for layer in range(2):
        mine = core == layer
        named = [jnp.where(mine, a, b) for a, b in zip(own, received)]
        g1, b1, wq, bqv, wo, bo, g2, b2, wu, bu, wd, bd = named
        bq = jnp.concatenate([bqv[:features], jnp.zeros((features,), F32), bqv[features:]])
        rows = [v[None] for v in (g1, b1, bq, bo, g2, b2, bu, bd)]
        g1, b1, bq, bo, g2, b2, bu, bd = rows
        layers.append((g1, b1, wq, bq, wo, bo, g2, b2, wu, bu, wd, bd))
    count = lax.dynamic_index_in_dim(image_count[:, 0], core, 0, keepdims=False)
    outer = jnp.stack([count, core.astype(jnp.int32)])
    inner = jnp.stack([count, jnp.zeros((), jnp.int32)])

    saved = []
    acts = []
    images = inputs
    for layer in range(2):
        act, *kept = forward(outer if layer == 0 else inner, images, layers[layer])
        saved.append((images, kept))
        acts.append(act)
        images = act
    grad = cotangent
    grads = [None, None]
    bigs = [None, None]
    vecs = [None, None]
    for layer in (1, 0):
        g1, b1, wq, bq, wo, bo, g2, b2, wu, bu, wd, bd = layers[layer]
        images, (normed, joined, p, attended, middle, second, active, slope) = saved[layer]
        grad_middle, up, down, vec_mlp = mlp_backward(
            outer if layer == 1 else inner, grad, (active, slope, second, middle), (g2, wu, wd)
        )
        grad, big_att, vec_att = attention_backward(
            outer if layer == 0 else inner,
            grad_middle,
            images,
            (normed, joined, p, attended),
            (g1, wq, wo),
        )
        grads[layer] = grad
        bigs[layer] = (reduce_mlp(up, down, first), reduce_attention(big_att, first))
        vecs[layer] = (vec_mlp, vec_att)

    def both(values):
        low, high = values
        from_high = lax.ppermute(low, "segment", [(1, 0)])
        from_low = lax.ppermute(high, "segment", [(0, 1)])
        return jnp.where(
            first,
            jnp.concatenate([low, from_high], 0),
            jnp.concatenate([from_low, high], 0),
        )[None]

    activations = both(acts)
    input_grads = both(grads)

    share = features // dp
    units = params[8].shape[2]

    def exchange(low, high):
        mine = jnp.where(first, low, high)
        other = swap_cores(jnp.where(first, high, low))
        return jnp.where(first, mine, other), jnp.where(first, other, mine)

    g_up, g_down = exchange(bigs[0][0], bigs[1][0])
    attention = jnp.concatenate(exchange(bigs[0][1], bigs[1][1]), axis=1)
    g_up = g_up.reshape(units // features, share, features).swapaxes(0, 1).reshape(share, units)
    g_qkv = attention[:, : 3 * features]
    g_out = attention[:, 3 * features :]

    def vector_shards(layer):
        vec_mlp, vec_att = vecs[layer]
        qv = jnp.concatenate([vec_att[0, :features], vec_att[0, 2 * features : 3 * features]])
        named = [
            vec_att[2, :features],
            vec_att[3, :features],
            qv,
            vec_att[1, :features],
            vec_mlp[2, :features],
            vec_mlp[3, :features],
            vec_mlp[0],
            vec_mlp[1, :features],
        ]
        return jnp.concatenate([v.reshape(dp, -1) for v in named], axis=1)

    vec = [vector_shards(layer) for layer in range(2)]
    vec = jnp.where(first, vec[0], vec[1]) + swap_cores(jnp.where(first, vec[1], vec[0]))
    bits = dp.bit_length() - 1
    vec = reduce_shards(vec, list(range(max(bits - 2, 0))))
    at = 0
    parts = []
    for n in (1, 1, 2, 1, 1, 1, units // features, 1):
        parts.append(vec[at : at + n * share])
        at += n * share
    ln1_gain, ln1_bias, b_qv, b_out, ln2_gain, ln2_bias, b_up, b_down = parts
    outs = (
        ln1_gain,
        ln1_bias,
        g_qkv,
        b_qv,
        g_out,
        b_out,
        ln2_gain,
        ln2_bias,
        g_up,
        b_up,
        g_down,
        b_down,
    )
    return (activations, input_grads) + tuple(o[None] for o in outs)


def solution(mesh):
    in_specs = (
        P(None, "dp", None, None),
        P(None, "dp"),
        P(None, "dp", None, None),
        P("segment", None),
        P("segment", None),
        P("segment", None, None),
        P("segment", None),
        P("segment", None, None),
        P("segment", None),
        P("segment", None),
        P("segment", None),
        P("segment", None, None),
        P("segment", None),
        P("segment", None, None),
        P("segment", None),
    )
    out_specs = (
        P("segment", None, "dp", None, None),
        P("segment", None, "dp", None, None),
        P("segment", "dp"),
        P("segment", "dp"),
        P("segment", "dp", None),
        P("segment", "dp"),
        P("segment", "dp", None),
        P("segment", "dp"),
        P("segment", "dp"),
        P("segment", "dp"),
        P("segment", "dp", None),
        P("segment", "dp"),
        P("segment", "dp", None),
        P("segment", "dp"),
    )
    return jax.shard_map(
        on_device, mesh=mesh, in_specs=in_specs, out_specs=out_specs, check_vma=False
    )
```

```python
import jax
import jax.numpy as jnp
from jax import lax
from jax.experimental import pallas as pl
from jax.experimental.pallas import tpu as pltpu
from jax.sharding import PartitionSpec as P

HEAD = 64
EPSILON = 1e-06
BF16 = jnp.bfloat16
F32 = jnp.float32
GROUP = 2
VMEM_LIMIT = 58 * 1024 * 1024


def dot(a, b):
    return lax.dot_general(a, b, (((1,), (0,)), ((), ())), preferred_element_type=F32)


def dot_nt(a, b):
    return lax.dot_general(a, b, (((1,), (1,)), ((), ())), preferred_element_type=F32)


def dot_tn(a, b):
    return lax.dot_general(a, b, (((0,), (0,)), ((), ())), preferred_element_type=F32)


def normalized(rows):
    centered = rows - jnp.mean(rows, axis=-1, keepdims=True)
    spread = jnp.mean(centered * centered, axis=-1, keepdims=True)
    inverse = lax.rsqrt(spread + EPSILON)
    return centered * inverse, inverse


def norm_backward(rows, grad, gain):
    hat, inverse = normalized(rows)
    scaled = grad * gain
    inner = jnp.mean(scaled * hat, axis=-1, keepdims=True)
    dx = inverse * (scaled - jnp.mean(scaled, axis=-1, keepdims=True) - hat * inner)
    return dx, grad * hat


def gelu_and_slope(x):
    bell = jnp.exp(x * x * -0.5)
    t = 1.0 / (1.0 + jnp.abs(x) * (0.3275911 * 0.7071067811865476))
    poly = t * (
        0.5 * 0.254829592
        + t
        * (
            0.5 * -0.284496736
            + t * (0.5 * 1.421413741 + t * (0.5 * -1.453152027 + t * (0.5 * 1.061405429)))
        )
    )
    tail = poly * bell
    cdf = jnp.where(x >= 0.0, 1.0 - tail, tail)
    return x * cdf, cdf + x * (bell * 0.3989422804014327)


def fold(rows):
    total = rows[0:8]
    for at in range(8, rows.shape[0], 8):
        total = total + rows[at : at + 8]
    return total


def row_chunks(total, size=32):
    return [(at, min(size, total - at)) for at in range(0, total, size)]


def layers_kernel(
    padded,
    keys,
    meta,
    h_ref,
    cot_ref,
    own_vec,
    got_vec,
    own_qkv,
    own_out,
    own_up,
    own_down,
    got_qkv,
    got_out,
    got_up,
    got_down,
    mine_ref,
    away_ref,
    mine_wide,
    away_wide,
    mine_tall,
    away_tall,
    w_qkv,
    w_out,
    w_up,
    w_down,
    vecs,
    hidden,
    normed,
    joined,
    weights,
    attended,
    middle,
    second,
    active,
    slope,
    before,
    grad_out,
    grad_low,
    grad_before,
    grad_joined,
    grad_norm,
    sum_up,
    sum_down,
    sum_att,
    vec_one,
    vec_up,
    vec_qkv,
    wide,
    tall,
    load_sem,
    store_sem,
):
    step = pl.program_id(0)
    count = meta[0]
    core = meta[1]
    tokens, features = h_ref.shape[2:]
    heads = features // HEAD
    rows = GROUP * padded
    units = w_up.shape[2]
    own = (own_qkv, own_out, own_up, own_down)
    got = (got_qkv, got_out, got_up, got_down)
    held = (w_qkv, w_out, w_up, w_down)
    at_g1, at_b1, at_qkv = 0, features, 2 * features
    at_bo, at_g2, at_b2, at_bd, at_up = (n * features for n in (5, 6, 7, 8, 9))

    def vec(layer, at, size=features):
        return vecs[pl.ds(layer, 1), at : at + size]

    def load(source, n, layer):
        return pltpu.make_async_copy(source[n].at[0], held[n].at[layer], load_sem.at[layer, n])

    @pl.when(step == 0)
    def _():
        for layer in range(2):
            for n in range(4):

                @pl.when(core == layer)
                def _():
                    load(own, n, layer).start()

                @pl.when(core != layer)
                def _():
                    load(got, n, layer).start()

        for layer in range(2):
            mine = jnp.full(own_vec.shape, core == layer)
            vecs[layer : layer + 1] = jnp.where(mine, own_vec[...], got_vec[...])
        for ref in (sum_up, sum_down, sum_att, vec_one, vec_up, vec_qkv):
            for layer in range(2):
                ref[layer] = jnp.zeros(ref.shape[1:], F32)
        for layer in range(2):
            for j in range(GROUP):
                joined[layer, j * keys + padded : (j + 1) * keys] = jnp.zeros(
                    (keys - padded, 3 * features), BF16
                )

    def leave(layer, kind, j, value):
        @pl.when(core == layer)
        def _():
            mine_ref[kind, j] = value

        @pl.when(core != layer)
        def _():
            away_ref[kind, j] = value

    lane = lax.broadcasted_iota(jnp.int32, (padded, 2 * HEAD), 1)

    def forward(layer):
        @pl.when(step == 0)
        def _():
            for n in range(4):
                load(own, n, layer).wait()

        for at, size in row_chunks(rows):
            hat, _ = normalized(hidden[layer, at : at + size])
            value = hat * vec(layer, at_g1) + vec(layer, at_b1)
            normed[layer, at : at + size] = value.astype(BF16)
        for j in range(GROUP):
            lines = normed[layer, j * padded : (j + 1) * padded]
            for part in range(3):
                columns = slice(part * features, (part + 1) * features)
                value = dot(lines, w_qkv[layer, :, columns]) + vec(
                    layer, at_qkv + part * features
                )
                value = value.astype(BF16)
                if part == 0:
                    value = value * jnp.asarray(HEAD**-0.5, BF16)
                joined[layer, j * keys : j * keys + padded, columns] = value
        real = lax.broadcasted_iota(jnp.int32, (padded, keys), 1) < tokens
        for j in range(GROUP):
            for pair in range(heads // 2):
                at = pair * 2 * HEAD
                span = slice(j * keys, (j + 1) * keys)
                q = joined[layer, j * keys : j * keys + padded, at : at + 2 * HEAD]
                k = joined[layer, span, features + at : features + at + 2 * HEAD]
                v = joined[layer, span, 2 * features + at : 2 * features + at + 2 * HEAD]
                parts = []
                for half in range(2):
                    mine = (lane < HEAD) if half == 0 else (lane >= HEAD)
                    s = dot_nt(jnp.where(mine, q, jnp.zeros_like(q)), k)
                    s = jnp.where(real, s, -1e30)
                    e = jnp.exp(s - jnp.max(s, axis=-1, keepdims=True))
                    p = (e * (1.0 / jnp.sum(e, axis=-1, keepdims=True))).astype(BF16)
                    weights[layer, j, 2 * pair + half] = p
                    parts.append(dot(p, v))
                attended[layer, j * padded : (j + 1) * padded, at : at + 2 * HEAD] = jnp.where(
                    lane < HEAD, parts[0], parts[1]
                ).astype(BF16)
        middle[layer] = dot(attended[layer], w_out[layer])
        for at, size in row_chunks(rows):
            value = middle[layer, at : at + size] + hidden[layer, at : at + size]
            value = value + vec(layer, at_bo)
            middle[layer, at : at + size] = value
            hat, _ = normalized(value)
            value = hat * vec(layer, at_g2) + vec(layer, at_b2)
            second[layer, at : at + size] = value.astype(BF16)
        width = features
        for j in range(GROUP):
            lines = slice(j * padded, (j + 1) * padded)
            for c in range(units // width):
                columns = slice(c * width, (c + 1) * width)
                before[lines, columns] = dot(second[layer, lines], w_up[layer, :, columns])
                for at, size in row_chunks(padded, 16):
                    piece = slice(j * padded + at, j * padded + at + size)
                    value, change = gelu_and_slope(
                        before[piece, columns] + vec(layer, at_up + c * width, width)
                    )
                    active[layer, piece, columns] = value.astype(BF16)
                    slope[layer, piece, columns] = change.astype(BF16)
            keep = jnp.where(step * GROUP + j < count, 1.0, 0.0)
            result = dot(active[layer, lines], w_down[layer]) + middle[layer, lines]
            result = ((result + vec(layer, at_bd)) * keep).astype(BF16)
            leave(layer, 0, j, result[:tokens])
            hidden[layer + 1, lines] = result.astype(F32)

    def backward(layer):
        for at, size in row_chunks(rows):
            value = grad_out[at : at + size]
            grad_low[at : at + size] = value.astype(BF16)
            vec_one[layer, 0:8] += fold(value)
        width = features
        sum_down[layer] += dot_tn(grad_low[...], active[layer])
        for j in range(GROUP):
            lines = slice(j * padded, (j + 1) * padded)
            for c in range(units // width):
                columns = slice(c * width, (c + 1) * width)
                piece = dot_nt(grad_low[lines], w_down[layer, columns, :])
                piece = (piece * slope[layer, lines, columns].astype(F32)).astype(BF16)
                grad_before[lines, columns] = piece
                vec_up[layer, :, columns] += fold(piece.astype(F32))
            grad_norm[lines] = dot_nt(grad_before[lines], w_up[layer])
        sum_up[layer] += dot_tn(second[layer], grad_before[...])
        for at, size in row_chunks(rows):
            grad = grad_norm[at : at + size]
            dx, by_hat = norm_backward(middle[layer, at : at + size], grad, vec(layer, at_g2))
            vec_one[layer, 8:16] += fold(by_hat)
            vec_one[layer, 16:24] += fold(grad)
            value = grad_out[at : at + size] + dx
            grad_out[at : at + size] = value
            value = value.astype(BF16)
            grad_low[at : at + size] = value
            vec_one[layer, 24:32] += fold(value.astype(F32))
        sum_att[layer, :, 3 * features :] += dot_tn(attended[layer], grad_low[...])
        grad_low[...] = dot_nt(grad_low[...], w_out[layer]).astype(BF16)
        for j in range(GROUP):
            lines = slice(j * padded, (j + 1) * padded)
            for pair in range(heads // 2):
                at = pair * 2 * HEAD
                span = slice(j * keys, (j + 1) * keys)
                q = joined[layer, j * keys : j * keys + padded, at : at + 2 * HEAD]
                k = joined[layer, span, features + at : features + at + 2 * HEAD]
                v = joined[layer, span, 2 * features + at : 2 * features + at + 2 * HEAD]
                ga = grad_low[lines, at : at + 2 * HEAD]
                gq, gk, gv = [], [], []
                for half in range(2):
                    mine = (lane < HEAD) if half == 0 else (lane >= HEAD)
                    gp = dot_nt(jnp.where(mine, ga, jnp.zeros_like(ga)), v)
                    p = weights[layer, j, 2 * pair + half]
                    p_wide = p.astype(F32)
                    by = p_wide * gp
                    gs = (by - p_wide * jnp.sum(by, axis=-1, keepdims=True)).astype(BF16)
                    gq.append(dot(gs, k))
                    gk.append(dot_tn(gs, q)[:padded])
                    gv.append(dot_tn(p, ga)[:padded])
                left = lane < HEAD
                parts = (
                    jnp.where(left, gq[0], gq[1]) * HEAD**-0.5,
                    jnp.where(left, gk[0], gk[1]),
                    jnp.where(left, gv[0], gv[1]),
                )
                for n, part in enumerate(parts):
                    column = n * features + at
                    part = part.astype(BF16)
                    grad_joined[lines, column : column + 2 * HEAD] = part
                    vec_qkv[layer, :, column : column + 2 * HEAD] += fold(part.astype(F32))
        sum_att[layer, :, : 3 * features] += dot_tn(normed[layer], grad_joined[...])
        grad_norm[...] = dot_nt(grad_joined[...], w_qkv[layer])
        for at, size in row_chunks(rows):
            grad = grad_norm[at : at + size]
            dx, by_hat = norm_backward(hidden[layer, at : at + size], grad, vec(layer, at_g1))
            vec_one[layer, 32:40] += fold(by_hat)
            vec_one[layer, 40:48] += fold(grad)
            value = grad_out[at : at + size] + dx
            grad_out[at : at + size] = value.astype(BF16).astype(F32)
        for j in range(GROUP):
            leave(layer, 1, j, grad_out[j * padded : j * padded + tokens].astype(BF16))

    @pl.when(step * GROUP >= count)
    def _():
        mine_ref[...] = jnp.zeros_like(mine_ref)
        away_ref[...] = jnp.zeros_like(away_ref)

    @pl.when(step * GROUP < count)
    def _():
        for j in range(GROUP):
            tail = slice(j * padded + padded - 16, (j + 1) * padded)
            hidden[0, tail] = jnp.zeros((16, features), F32)
            hidden[0, j * padded : j * padded + tokens] = h_ref[0, j].astype(F32)
        lax.fori_loop(0, 2, lambda layer, carry: (forward(layer), carry)[1], 0)
        for j in range(GROUP):
            keep = jnp.where(step * GROUP + j < count, 1.0, 0.0)
            tail = slice(j * padded + padded - 16, (j + 1) * padded)
            grad_out[tail] = jnp.zeros((16, features), F32)
            grad_out[j * padded : j * padded + tokens] = cot_ref[0, j].astype(F32) * keep
        lax.fori_loop(0, 2, lambda at, carry: (backward(1 - at), carry)[1], 0)

    def store(layer, kind, target):
        stage = (wide, tall)[kind].at[layer]
        return pltpu.make_async_copy(stage, target, store_sem.at[layer, kind])

    @pl.when(step == pl.num_programs(0) - 1)
    def _():
        for layer in range(2):
            for c in range(units // features):
                columns = slice(c * features, (c + 1) * features)
                tall[layer, columns, :] = sum_down[layer, :, columns].T.astype(BF16)
            wide[layer, :, :units] = sum_up[layer].astype(BF16)
            wide[layer, :, units : units + 4 * features] = sum_att[layer].astype(BF16)
            line = lax.broadcasted_iota(jnp.int32, (128, features), 0)
            plain = jnp.zeros((128, features), F32)
            for n, group in enumerate((4, 5, 3, 1, 2, 0)):
                total = jnp.sum(vec_one[layer, 8 * group : 8 * group + 8], axis=0, keepdims=True)
                plain = plain + jnp.where(line == n, total, 0.0)
            qkv = jnp.sum(vec_qkv[layer], axis=0, keepdims=True)
            qv = jnp.concatenate([qkv[:, :features], qkv[:, 2 * features :]], axis=1)
            up = jnp.sum(vec_up[layer], axis=0, keepdims=True)
            columns = jnp.zeros((features, 128), F32)
            for first_line, total in ((0, plain), (6, qv), (8, up)):
                size = total.shape[1]
                each = size // features
                position = lax.broadcasted_iota(jnp.int32, (128, size), 1)
                row = lax.broadcasted_iota(jnp.int32, (128, size), 0)
                if each > 1:
                    total = jnp.where(row - first_line == position % each, total, 0.0)
                target = lax.broadcasted_iota(jnp.int32, (features, size), 0)
                source = lax.broadcasted_iota(jnp.int32, (features, size), 1)
                pick = jnp.where(source // each == target, 1.0, 0.0).astype(BF16)
                columns = columns + dot_nt(pick, total.astype(BF16))
            wide[layer, :, units + 4 * features :] = columns.astype(BF16)
            for kind, (mine, away) in enumerate(((mine_wide, away_wide), (mine_tall, away_tall))):

                @pl.when(core == layer)
                def _():
                    store(layer, kind, mine).start()

                @pl.when(core != layer)
                def _():
                    store(layer, kind, away).start()

        for layer in range(2):
            for kind, mine in enumerate((mine_wide, mine_tall)):
                store(layer, kind, mine).wait()


def run_layers(meta, inputs, cotangent, vectors, weights):
    slots, tokens, features = inputs.shape[1:]
    padded = -(-tokens // 16) * 16
    keys = -(-tokens // 128) * 128
    heads = features // HEAD
    steps = slots // GROUP
    block = GROUP * padded
    units = weights[0][2].shape[2]
    packed = vectors[0].shape[1]
    wide = units + 4 * features + 128
    images = pl.BlockSpec((1, GROUP, tokens, features), lambda i, meta: (meta[1], i, 0, 0))
    kinds = pl.BlockSpec((2, GROUP, tokens, features), lambda i, meta: (0, i, 0, 0))
    vector = pl.BlockSpec((1, packed), lambda i, meta: (0, 0))
    anywhere = pl.BlockSpec(memory_space=pl.ANY)
    both = (
        ((features, 3 * features), BF16),
        ((features, features), BF16),
        ((features, units), BF16),
        ((units, features), BF16),
        ((packed,), F32),
    )
    saved = (
        ((block, features), BF16),
        ((GROUP * keys, 3 * features), BF16),
        ((GROUP, heads, padded, keys), BF16),
        ((block, features), BF16),
        ((block, features), F32),
        ((block, features), BF16),
        ((block, units), BF16),
        ((block, units), BF16),
    )
    sums = (
        ((features, units), F32),
        ((features, units), F32),
        ((features, 4 * features), F32),
        ((48, features), F32),
        ((8, units), F32),
        ((8, 3 * features), F32),
        ((features, wide), BF16),
        ((units, features), BF16),
    )

    def two(shapes):
        return [pltpu.VMEM((2,) + shape, kind) for shape, kind in shapes]

    scratch = (
        two(both)
        + [pltpu.VMEM((3, block, features), F32)]
        + two(saved)
        + [
            pltpu.VMEM((block, units), F32),
            pltpu.VMEM((block, features), F32),
            pltpu.VMEM((block, features), BF16),
            pltpu.VMEM((block, units), BF16),
            pltpu.VMEM((block, 3 * features), BF16),
            pltpu.VMEM((block, features), F32),
        ]
        + two(sums)
        + [pltpu.SemaphoreType.DMA((2, 4)), pltpu.SemaphoreType.DMA((2, 2))]
    )
    return pl.pallas_call(
        lambda *refs: layers_kernel(padded, keys, *refs),
        grid_spec=pltpu.PrefetchScalarGridSpec(
            num_scalar_prefetch=1,
            grid=(steps,),
            in_specs=[images, images, vector, vector] + [anywhere] * 8,
            out_specs=[kinds, kinds] + [anywhere] * 4,
            scratch_shapes=scratch,
        ),
        out_shape=[jax.ShapeDtypeStruct((2, slots, tokens, features), BF16)] * 2
        + [jax.ShapeDtypeStruct((features, wide), BF16)] * 2
        + [jax.ShapeDtypeStruct((units, features), BF16)] * 2,
        compiler_params=pltpu.CompilerParams(
            vmem_limit_bytes=VMEM_LIMIT, dimension_semantics=("arbitrary",)
        ),
        cost_estimate=pl.CostEstimate(
            flops=80_000_000_000, bytes_accessed=30_000_000, transcendentals=0
        ),
    )(meta, inputs, cotangent, *vectors, *weights[0], *weights[1])


def swap_cores(block):
    return lax.ppermute(block, "segment", [(0, 1), (1, 0)])


def reduce_shards(mine, got, orders, first):
    dp = lax.axis_size("dp")
    me = lax.axis_index("dp")
    bits = dp.bit_length() - 1
    rest = (mine.shape[0] // dp, mine.shape[1])
    block = mine.astype(F32) + got.astype(F32)
    held = [list(range(bits)) for _ in orders]
    for n in range(bits):
        below = [left.index(order[n]) for order, left in zip(orders, held)]
        bit = [(me >> order[n]) & 1 for order in orders]
        for order, left in zip(orders, held):
            left.remove(order[n])

        def part(at, index):
            view = block.reshape((-1, 2, 1 << at) + rest)
            taken = lax.dynamic_index_in_dim(view, index, 1, keepdims=False)
            return taken.reshape((-1,) + rest)

        if below[0] == below[1]:
            mine = jnp.where(first, bit[0], bit[1])
            keep, send = part(below[0], mine), part(below[0], 1 - mine)
        else:
            keep = jnp.where(first, part(below[0], bit[0]), part(below[1], bit[1]))
            send = jnp.where(first, part(below[0], 1 - bit[0]), part(below[1], 1 - bit[1]))
        route = [
            (core * dp + i, core * dp + (i ^ (1 << order[n])))
            for core, order in enumerate(orders)
            for i in range(dp)
        ]
        arrived = lax.ppermute(send.astype(BF16), ("segment", "dp"), route)
        block = keep.astype(F32) + arrived.astype(F32)
        if n < bits - 1:
            block = block.astype(BF16)
    return block.reshape(rest)


def on_device(inputs, image_count, cotangent, *params):
    dp = lax.axis_size("dp")
    core = lax.axis_index("segment")
    first = core == 0
    features = inputs.shape[3]
    g1, b1, w_qkv, b_qv, w_out, b_out, g2, b2, w_up, b_up, w_down, b_down = params
    units = w_up.shape[2]
    own_weights = (w_qkv, w_out, w_up, w_down)
    got_weights = tuple(swap_cores(w) for w in own_weights)
    zeros = jnp.zeros((1, features), F32)
    own_vec = jnp.concatenate(
        [g1, b1, b_qv[:, :features], zeros, b_qv[:, features:], b_out, g2, b2, b_down, b_up], axis=1
    )
    got_vec = swap_cores(own_vec)
    count = lax.dynamic_index_in_dim(image_count[:, 0], core, 0, keepdims=False)
    meta = jnp.stack([count, core.astype(jnp.int32)])
    mine, away, mine_wide, away_wide, mine_tall, away_tall = run_layers(
        meta, inputs, cotangent, (own_vec, got_vec), (own_weights, got_weights)
    )
    got_wide = swap_cores(away_wide)
    got_tall = swap_cores(away_tall)
    got = swap_cores(away)
    bits = dp.bit_length() - 1
    near = list(range(min(bits, 3)))
    far = list(range(len(near), bits))

    def turned(by):
        return near[by % len(near) :] + near[: by % len(near)] + far

    wide = reduce_shards(mine_wide, got_wide, (turned(0), turned(2)), first)
    tall = reduce_shards(mine_tall, got_tall, (turned(1), turned(1)), first)
    both = jnp.stack([jnp.where(first, mine, got), jnp.where(first, got, mine)], axis=1)
    share = features // dp
    g_up = wide[:, :units]
    g_qkv = wide[:, units : units + 3 * features]
    g_out = wide[:, units + 3 * features : units + 4 * features]
    columns = wide[:, units + 4 * features :]
    ln1_gain, ln1_bias, g_bo, ln2_gain, ln2_bias, g_bd = (columns[:, n] for n in range(6))
    g_bqv = columns[:, 6:8].reshape(2 * share)
    g_bup = columns[:, 8 : 8 + units // features].reshape(-1)
    outs = (ln1_gain, ln1_bias, g_qkv, g_bqv, g_out, g_bo, ln2_gain, ln2_bias, g_up, g_bup, tall, g_bd)
    return (both[0][None], both[1][None]) + tuple(o[None] for o in outs)


def solution(mesh):
    in_specs = (
        P(None, "dp", None, None),
        P(None, "dp"),
        P(None, "dp", None, None),
        P("segment", None),
        P("segment", None),
        P("segment", None, None),
        P("segment", None),
        P("segment", None, None),
        P("segment", None),
        P("segment", None),
        P("segment", None),
        P("segment", None, None),
        P("segment", None),
        P("segment", None, None),
        P("segment", None),
    )
    out_specs = (
        P("segment", None, "dp", None, None),
        P("segment", None, "dp", None, None),
        P("segment", "dp"),
        P("segment", "dp"),
        P("segment", "dp", None),
        P("segment", "dp"),
        P("segment", "dp", None),
        P("segment", "dp"),
        P("segment", "dp"),
        P("segment", "dp"),
        P("segment", "dp", None),
        P("segment", "dp"),
        P("segment", "dp", None),
        P("segment", "dp"),
    )
    return jax.shard_map(
        on_device, mesh=mesh, in_specs=in_specs, out_specs=out_specs, check_vma=False
    )
```

```python
import jax
import jax.numpy as jnp
from jax import lax
from jax.experimental import pallas as pl
from jax.experimental.pallas import tpu as pltpu
from jax.sharding import PartitionSpec as P

HEAD = 64
EPSILON = 1e-06
BF16 = jnp.bfloat16
F32 = jnp.float32
GROUP = 2
VMEM_LIMIT = 62 * 1024 * 1024


def dot(a, b):
    return lax.dot_general(a, b, (((1,), (0,)), ((), ())), preferred_element_type=F32)


def dot_nt(a, b):
    return lax.dot_general(a, b, (((1,), (1,)), ((), ())), preferred_element_type=F32)


def dot_tn(a, b):
    return lax.dot_general(a, b, (((0,), (0,)), ((), ())), preferred_element_type=F32)


def normalized(rows):
    centered = rows - jnp.mean(rows, axis=-1, keepdims=True)
    spread = jnp.mean(centered * centered, axis=-1, keepdims=True)
    inverse = lax.rsqrt(spread + EPSILON)
    return centered * inverse, inverse


def norm_backward(rows, grad, gain):
    hat, inverse = normalized(rows)
    scaled = grad * gain
    inner = jnp.mean(scaled * hat, axis=-1, keepdims=True)
    dx = inverse * (scaled - jnp.mean(scaled, axis=-1, keepdims=True) - hat * inner)
    return dx, grad * hat


def gelu_and_slope(x):
    bell = jnp.exp(x * x * -0.5)
    under = 1.0 + jnp.abs(x) * (0.3275911 * 0.7071067811865476)
    t = pl.reciprocal(under, approx=True)
    t = t * (2.0 - under * t)
    poly = t * (
        0.5 * 0.254829592
        + t
        * (
            0.5 * -0.284496736
            + t * (0.5 * 1.421413741 + t * (0.5 * -1.453152027 + t * (0.5 * 1.061405429)))
        )
    )
    tail = poly * bell
    cdf = jnp.where(x >= 0.0, 1.0 - tail, tail)
    return x * cdf, cdf + x * (bell * 0.3989422804014327)


def fold(rows):
    total = rows[0:8]
    for at in range(8, rows.shape[0], 8):
        total = total + rows[at : at + 8]
    return total


def row_chunks(total, size=32):
    return [(at, min(size, total - at)) for at in range(0, total, size)]


def spans(total, width):
    return [slice(at, min(at + width, total)) for at in range(0, total, width)]


def layers_kernel(
    padded,
    keys,
    meta,
    h_ref,
    cot_ref,
    own_vec,
    got_vec,
    own_qkv,
    own_out,
    own_up,
    own_down,
    got_qkv,
    got_out,
    got_up,
    got_down,
    mine_ref,
    away_ref,
    mine_wide,
    away_wide,
    mine_tall,
    away_tall,
    w_qkv,
    w_out,
    w_up,
    w_down,
    vecs,
    hidden,
    normed,
    queries,
    kv,
    weights,
    attended,
    middle,
    second,
    active,
    slope,
    before,
    grad_out,
    grad_low,
    out_low,
    grad_heads,
    grad_before,
    grad_joined,
    grad_norm,
    scores,
    grad_scores,
    sum_up,
    sum_down,
    sum_att,
    vec_one,
    vec_up,
    vec_qkv,
    wide,
    tall,
    load_sem,
    store_sem,
):
    step = pl.program_id(0)
    last = pl.num_programs(0) - 1
    count = meta[0]
    core = meta[1]
    running = step * GROUP < count
    tokens, features = h_ref.shape[2:]
    heads = features // HEAD
    rows = GROUP * padded
    units = w_up.shape[2]
    couple = 2 * HEAD
    own = (own_qkv, own_out, own_up, own_down)
    got = (got_qkv, got_out, got_up, got_down)
    held = (w_qkv, w_out, w_up, w_down)
    at_g1, at_b1, at_qkv = 0, features, 2 * features
    at_bo, at_g2, at_b2, at_bd, at_up = (n * features for n in (5, 6, 7, 8, 9))

    def vec(layer, at, size=features):
        return vecs[pl.ds(layer, 1), at : at + size]

    def load(source, n, layer):
        return pltpu.make_async_copy(source[n].at[0], held[n].at[layer], load_sem.at[layer, n])

    @pl.when(step == 0)
    def _():
        for layer in range(2):
            for n in range(4):

                @pl.when(core == layer)
                def _():
                    load(own, n, layer).start()

                @pl.when(core != layer)
                def _():
                    load(got, n, layer).start()

        for layer in range(2):
            mine = jnp.full(own_vec.shape, core == layer)
            vecs[layer : layer + 1] = jnp.where(mine, own_vec[...], got_vec[...])
        for ref in (sum_up, sum_down, sum_att, vec_one, vec_up, vec_qkv):
            for layer in range(2):
                ref[layer] = jnp.zeros(ref.shape[1:], F32)
        for layer in range(2):
            for j in range(GROUP):
                kv[layer, j * keys + padded : (j + 1) * keys] = jnp.zeros(
                    (keys - padded, 2 * features), BF16
                )

    def leave(layer, kind, j, value):
        @pl.when(core == layer)
        def _():
            mine_ref[kind, j] = value

        @pl.when(core != layer)
        def _():
            away_ref[kind, j] = value

    lane = lax.broadcasted_iota(jnp.int32, (padded, couple), 1)
    left = lane < HEAD
    image = [slice(j * padded, (j + 1) * padded) for j in range(GROUP)]
    images_keys = [slice(j * keys, (j + 1) * keys) for j in range(GROUP)]
    pairs = [slice(n * couple, (n + 1) * couple) for n in range(heads // 2)]
    tasks = [(j, n) for j in range(GROUP) for n in range(heads // 2)]
    chunks = spans(units, 512)

    def stacked(value):
        nothing = jnp.zeros_like(value)
        return jnp.where(left, value, nothing), jnp.where(left, nothing, value)

    def key_of(layer, j, n):
        return kv[layer, images_keys[j], pairs[n]]

    def value_of(layer, j, n):
        at = features + n * couple
        return kv[layer, images_keys[j], at : at + couple]

    def unstacked(value):
        return jnp.where(left, value[:padded], value[padded:])

    def forward(layer):
        @pl.when(step == 0)
        def _():
            for n in range(4):
                load(own, n, layer).wait()

        for at, size in row_chunks(rows):
            hat, _ = normalized(hidden[layer, at : at + size])
            value = hat * vec(layer, at_g1) + vec(layer, at_b1)
            normed[layer, at : at + size] = value.astype(BF16)
        value = dot(normed[layer], w_qkv[layer, :, :features]) + vec(layer, at_qkv)
        value = value.astype(BF16) * jnp.asarray(HEAD**-0.5, BF16)
        for j, n in tasks:
            for half, part in enumerate(stacked(value[image[j], pairs[n]])):
                queries[layer, j, n, half * padded : (half + 1) * padded] = part
        for columns in spans(2 * features, 512):
            at, size = features + columns.start, columns.stop - columns.start
            value = dot(normed[layer], w_qkv[layer, :, at : at + size])
            value = (value + vec(layer, at_qkv + at, size)).astype(BF16)
            for j in range(GROUP):
                kv[layer, j * keys : j * keys + padded, columns] = value[image[j]]

        def score(u):
            j, n = tasks[u]
            scores[u % 2] = dot_nt(queries[layer, j, n], key_of(layer, j, n))

        def soften(u):
            j, n = tasks[u]
            for at, size in row_chunks(2 * padded):
                real = lax.broadcasted_iota(jnp.int32, (size, keys), 1) < tokens
                s = jnp.where(real, scores[u % 2, at : at + size], -1e30)
                e = jnp.exp(s - jnp.max(s, axis=-1, keepdims=True))
                p = e * (1.0 / jnp.sum(e, axis=-1, keepdims=True))
                weights[layer, j, n, at : at + size] = p.astype(BF16)

        def attend(u):
            j, n = tasks[u]
            value = unstacked(dot(weights[layer, j, n], value_of(layer, j, n)))
            attended[layer, image[j], pairs[n]] = value.astype(BF16)

        def project(j):
            middle[layer, image[j]] = dot(attended[layer, image[j]], w_out[layer])

        def norm_two(j):
            for at, size in row_chunks(padded, 16):
                at = j * padded + at
                value = middle[layer, at : at + size] + hidden[layer, at : at + size]
                value = value + vec(layer, at_bo)
                middle[layer, at : at + size] = value
                hat, _ = normalized(value)
                value = hat * vec(layer, at_g2) + vec(layer, at_b2)
                second[layer, at : at + size] = value.astype(BF16)

        score(0)
        for u in range(len(tasks)):
            if u + 1 < len(tasks):
                score(u + 1)
            if u:
                attend(u - 1)
                if tasks[u - 1][1] == heads // 2 - 1:
                    project(tasks[u - 1][0])
            soften(u)
            if u and tasks[u - 1][1] == heads // 2 - 1:
                norm_two(tasks[u - 1][0])
        attend(len(tasks) - 1)
        project(GROUP - 1)
        norm_two(GROUP - 1)

        def up(c):
            before[:, chunks[c]] = dot(second[layer], w_up[layer, :, chunks[c]])

        def curve(c):
            columns = chunks[c]
            for at, size in row_chunks(rows, 16):
                value, change = gelu_and_slope(
                    before[at : at + size, columns]
                    + vec(layer, at_up + columns.start, columns.stop - columns.start)
                )
                active[layer, at : at + size, columns] = value.astype(BF16)
                slope[layer, at : at + size, columns] = change.astype(BF16)

        def down(c):
            value = dot(active[layer, :, chunks[c]], w_down[layer, chunks[c]])
            if c:
                value = value + grad_norm[...]
            grad_norm[...] = value

        up(0)
        for c in range(len(chunks)):
            if c + 1 < len(chunks):
                up(c + 1)
            if c:
                down(c - 1)
            curve(c)
        down(len(chunks) - 1)
        for j in range(GROUP):
            keep = jnp.where(step * GROUP + j < count, 1.0, 0.0)
            result = grad_norm[image[j]] + middle[layer, image[j]]
            result = ((result + vec(layer, at_bd)) * keep).astype(BF16)
            leave(layer, 0, j, result[:tokens])
            hidden[layer + 1, image[j]] = result.astype(F32)

    def backward(layer):
        for at, size in row_chunks(rows):
            value = grad_out[at : at + size]
            grad_low[at : at + size] = value.astype(BF16)
            vec_one[layer, 0:8] += fold(value)

        def activation(c):
            before[:, chunks[c]] = dot_nt(grad_low[...], w_down[layer, chunks[c]])

        def multiply(c):
            columns = chunks[c]
            total = jnp.zeros((8, columns.stop - columns.start), F32)
            for at, size in row_chunks(rows, 16):
                lines = slice(at, at + size)
                piece = before[lines, columns] * slope[layer, lines, columns].astype(F32)
                piece = piece.astype(BF16)
                grad_before[lines, columns] = piece
                total = total + fold(piece.astype(F32))
            vec_up[layer, :, columns] += total

        activation(0)
        for c in range(len(chunks)):
            if c + 1 < len(chunks):
                activation(c + 1)
            sum_down[layer, :, chunks[c]] += dot_tn(grad_low[...], active[layer, :, chunks[c]])
            multiply(c)

        def norm_two(j):
            one, two, three = (jnp.zeros((8, features), F32) for _ in range(3))
            for at, size in row_chunks(padded, 16):
                lines = slice(j * padded + at, j * padded + at + size)
                grad = grad_norm[lines]
                dx, by_hat = norm_backward(middle[layer, lines], grad, vec(layer, at_g2))
                one = one + fold(by_hat)
                two = two + fold(grad)
                value = grad_out[lines] + dx
                grad_out[lines] = value
                value = value.astype(BF16)
                out_low[lines] = value
                three = three + fold(value.astype(F32))
            vec_one[layer, 8:16] += one
            vec_one[layer, 16:24] += two
            vec_one[layer, 24:32] += three

        for j in range(GROUP):
            grad_norm[image[j]] = dot_nt(grad_before[image[j]], w_up[layer])
        for c in range(len(chunks)):
            sum_up[layer, :, chunks[c]] += dot_tn(second[layer], grad_before[:, chunks[c]])
            if c < GROUP:
                norm_two(c)
        for j in range(GROUP):
            value = dot_nt(out_low[image[j]], w_out[layer]).astype(BF16)
            for n in range(heads // 2):
                for half, part in enumerate(stacked(value[:, pairs[n]])):
                    grad_heads[j, n, half * padded : (half + 1) * padded] = part

        def grad_weights(u):
            j, n = tasks[u]
            scores[u % 2] = dot_nt(grad_heads[j, n], value_of(layer, j, n))

        def soften_back(u):
            j, n = tasks[u]
            for at, size in row_chunks(2 * padded):
                p = weights[layer, j, n, at : at + size].astype(F32)
                by = p * scores[u % 2, at : at + size]
                by = by - p * jnp.sum(by, axis=-1, keepdims=True)
                grad_scores[u % 2, at : at + size] = by.astype(BF16)

        def into(layer, j, column, part):
            part = part.astype(BF16)
            grad_joined[image[j], column : column + couple] = part
            vec_qkv[layer, :, column : column + couple] += fold(part.astype(F32))

        def attention_value(u):
            j, n = tasks[u]
            part = dot_tn(weights[layer, j, n], grad_heads[j, n])[:padded]
            into(layer, j, 2 * features + n * couple, part)

        def attention_rest(u):
            j, n = tasks[u]
            part = unstacked(dot(grad_scores[u % 2], key_of(layer, j, n))) * HEAD**-0.5
            into(layer, j, n * couple, part)
            part = dot_tn(grad_scores[u % 2], queries[layer, j, n])[:padded]
            into(layer, j, features + n * couple, part)

        grad_weights(0)
        for u in range(len(tasks)):
            if u + 1 < len(tasks):
                grad_weights(u + 1)
            if u:
                attention_rest(u - 1)
            else:
                sum_att[layer, :, 3 * features :] += dot_tn(attended[layer], out_low[...])
            attention_value(u)
            soften_back(u)
        attention_rest(len(tasks) - 1)

        def norm_one(j):
            one, two = (jnp.zeros((8, features), F32) for _ in range(2))
            for at, size in row_chunks(padded, 16):
                lines = slice(j * padded + at, j * padded + at + size)
                grad = grad_norm[lines]
                dx, by_hat = norm_backward(hidden[layer, lines], grad, vec(layer, at_g1))
                one = one + fold(by_hat)
                two = two + fold(grad)
                value = grad_out[lines] + dx
                grad_out[lines] = value.astype(BF16).astype(F32)
            vec_one[layer, 32:40] += one
            vec_one[layer, 40:48] += two

        for j in range(GROUP):
            grad_norm[image[j]] = dot_nt(grad_joined[image[j]], w_qkv[layer])
        for c, columns in enumerate(spans(3 * features, 512)):
            sum_att[layer, :, columns] += dot_tn(normed[layer], grad_joined[:, columns])
            if c < GROUP:
                norm_one(c)
        for j in range(GROUP):
            leave(layer, 1, j, grad_out[j * padded : j * padded + tokens].astype(BF16))

    def store(layer, kind, target):
        stage = (wide, tall)[kind].at[layer]
        return pltpu.make_async_copy(stage, target, store_sem.at[layer, kind])

    def finish(layer):
        wide[layer, :, :units] = sum_up[layer].astype(BF16)
        wide[layer, :, units : units + 4 * features] = sum_att[layer].astype(BF16)
        line = lax.broadcasted_iota(jnp.int32, (128, features), 0)
        plain = jnp.zeros((128, features), F32)
        for n, group in enumerate((4, 5, 3, 1, 2, 0)):
            total = jnp.sum(vec_one[layer, 8 * group : 8 * group + 8], axis=0, keepdims=True)
            plain = plain + jnp.where(line == n, total, 0.0)
        qkv = jnp.sum(vec_qkv[layer], axis=0, keepdims=True)
        qv = jnp.concatenate([qkv[:, :features], qkv[:, 2 * features :]], axis=1)
        total_up = jnp.sum(vec_up[layer], axis=0, keepdims=True)
        columns = jnp.zeros((features, 128), F32)
        for first_line, total in ((0, plain), (6, qv), (8, total_up)):
            size = total.shape[1]
            each = size // features
            position = lax.broadcasted_iota(jnp.int32, (128, size), 1)
            row = lax.broadcasted_iota(jnp.int32, (128, size), 0)
            if each > 1:
                total = jnp.where(row - first_line == position % each, total, 0.0)
            target = lax.broadcasted_iota(jnp.int32, (features, size), 0)
            source = lax.broadcasted_iota(jnp.int32, (features, size), 1)
            pick = jnp.where(source // each == target, 1.0, 0.0).astype(BF16)
            columns = columns + dot_nt(pick, total.astype(BF16))
        wide[layer, :, units + 4 * features :] = columns.astype(BF16)

        def send(kind, mine, away):
            @pl.when(core == layer)
            def _():
                store(layer, kind, mine).start()

            @pl.when(core != layer)
            def _():
                store(layer, kind, away).start()

        send(0, mine_wide, away_wide)
        for columns in spans(units, features):
            tall[layer, columns, :] = sum_down[layer, :, columns].T.astype(BF16)
        send(1, mine_tall, away_tall)

    @pl.when(jnp.logical_not(running))
    def _():
        mine_ref[...] = jnp.zeros_like(mine_ref)
        away_ref[...] = jnp.zeros_like(away_ref)

    @pl.when(running)
    def _():
        for j in range(GROUP):
            tail = slice(j * padded + padded - 16, (j + 1) * padded)
            hidden[0, tail] = jnp.zeros((16, features), F32)
            hidden[0, j * padded : j * padded + tokens] = h_ref[0, j].astype(F32)
        lax.fori_loop(0, 2, lambda layer, carry: (forward(layer), carry)[1], 0)
        for j in range(GROUP):
            keep = jnp.where(step * GROUP + j < count, 1.0, 0.0)
            tail = slice(j * padded + padded - 16, (j + 1) * padded)
            grad_out[tail] = jnp.zeros((16, features), F32)
            grad_out[j * padded : j * padded + tokens] = cot_ref[0, j].astype(F32) * keep

    def second_half(at, carry):
        layer = 1 - at

        @pl.when(running)
        def _():
            backward(layer)

        @pl.when(step == last)
        def _():
            finish(layer)

        return carry

    lax.fori_loop(0, 2, second_half, 0)

    @pl.when(step == last)
    def _():
        for layer in range(2):
            for kind, mine in enumerate((mine_wide, mine_tall)):
                store(layer, kind, mine).wait()


def run_layers(meta, inputs, cotangent, vectors, weights):
    slots, tokens, features = inputs.shape[1:]
    padded = -(-tokens // 16) * 16
    keys = -(-tokens // 128) * 128
    heads = features // HEAD
    steps = slots // GROUP
    block = GROUP * padded
    units = weights[0][2].shape[2]
    packed = vectors[0].shape[1]
    wide = units + 4 * features + 128
    images = pl.BlockSpec((1, GROUP, tokens, features), lambda i, meta: (meta[1], i, 0, 0))
    kinds = pl.BlockSpec((2, GROUP, tokens, features), lambda i, meta: (0, i, 0, 0))
    vector = pl.BlockSpec((1, packed), lambda i, meta: (0, 0))
    anywhere = pl.BlockSpec(memory_space=pl.ANY)
    both = (
        ((features, 3 * features), BF16),
        ((features, features), BF16),
        ((features, units), BF16),
        ((units, features), BF16),
        ((packed,), F32),
    )
    saved = (
        ((block, features), BF16),
        ((GROUP, heads // 2, 2 * padded, 2 * HEAD), BF16),
        ((GROUP * keys, 2 * features), BF16),
        ((GROUP, heads // 2, 2 * padded, keys), BF16),
        ((block, features), BF16),
        ((block, features), F32),
        ((block, features), BF16),
        ((block, units), BF16),
        ((block, units), BF16),
    )
    sums = (
        ((features, units), F32),
        ((features, units), F32),
        ((features, 4 * features), F32),
        ((48, features), F32),
        ((8, units), F32),
        ((8, 3 * features), F32),
        ((features, wide), BF16),
        ((units, features), BF16),
    )

    def two(shapes):
        return [pltpu.VMEM((2,) + shape, kind) for shape, kind in shapes]

    scratch = (
        two(both)
        + [pltpu.VMEM((3, block, features), F32)]
        + two(saved)
        + [
            pltpu.VMEM((block, units), F32),
            pltpu.VMEM((block, features), F32),
            pltpu.VMEM((block, features), BF16),
            pltpu.VMEM((block, features), BF16),
            pltpu.VMEM((GROUP, heads // 2, 2 * padded, 2 * HEAD), BF16),
            pltpu.VMEM((block, units), BF16),
            pltpu.VMEM((block, 3 * features), BF16),
            pltpu.VMEM((block, features), F32),
            pltpu.VMEM((2, 2 * padded, keys), F32),
            pltpu.VMEM((2, 2 * padded, keys), BF16),
        ]
        + two(sums)
        + [pltpu.SemaphoreType.DMA((2, 4)), pltpu.SemaphoreType.DMA((2, 2))]
    )
    return pl.pallas_call(
        lambda *refs: layers_kernel(padded, keys, *refs),
        grid_spec=pltpu.PrefetchScalarGridSpec(
            num_scalar_prefetch=1,
            grid=(steps,),
            in_specs=[images, images, vector, vector] + [anywhere] * 8,
            out_specs=[kinds, kinds] + [anywhere] * 4,
            scratch_shapes=scratch,
        ),
        out_shape=[jax.ShapeDtypeStruct((2, slots, tokens, features), BF16)] * 2
        + [jax.ShapeDtypeStruct((features, wide), BF16)] * 2
        + [jax.ShapeDtypeStruct((units, features), BF16)] * 2,
        compiler_params=pltpu.CompilerParams(
            vmem_limit_bytes=VMEM_LIMIT, dimension_semantics=("arbitrary",)
        ),
        cost_estimate=pl.CostEstimate(
            flops=80_000_000_000, bytes_accessed=30_000_000, transcendentals=0
        ),
    )(meta, inputs, cotangent, *vectors, *weights[0], *weights[1])


def pack_vectors(arrays):
    total = sum(a.shape[1] for a in arrays)

    def body(*refs):
        at = 0
        for ref in refs[:-1]:
            refs[-1][:, at : at + ref.shape[1]] = ref[...]
            at += ref.shape[1]

    return pl.pallas_call(body, out_shape=jax.ShapeDtypeStruct((1, total), F32))(*arrays)


def swap_cores(block):
    return lax.ppermute(block, "segment", [(0, 1), (1, 0)])


def reduce_shards(mine, got, orders, first):
    dp = lax.axis_size("dp")
    me = lax.axis_index("dp")
    bits = dp.bit_length() - 1
    rest = (mine.shape[0] // dp, mine.shape[1])
    block = (mine, got)
    held = [list(range(bits)) for _ in orders]
    for n in range(bits):
        below = [left.index(order[n]) for order, left in zip(orders, held)]
        bit = [(me >> order[n]) & 1 for order in orders]
        for order, left in zip(orders, held):
            left.remove(order[n])

        def part(at, index):
            total = 0.0
            for term in block:
                view = term.reshape((-1, 2, 1 << at) + rest)
                taken = lax.dynamic_index_in_dim(view, index, 1, keepdims=False)
                total = total + taken.reshape((-1,) + rest).astype(F32)
            return total

        if below[0] == below[1]:
            mine = jnp.where(first, bit[0], bit[1])
            keep, send = part(below[0], mine), part(below[0], 1 - mine)
        else:
            keep = jnp.where(first, part(below[0], bit[0]), part(below[1], bit[1]))
            send = jnp.where(first, part(below[0], 1 - bit[0]), part(below[1], 1 - bit[1]))
        route = [
            (core * dp + i, core * dp + (i ^ (1 << order[n])))
            for core, order in enumerate(orders)
            for i in range(dp)
        ]
        arrived = lax.ppermute(send.astype(BF16), ("segment", "dp"), route)
        total = keep + arrived.astype(F32)
        block = (total.astype(BF16),)
    return total.reshape(rest)


def on_device(inputs, image_count, cotangent, *params):
    dp = lax.axis_size("dp")
    core = lax.axis_index("segment")
    first = core == 0
    features = inputs.shape[3]
    g1, b1, w_qkv, b_qv, w_out, b_out, g2, b2, w_up, b_up, w_down, b_down = params
    units = w_up.shape[2]
    own_weights = (w_qkv, w_out, w_up, w_down)
    got_weights = tuple(swap_cores(w) for w in own_weights)
    zeros = jnp.zeros((1, features), F32)
    own_vec = pack_vectors(
        [g1, b1, b_qv[:, :features], zeros, b_qv[:, features:], b_out, g2, b2, b_down, b_up]
    )
    got_vec = swap_cores(own_vec)
    count = lax.dynamic_index_in_dim(image_count[:, 0], core, 0, keepdims=False)
    meta = jnp.stack([count, core.astype(jnp.int32)])
    mine, away, mine_wide, away_wide, mine_tall, away_tall = run_layers(
        meta, inputs, cotangent, (own_vec, got_vec), (own_weights, got_weights)
    )
    got_wide = swap_cores(away_wide)
    away_tall, got_wide = lax.optimization_barrier((away_tall, got_wide))
    got_tall = swap_cores(away_tall)
    got = swap_cores(away)
    bits = dp.bit_length() - 1
    near = list(range(min(bits, 3)))
    far = list(range(len(near), bits))

    def turned(by):
        return near[by % len(near) :] + near[: by % len(near)] + far

    wide = reduce_shards(mine_wide, got_wide, (turned(0), turned(2)), first)
    tall = reduce_shards(mine_tall, got_tall, (turned(1), turned(1)), first)
    both = jnp.stack([jnp.where(first, mine, got), jnp.where(first, got, mine)], axis=1)
    share = features // dp
    g_up = wide[:, :units]
    g_qkv = wide[:, units : units + 3 * features]
    g_out = wide[:, units + 3 * features : units + 4 * features]
    columns = wide[:, units + 4 * features :]
    ln1_gain, ln1_bias, g_bo, ln2_gain, ln2_bias, g_bd = (columns[:, n] for n in range(6))
    g_bqv = columns[:, 6:8].reshape(2 * share)
    g_bup = columns[:, 8 : 8 + units // features].reshape(-1)
    outs = (ln1_gain, ln1_bias, g_qkv, g_bqv, g_out, g_bo, ln2_gain, ln2_bias, g_up, g_bup, tall, g_bd)
    return (both[0][None], both[1][None]) + tuple(o[None] for o in outs)


def solution(mesh):
    in_specs = (
        P(None, "dp", None, None),
        P(None, "dp"),
        P(None, "dp", None, None),
        P("segment", None),
        P("segment", None),
        P("segment", None, None),
        P("segment", None),
        P("segment", None, None),
        P("segment", None),
        P("segment", None),
        P("segment", None),
        P("segment", None, None),
        P("segment", None),
        P("segment", None, None),
        P("segment", None),
    )
    out_specs = (
        P("segment", None, "dp", None, None),
        P("segment", None, "dp", None, None),
        P("segment", "dp"),
        P("segment", "dp"),
        P("segment", "dp", None),
        P("segment", "dp"),
        P("segment", "dp", None),
        P("segment", "dp"),
        P("segment", "dp"),
        P("segment", "dp"),
        P("segment", "dp", None),
        P("segment", "dp"),
        P("segment", "dp", None),
        P("segment", "dp"),
    )
    return jax.shard_map(
        on_device, mesh=mesh, in_specs=in_specs, out_specs=out_specs, check_vma=False
    )
```

```python
import jax
import jax.numpy as jnp
from jax import lax
from jax.experimental import pallas as pl
from jax.experimental.pallas import tpu as pltpu
from jax.sharding import PartitionSpec as P

HEAD = 64
EPSILON = 1e-06
BF16 = jnp.bfloat16
F32 = jnp.float32
GROUP = 2
VMEM_LIMIT = 62 * 1024 * 1024


def dot(a, b):
    return lax.dot_general(a, b, (((1,), (0,)), ((), ())), preferred_element_type=F32)


def dot_nt(a, b):
    return lax.dot_general(a, b, (((1,), (1,)), ((), ())), preferred_element_type=F32)


def dot_tn(a, b):
    return lax.dot_general(a, b, (((0,), (0,)), ((), ())), preferred_element_type=F32)


def normalized(rows):
    centered = rows - jnp.mean(rows, axis=-1, keepdims=True)
    spread = jnp.mean(centered * centered, axis=-1, keepdims=True)
    inverse = lax.rsqrt(spread + EPSILON)
    return centered * inverse, inverse


def norm_backward(rows, grad, gain):
    hat, inverse = normalized(rows)
    scaled = grad * gain
    inner = jnp.mean(scaled * hat, axis=-1, keepdims=True)
    dx = inverse * (scaled - jnp.mean(scaled, axis=-1, keepdims=True) - hat * inner)
    return dx, grad * hat


def reciprocal(x):
    guess = pl.reciprocal(x, approx=True)
    return guess * (2.0 - x * guess)


def gelu_and_slope(x):
    bell = jnp.exp(x * x * -0.5)
    t = reciprocal(1.0 + jnp.abs(x) * (0.3275911 * 0.7071067811865476))
    poly = t * (
        0.5 * 0.254829592
        + t
        * (
            0.5 * -0.284496736
            + t * (0.5 * 1.421413741 + t * (0.5 * -1.453152027 + t * (0.5 * 1.061405429)))
        )
    )
    tail = poly * bell
    cdf = jnp.where(x >= 0.0, 1.0 - tail, tail)
    return x * cdf, cdf + x * (bell * 0.3989422804014327)


def fold(rows):
    total = rows[0:8]
    for at in range(8, rows.shape[0], 8):
        total = total + rows[at : at + 8]
    return total


def row_chunks(total, size=64):
    return [(at, min(size, total - at)) for at in range(0, total, size)]


def spans(total, width):
    return [slice(at, min(at + width, total)) for at in range(0, total, width)]


def layers_kernel(
    padded,
    keys,
    counts,
    which,
    h_ref,
    cot_ref,
    own_vec,
    got_vec,
    own_qkv,
    own_out,
    own_up,
    own_down,
    got_qkv,
    got_out,
    got_up,
    got_down,
    mine_ref,
    away_ref,
    mine_wide,
    away_wide,
    mine_tall,
    away_tall,
    w_qkv,
    w_out,
    w_up,
    w_down,
    vecs,
    hidden,
    normed,
    queries,
    kv,
    weights,
    attended,
    middle,
    second,
    active,
    slope,
    before,
    grad_out,
    grad_low,
    out_low,
    grad_heads,
    grad_before,
    grad_joined,
    grad_norm,
    scores,
    grad_scores,
    sum_up,
    sum_down,
    sum_att,
    vec_one,
    vec_up,
    vec_qkv,
    wide,
    tall,
    load_sem,
    store_sem,
):
    step = pl.program_id(0)
    last = pl.num_programs(0) - 1
    core = which[0]
    count = counts[core]
    running = step * GROUP < count
    tokens, features = h_ref.shape[2:]
    heads = features // HEAD
    rows = GROUP * padded
    units = w_up.shape[2]
    couple = 2 * HEAD
    own = (own_qkv, own_out, own_up, own_down)
    got = (got_qkv, got_out, got_up, got_down)
    held = (w_qkv, w_out, w_up, w_down)
    at_g1, at_b1, at_qkv = 0, features, 2 * features
    at_bo, at_g2, at_b2, at_bd, at_up = (n * features for n in (5, 6, 7, 8, 9))

    def vec(layer, at, size=features):
        return vecs[pl.ds(layer, 1), at : at + size]

    def load(source, n, layer):
        return pltpu.make_async_copy(source[n].at[0], held[n].at[layer], load_sem.at[layer, n])

    @pl.when(step == 0)
    def _():
        for layer in range(2):
            for n in range(4):

                @pl.when(core == layer)
                def _():
                    load(own, n, layer).start()

                @pl.when(core != layer)
                def _():
                    load(got, n, layer).start()

        for layer in range(2):
            mine = jnp.full(own_vec.shape, core == layer)
            vecs[layer : layer + 1] = jnp.where(mine, own_vec[...], got_vec[...])
        for ref in (sum_up, sum_down, sum_att, vec_one, vec_up, vec_qkv):
            for layer in range(2):
                ref[layer] = jnp.zeros(ref.shape[1:], F32)
        for layer in range(2):
            for j in range(GROUP):
                kv[layer, j * keys + padded : (j + 1) * keys] = jnp.zeros(
                    (keys - padded, 2 * features), BF16
                )

    def leave(layer, kind, j, value):
        @pl.when(core == layer)
        def _():
            mine_ref[kind, j] = value

        @pl.when(core != layer)
        def _():
            away_ref[kind, j] = value

    lane = lax.broadcasted_iota(jnp.int32, (padded, couple), 1)
    left = lane < HEAD
    image = [slice(j * padded, (j + 1) * padded) for j in range(GROUP)]
    images_keys = [slice(j * keys, (j + 1) * keys) for j in range(GROUP)]
    pairs = [slice(n * couple, (n + 1) * couple) for n in range(heads // 2)]
    tasks = [(j, n) for j in range(GROUP) for n in range(heads // 2)]
    chunks = spans(units, 512)

    def stacked(value):
        nothing = jnp.zeros_like(value)
        return jnp.where(left, value, nothing), jnp.where(left, nothing, value)

    def key_of(layer, j, n):
        return kv[layer, images_keys[j], pairs[n]]

    def value_of(layer, j, n):
        at = features + n * couple
        return kv[layer, images_keys[j], at : at + couple]

    def unstacked(value):
        return jnp.where(left, value[:padded], value[padded:])

    def forward(layer):
        @pl.when(step == 0)
        def _():
            for n in range(4):
                load(own, n, layer).wait()

        for at, size in row_chunks(rows):
            hat, _ = normalized(hidden[layer, at : at + size])
            value = hat * vec(layer, at_g1) + vec(layer, at_b1)
            normed[layer, at : at + size] = value.astype(BF16)
        value = dot(normed[layer], w_qkv[layer, :, :features]) + vec(layer, at_qkv)
        value = value.astype(BF16) * jnp.asarray(HEAD**-0.5, BF16)
        for j, n in tasks:
            for half, part in enumerate(stacked(value[image[j], pairs[n]])):
                queries[layer, j, n, half * padded : (half + 1) * padded] = part
        for columns in spans(2 * features, 512):
            at, size = features + columns.start, columns.stop - columns.start
            value = dot(normed[layer], w_qkv[layer, :, at : at + size])
            value = (value + vec(layer, at_qkv + at, size)).astype(BF16)
            for j in range(GROUP):
                kv[layer, j * keys : j * keys + padded, columns] = value[image[j]]

        def score(u):
            j, n = tasks[u]
            scores[u % 2] = dot_nt(queries[layer, j, n], key_of(layer, j, n))

        def soften(u):
            j, n = tasks[u]
            for at, size in row_chunks(2 * padded):
                real = lax.broadcasted_iota(jnp.int32, (size, keys), 1) < tokens
                s = jnp.where(real, scores[u % 2, at : at + size], -1e30)
                e = jnp.exp(s - jnp.max(s, axis=-1, keepdims=True))
                p = e * reciprocal(jnp.sum(e, axis=-1, keepdims=True))
                weights[layer, j, n, at : at + size] = p.astype(BF16)

        def attend(u):
            j, n = tasks[u]
            value = unstacked(dot(weights[layer, j, n], value_of(layer, j, n)))
            attended[layer, image[j], pairs[n]] = value.astype(BF16)

        def project(j):
            middle[layer, image[j]] = dot(attended[layer, image[j]], w_out[layer])

        def norm_two(j):
            for at, size in row_chunks(padded):
                at = j * padded + at
                value = middle[layer, at : at + size] + hidden[layer, at : at + size]
                value = value + vec(layer, at_bo)
                middle[layer, at : at + size] = value
                hat, _ = normalized(value)
                value = hat * vec(layer, at_g2) + vec(layer, at_b2)
                second[layer, at : at + size] = value.astype(BF16)

        score(0)
        for u in range(len(tasks)):
            if u + 1 < len(tasks):
                score(u + 1)
            if u:
                attend(u - 1)
                if tasks[u - 1][1] == heads // 2 - 1:
                    project(tasks[u - 1][0])
            soften(u)
            if u and tasks[u - 1][1] == heads // 2 - 1:
                norm_two(tasks[u - 1][0])
        attend(len(tasks) - 1)
        project(GROUP - 1)
        norm_two(GROUP - 1)

        def up(c):
            before[:, chunks[c]] = dot(second[layer], w_up[layer, :, chunks[c]])

        def curve(c):
            columns = chunks[c]
            for at, size in row_chunks(rows, 16):
                value, change = gelu_and_slope(
                    before[at : at + size, columns]
                    + vec(layer, at_up + columns.start, columns.stop - columns.start)
                )
                active[layer, at : at + size, columns] = value.astype(BF16)
                slope[layer, at : at + size, columns] = change.astype(BF16)

        def down(c):
            value = dot(active[layer, :, chunks[c]], w_down[layer, chunks[c]])
            if c:
                value = value + grad_norm[...]
            grad_norm[...] = value

        up(0)
        for c in range(len(chunks)):
            if c + 1 < len(chunks):
                up(c + 1)
            if c:
                down(c - 1)
            curve(c)
        down(len(chunks) - 1)
        for j in range(GROUP):
            keep = jnp.where(step * GROUP + j < count, 1.0, 0.0)
            result = grad_norm[image[j]] + middle[layer, image[j]]
            result = ((result + vec(layer, at_bd)) * keep).astype(BF16)
            leave(layer, 0, j, result[:tokens])
            hidden[layer + 1, image[j]] = result.astype(F32)

    def backward(layer):
        for at, size in row_chunks(rows):
            value = grad_out[at : at + size]
            grad_low[at : at + size] = value.astype(BF16)
            vec_one[layer, 0:8] += fold(value)

        def activation(c):
            before[:, chunks[c]] = dot_nt(grad_low[...], w_down[layer, chunks[c]])

        def multiply(c):
            columns = chunks[c]
            total = jnp.zeros((8, columns.stop - columns.start), F32)
            for at, size in row_chunks(rows, 16):
                lines = slice(at, at + size)
                piece = before[lines, columns] * slope[layer, lines, columns].astype(F32)
                piece = piece.astype(BF16)
                grad_before[lines, columns] = piece
                total = total + fold(piece.astype(F32))
            vec_up[layer, :, columns] += total

        activation(0)
        for c in range(len(chunks)):
            if c + 1 < len(chunks):
                activation(c + 1)
            sum_down[layer, :, chunks[c]] += dot_tn(grad_low[...], active[layer, :, chunks[c]])
            multiply(c)

        def norm_two(j):
            one, two, three = (jnp.zeros((8, features), F32) for _ in range(3))
            for at, size in row_chunks(padded):
                lines = slice(j * padded + at, j * padded + at + size)
                grad = grad_norm[lines]
                dx, by_hat = norm_backward(middle[layer, lines], grad, vec(layer, at_g2))
                one = one + fold(by_hat)
                two = two + fold(grad)
                value = grad_out[lines] + dx
                grad_out[lines] = value
                value = value.astype(BF16)
                out_low[lines] = value
                three = three + fold(value.astype(F32))
            vec_one[layer, 8:16] += one
            vec_one[layer, 16:24] += two
            vec_one[layer, 24:32] += three

        for j in range(GROUP):
            grad_norm[image[j]] = dot_nt(grad_before[image[j]], w_up[layer])
        for c in range(len(chunks)):
            sum_up[layer, :, chunks[c]] += dot_tn(second[layer], grad_before[:, chunks[c]])
            if c < GROUP:
                norm_two(c)
        for j in range(GROUP):
            value = dot_nt(out_low[image[j]], w_out[layer]).astype(BF16)
            for n in range(heads // 2):
                for half, part in enumerate(stacked(value[:, pairs[n]])):
                    grad_heads[j, n, half * padded : (half + 1) * padded] = part

        def grad_weights(u):
            j, n = tasks[u]
            scores[u % 2] = dot_nt(grad_heads[j, n], value_of(layer, j, n))

        def soften_back(u):
            j, n = tasks[u]
            for at, size in row_chunks(2 * padded):
                p = weights[layer, j, n, at : at + size].astype(F32)
                by = p * scores[u % 2, at : at + size]
                by = by - p * jnp.sum(by, axis=-1, keepdims=True)
                grad_scores[u % 2, at : at + size] = by.astype(BF16)

        def into(layer, j, column, part):
            part = part.astype(BF16)
            grad_joined[image[j], column : column + couple] = part
            vec_qkv[layer, :, column : column + couple] += fold(part.astype(F32))

        def attention_value(u):
            j, n = tasks[u]
            part = dot_tn(weights[layer, j, n], grad_heads[j, n])[:padded]
            into(layer, j, 2 * features + n * couple, part)

        def attention_rest(u):
            j, n = tasks[u]
            part = unstacked(dot(grad_scores[u % 2], key_of(layer, j, n))) * HEAD**-0.5
            into(layer, j, n * couple, part)
            part = dot_tn(grad_scores[u % 2], queries[layer, j, n])[:padded]
            into(layer, j, features + n * couple, part)

        grad_weights(0)
        for u in range(len(tasks)):
            if u + 1 < len(tasks):
                grad_weights(u + 1)
            if u:
                attention_rest(u - 1)
            else:
                sum_att[layer, :, 3 * features :] += dot_tn(attended[layer], out_low[...])
            attention_value(u)
            soften_back(u)
        attention_rest(len(tasks) - 1)

        def norm_one(j):
            one, two = (jnp.zeros((8, features), F32) for _ in range(2))
            for at, size in row_chunks(padded):
                lines = slice(j * padded + at, j * padded + at + size)
                grad = grad_norm[lines]
                dx, by_hat = norm_backward(hidden[layer, lines], grad, vec(layer, at_g1))
                one = one + fold(by_hat)
                two = two + fold(grad)
                value = grad_out[lines] + dx
                grad_out[lines] = value.astype(BF16).astype(F32)
            vec_one[layer, 32:40] += one
            vec_one[layer, 40:48] += two

        for j in range(GROUP):
            grad_norm[image[j]] = dot_nt(grad_joined[image[j]], w_qkv[layer])
        for c, columns in enumerate(spans(3 * features, 512)):
            sum_att[layer, :, columns] += dot_tn(normed[layer], grad_joined[:, columns])
            if c < GROUP:
                norm_one(c)
        for j in range(GROUP):
            leave(layer, 1, j, grad_out[j * padded : j * padded + tokens].astype(BF16))

    def store(layer, kind, target):
        stage = (wide, tall)[kind].at[layer]
        return pltpu.make_async_copy(stage, target, store_sem.at[layer, kind])

    def finish(layer):
        wide[layer, :, :units] = sum_up[layer].astype(BF16)
        wide[layer, :, units : units + 4 * features] = sum_att[layer].astype(BF16)
        line = lax.broadcasted_iota(jnp.int32, (128, features), 0)
        plain = jnp.zeros((128, features), F32)
        for n, group in enumerate((4, 5, 3, 1, 2, 0)):
            total = jnp.sum(vec_one[layer, 8 * group : 8 * group + 8], axis=0, keepdims=True)
            plain = plain + jnp.where(line == n, total, 0.0)
        qkv = jnp.sum(vec_qkv[layer], axis=0, keepdims=True)
        qv = jnp.concatenate([qkv[:, :features], qkv[:, 2 * features :]], axis=1)
        total_up = jnp.sum(vec_up[layer], axis=0, keepdims=True)
        columns = jnp.zeros((features, 128), F32)
        for first_line, total in ((0, plain), (6, qv), (8, total_up)):
            size = total.shape[1]
            each = size // features
            position = lax.broadcasted_iota(jnp.int32, (128, size), 1)
            row = lax.broadcasted_iota(jnp.int32, (128, size), 0)
            if each > 1:
                total = jnp.where(row - first_line == (position & (each - 1)), total, 0.0)
            target = lax.broadcasted_iota(jnp.int32, (features, size), 0)
            source = lax.broadcasted_iota(jnp.int32, (features, size), 1)
            inside = (source >= target * each) & (source < target * each + each)
            pick = jnp.where(inside, 1.0, 0.0).astype(BF16)
            columns = columns + dot_nt(pick, total.astype(BF16))
        wide[layer, :, units + 4 * features :] = columns.astype(BF16)

        def send(kind, mine, away):
            @pl.when(core == layer)
            def _():
                store(layer, kind, mine).start()

            @pl.when(core != layer)
            def _():
                store(layer, kind, away).start()

        send(0, mine_wide, away_wide)
        for columns in spans(units, features):
            tall[layer, columns, :] = sum_down[layer, :, columns].T.astype(BF16)
        send(1, mine_tall, away_tall)

    @pl.when(jnp.logical_not(running))
    def _():
        mine_ref[...] = jnp.zeros_like(mine_ref)
        away_ref[...] = jnp.zeros_like(away_ref)

    @pl.when(running)
    def _():
        for j in range(GROUP):
            tail = slice(j * padded + padded - 16, (j + 1) * padded)
            hidden[0, tail] = jnp.zeros((16, features), F32)
            hidden[0, j * padded : j * padded + tokens] = h_ref[0, j].astype(F32)
        lax.fori_loop(0, 2, lambda layer, carry: (forward(layer), carry)[1], 0)
        for j in range(GROUP):
            keep = jnp.where(step * GROUP + j < count, 1.0, 0.0)
            tail = slice(j * padded + padded - 16, (j + 1) * padded)
            grad_out[tail] = jnp.zeros((16, features), F32)
            grad_out[j * padded : j * padded + tokens] = cot_ref[0, j].astype(F32) * keep

    def second_half(at, carry):
        layer = 1 - at

        @pl.when(running)
        def _():
            backward(layer)

        @pl.when(step == last)
        def _():
            finish(layer)

        return carry

    lax.fori_loop(0, 2, second_half, 0)

    @pl.when(step == last)
    def _():
        for layer in range(2):
            for kind, mine in enumerate((mine_wide, mine_tall)):
                store(layer, kind, mine).wait()


def run_layers(counts, which, inputs, cotangent, vectors, weights):
    slots, tokens, features = inputs.shape[1:]
    padded = -(-tokens // 16) * 16
    keys = -(-tokens // 128) * 128
    heads = features // HEAD
    steps = slots // GROUP
    block = GROUP * padded
    units = weights[0][2].shape[2]
    packed = vectors[0].shape[1]
    wide = units + 4 * features + 128
    images = pl.BlockSpec((1, GROUP, tokens, features), lambda i, counts, which: (which[0], i, 0, 0))
    kinds = pl.BlockSpec((2, GROUP, tokens, features), lambda i, counts, which: (0, i, 0, 0))
    vector = pl.BlockSpec((1, packed), lambda i, counts, which: (0, 0))
    anywhere = pl.BlockSpec(memory_space=pl.ANY)
    both = (
        ((features, 3 * features), BF16),
        ((features, features), BF16),
        ((features, units), BF16),
        ((units, features), BF16),
        ((packed,), F32),
    )
    saved = (
        ((block, features), BF16),
        ((GROUP, heads // 2, 2 * padded, 2 * HEAD), BF16),
        ((GROUP * keys, 2 * features), BF16),
        ((GROUP, heads // 2, 2 * padded, keys), BF16),
        ((block, features), BF16),
        ((block, features), F32),
        ((block, features), BF16),
        ((block, units), BF16),
        ((block, units), BF16),
    )
    sums = (
        ((features, units), F32),
        ((features, units), F32),
        ((features, 4 * features), F32),
        ((48, features), F32),
        ((8, units), F32),
        ((8, 3 * features), F32),
        ((features, wide), BF16),
        ((units, features), BF16),
    )

    def two(shapes):
        return [pltpu.VMEM((2,) + shape, kind) for shape, kind in shapes]

    scratch = (
        two(both)
        + [pltpu.VMEM((3, block, features), F32)]
        + two(saved)
        + [
            pltpu.VMEM((block, units), F32),
            pltpu.VMEM((block, features), F32),
            pltpu.VMEM((block, features), BF16),
            pltpu.VMEM((block, features), BF16),
            pltpu.VMEM((GROUP, heads // 2, 2 * padded, 2 * HEAD), BF16),
            pltpu.VMEM((block, units), BF16),
            pltpu.VMEM((block, 3 * features), BF16),
            pltpu.VMEM((block, features), F32),
            pltpu.VMEM((2, 2 * padded, keys), F32),
            pltpu.VMEM((2, 2 * padded, keys), BF16),
        ]
        + two(sums)
        + [pltpu.SemaphoreType.DMA((2, 4)), pltpu.SemaphoreType.DMA((2, 2))]
    )
    return pl.pallas_call(
        lambda *refs: layers_kernel(padded, keys, *refs),
        grid_spec=pltpu.PrefetchScalarGridSpec(
            num_scalar_prefetch=2,
            grid=(steps,),
            in_specs=[images, images, vector, vector] + [anywhere] * 8,
            out_specs=[kinds, kinds] + [anywhere] * 4,
            scratch_shapes=scratch,
        ),
        out_shape=[jax.ShapeDtypeStruct((2, slots, tokens, features), BF16)] * 2
        + [jax.ShapeDtypeStruct((features, wide), BF16)] * 2
        + [jax.ShapeDtypeStruct((units, features), BF16)] * 2,
        compiler_params=pltpu.CompilerParams(
            vmem_limit_bytes=VMEM_LIMIT, dimension_semantics=("arbitrary",)
        ),
        cost_estimate=pl.CostEstimate(
            flops=80_000_000_000, bytes_accessed=30_000_000, transcendentals=0
        ),
    )(counts, which, inputs, cotangent, *vectors, *weights[0], *weights[1])


def pack_vectors(g1, b1, b_qv, *rest):
    features = g1.shape[1]
    arrays = (g1, b1, b_qv) + rest
    total = sum(a.shape[1] for a in arrays) + features

    def body(*refs):
        out = refs[-1]
        at = 0
        for n, ref in enumerate(refs[:-1]):
            if n == 2:
                out[:, at : at + features] = ref[:, :features]
                out[:, at + features : at + 2 * features] = jnp.zeros((1, features), F32)
                out[:, at + 2 * features : at + 3 * features] = ref[:, features:]
                at += 3 * features
            else:
                out[:, at : at + ref.shape[1]] = ref[...]
                at += ref.shape[1]

    return pl.pallas_call(body, out_shape=jax.ShapeDtypeStruct((1, total), F32))(*arrays)


def swap_cores(block):
    return lax.ppermute(block, "segment", [(0, 1), (1, 0)])


def reduce_shards(mine, got, orders, first):
    dp = lax.axis_size("dp")
    me = lax.axis_index("dp")
    bits = dp.bit_length() - 1
    rest = (mine.shape[0] // dp, mine.shape[1])
    terms = (mine, got)
    held = [list(range(bits)) for _ in orders]
    first_send = None
    for n in range(bits):
        below = [left.index(order[n]) for order, left in zip(orders, held)]
        bit = [(me >> order[n]) & 1 for order in orders]
        for order, left in zip(orders, held):
            left.remove(order[n])

        def slices(at, index):
            taken = []
            for term in terms:
                view = term.reshape((-1, 2, 1 << at) + rest)
                part = lax.dynamic_index_in_dim(view, index, 1, keepdims=False)
                taken.append(part.reshape((-1,) + rest))
            return taken

        def half(other):
            if below[0] == below[1]:
                index = jnp.where(first, bit[0], bit[1])
                taken = slices(below[0], 1 - index if other else index)
            else:
                index = [1 - b if other else b for b in bit]
                sides = zip(slices(below[0], index[0]), slices(below[1], index[1]))
                taken = [jnp.where(first, a, b) for a, b in sides]
            total = sum(part.astype(F32) for part in taken)
            return total.astype(BF16)

        send = half(True)
        first_send = send if n == 0 else first_send
        keep = half(False)
        if n == 0:
            keep, _ = lax.optimization_barrier((keep, send))
        route = [
            (core * dp + i, core * dp + (i ^ (1 << order[n])))
            for core, order in enumerate(orders)
            for i in range(dp)
        ]
        arrived = lax.ppermute(send, ("segment", "dp"), route)
        terms = (keep, arrived)
    return tuple(t.reshape(rest) for t in terms), first_send


def split_wide(terms, features, units):
    share = terms[0].shape[0]
    plain = 6

    def body(one, two, up, qkv, out, qv, bias_up, *vectors):
        total = one[...].astype(F32) + two[...].astype(F32)
        up[0] = total[:, :units]
        qkv[0] = total[:, units : units + 3 * features]
        out[0] = total[:, units + 3 * features : units + 4 * features]
        columns = total[:, units + 4 * features :]

        def spread(ref, first_column):
            size = ref.shape[1]
            width = size // share
            lane = lax.broadcasted_iota(jnp.int32, (share, size), 1)
            row = lax.broadcasted_iota(jnp.int32, (share, size), 0)
            value = jnp.zeros((share, size), F32)
            for n in range(width):
                column = columns[:, first_column + n : first_column + n + 1]
                value = value + jnp.where(lane == row * width + n, column, 0.0)
            ref[...] = jnp.sum(value, axis=0, keepdims=True)

        for n, ref in enumerate(vectors):
            spread(ref, n)
        spread(qv, plain)
        spread(bias_up, plain + 2)

    shapes = [(1, share, units), (1, share, 3 * features), (1, share, features)]
    shapes += [(1, 2 * share), (1, units // features * share)] + [(1, share)] * plain
    return pl.pallas_call(
        body, out_shape=[jax.ShapeDtypeStruct(shape, F32) for shape in shapes]
    )(*terms)


def on_device(inputs, image_count, cotangent, *params):
    dp = lax.axis_size("dp")
    core = lax.axis_index("segment")
    first = core == 0
    features = inputs.shape[3]
    g1, b1, w_qkv, b_qv, w_out, b_out, g2, b2, w_up, b_up, w_down, b_down = params
    units = w_up.shape[2]
    own_weights = (w_qkv, w_out, w_up, w_down)
    got_weights = tuple(swap_cores(w) for w in own_weights)
    own_vec = pack_vectors(g1, b1, b_qv, b_out, g2, b2, b_down, b_up)
    got_vec = swap_cores(own_vec)
    counts, which = image_count.reshape(-1), core.astype(jnp.int32).reshape(1)
    mine, away, mine_wide, away_wide, mine_tall, away_tall = run_layers(
        counts, which, inputs, cotangent, (own_vec, got_vec), (own_weights, got_weights)
    )
    got_wide = swap_cores(away_wide)
    away_tall, got_wide = lax.optimization_barrier((away_tall, got_wide))
    got_tall = swap_cores(away_tall)
    got = swap_cores(away)
    bits = dp.bit_length() - 1
    near = list(range(min(bits, 3)))
    far = list(range(len(near), bits))

    def turned(by):
        return near[by % len(near) :] + near[: by % len(near)] + far

    wide, _ = reduce_shards(mine_wide, got_wide, (turned(0), turned(2)), first)
    tall, tall_sent = reduce_shards(mine_tall, got_tall, (turned(1), turned(1)), first)
    got, _ = lax.optimization_barrier((got, tall_sent))
    both = jnp.stack([jnp.where(first, mine, got), jnp.where(first, got, mine)], axis=1)
    g_up, g_qkv, g_out, g_bqv, g_bup, *vectors = split_wide(wide, features, units)
    ln1_gain, ln1_bias, g_bo, ln2_gain, ln2_bias, g_bd = vectors
    g_down = (tall[0].astype(F32) + tall[1].astype(F32))[None]
    outs = (ln1_gain, ln1_bias, g_qkv, g_bqv, g_out, g_bo, ln2_gain, ln2_bias, g_up, g_bup)
    return (both[0][None], both[1][None]) + outs + (g_down, g_bd)


def solution(mesh):
    in_specs = (
        P(None, "dp", None, None),
        P(None, "dp"),
        P(None, "dp", None, None),
        P("segment", None),
        P("segment", None),
        P("segment", None, None),
        P("segment", None),
        P("segment", None, None),
        P("segment", None),
        P("segment", None),
        P("segment", None),
        P("segment", None, None),
        P("segment", None),
        P("segment", None, None),
        P("segment", None),
    )
    out_specs = (
        P("segment", None, "dp", None, None),
        P("segment", None, "dp", None, None),
        P("segment", "dp"),
        P("segment", "dp"),
        P("segment", "dp", None),
        P("segment", "dp"),
        P("segment", "dp", None),
        P("segment", "dp"),
        P("segment", "dp"),
        P("segment", "dp"),
        P("segment", "dp", None),
        P("segment", "dp"),
        P("segment", "dp", None),
        P("segment", "dp"),
    )
    return jax.shard_map(
        on_device, mesh=mesh, in_specs=in_specs, out_specs=out_specs, check_vma=False
    )
```

```python
import jax
import jax.numpy as jnp
from jax import lax
from jax.experimental import pallas as pl
from jax.experimental.pallas import tpu as pltpu
from jax.sharding import PartitionSpec as P

HEAD = 64
EPSILON = 1e-06
BF16 = jnp.bfloat16
F32 = jnp.float32
GROUP = 2
VMEM_LIMIT = 62 * 1024 * 1024


def dot(a, b):
    return lax.dot_general(a, b, (((1,), (0,)), ((), ())), preferred_element_type=F32)


def dot_nt(a, b):
    return lax.dot_general(a, b, (((1,), (1,)), ((), ())), preferred_element_type=F32)


def dot_tn(a, b):
    return lax.dot_general(a, b, (((0,), (0,)), ((), ())), preferred_element_type=F32)


def normalized(rows):
    centered = rows - jnp.mean(rows, axis=-1, keepdims=True)
    spread = jnp.mean(centered * centered, axis=-1, keepdims=True)
    inverse = lax.rsqrt(spread + EPSILON)
    return centered * inverse, inverse


def norm_backward(rows, grad, gain):
    hat, inverse = normalized(rows)
    scaled = grad * gain
    inner = jnp.mean(scaled * hat, axis=-1, keepdims=True)
    dx = inverse * (scaled - jnp.mean(scaled, axis=-1, keepdims=True) - hat * inner)
    return dx, grad * hat


def reciprocal(x):
    guess = pl.reciprocal(x, approx=True)
    return guess * (2.0 - x * guess)


def gelu_and_slope(x):
    bell = jnp.exp(x * x * -0.5)
    t = reciprocal(1.0 + jnp.abs(x) * (0.3275911 * 0.7071067811865476))
    poly = t * (
        0.5 * 0.254829592
        + t
        * (
            0.5 * -0.284496736
            + t * (0.5 * 1.421413741 + t * (0.5 * -1.453152027 + t * (0.5 * 1.061405429)))
        )
    )
    tail = poly * bell
    cdf = jnp.where(x >= 0.0, 1.0 - tail, tail)
    return x * cdf, cdf + x * (bell * 0.3989422804014327)


def fold(rows):
    total = rows[0:8]
    for at in range(8, rows.shape[0], 8):
        total = total + rows[at : at + 8]
    return total


def row_chunks(total, size=64):
    return [(at, min(size, total - at)) for at in range(0, total, size)]


def spans(total, width):
    return [slice(at, min(at + width, total)) for at in range(0, total, width)]


def layers_kernel(
    padded,
    keys,
    counts,
    which,
    h_ref,
    cot_ref,
    own_vec,
    got_vec,
    own_qkv,
    own_out,
    own_up,
    own_down,
    got_qkv,
    got_out,
    got_up,
    got_down,
    mine_ref,
    away_ref,
    mine_wide,
    away_wide,
    mine_tall,
    away_tall,
    w_qkv,
    w_out,
    w_up,
    w_down,
    vecs,
    hidden,
    normed,
    queries,
    kv,
    weights,
    attended,
    middle,
    second,
    active,
    slope,
    before,
    grad_out,
    grad_low,
    out_low,
    grad_heads,
    grad_before,
    grad_joined,
    grad_norm,
    scores,
    grad_scores,
    sum_up,
    sum_down,
    sum_att,
    vec_one,
    vec_up,
    vec_qkv,
    wide,
    tall,
    load_sem,
    store_sem,
):
    step = pl.program_id(0)
    last = pl.num_programs(0) - 1
    core = which[0]
    count = counts[core]
    running = step * GROUP < count
    tokens, features = h_ref.shape[2:]
    heads = features // HEAD
    rows = GROUP * padded
    units = w_up.shape[2]
    couple = 2 * HEAD
    own = (own_qkv, own_out, own_up, own_down)
    got = (got_qkv, got_out, got_up, got_down)
    held = (w_qkv, w_out, w_up, w_down)
    at_g1, at_b1, at_qkv = 0, features, 2 * features
    at_bo, at_g2, at_b2, at_bd, at_up = (n * features for n in (5, 6, 7, 8, 9))

    def vec(layer, at, size=features):
        return vecs[pl.ds(layer, 1), at : at + size]

    def load(source, n, layer):
        return pltpu.make_async_copy(source[n].at[0], held[n].at[layer], load_sem.at[layer, n])

    @pl.when(step == 0)
    def _():
        for layer in range(2):
            for n in range(4):

                @pl.when(core == layer)
                def _():
                    load(own, n, layer).start()

                @pl.when(core != layer)
                def _():
                    load(got, n, layer).start()

        for layer in range(2):
            mine = jnp.full(own_vec.shape, core == layer)
            vecs[layer : layer + 1] = jnp.where(mine, own_vec[...], got_vec[...])
        for ref in (sum_up, sum_down, sum_att, vec_one, vec_up, vec_qkv):
            for layer in range(2):
                ref[layer] = jnp.zeros(ref.shape[1:], F32)
        for layer in range(2):
            for j in range(GROUP):
                kv[layer, j * keys + padded : (j + 1) * keys] = jnp.zeros(
                    (keys - padded, 2 * features), BF16
                )

    def leave(layer, kind, j, value):
        @pl.when(core == layer)
        def _():
            mine_ref[kind, j] = value

        @pl.when(core != layer)
        def _():
            away_ref[kind, j] = value

    lane = lax.broadcasted_iota(jnp.int32, (padded, couple), 1)
    left = lane < HEAD
    image = [slice(j * padded, (j + 1) * padded) for j in range(GROUP)]
    images_keys = [slice(j * keys, (j + 1) * keys) for j in range(GROUP)]
    pairs = [slice(n * couple, (n + 1) * couple) for n in range(heads // 2)]
    tasks = [(j, n) for j in range(GROUP) for n in range(heads // 2)]
    chunks = spans(units, 512)

    def stacked(value):
        nothing = jnp.zeros_like(value)
        return jnp.where(left, value, nothing), jnp.where(left, nothing, value)

    def key_of(layer, j, n):
        return kv[layer, images_keys[j], pairs[n]]

    def value_of(layer, j, n):
        at = features + n * couple
        return kv[layer, images_keys[j], at : at + couple]

    def unstacked(value):
        return jnp.where(left, value[:padded], value[padded:])

    def forward(layer):
        @pl.when(step == 0)
        def _():
            for n in range(4):
                load(own, n, layer).wait()

        for at, size in row_chunks(rows):
            hat, _ = normalized(hidden[layer, at : at + size])
            value = hat * vec(layer, at_g1) + vec(layer, at_b1)
            normed[layer, at : at + size] = value.astype(BF16)
        value = dot(normed[layer], w_qkv[layer, :, :features]) + vec(layer, at_qkv)
        value = value.astype(BF16) * jnp.asarray(HEAD**-0.5, BF16)
        for j, n in tasks:
            for half, part in enumerate(stacked(value[image[j], pairs[n]])):
                queries[layer, j, n, half * padded : (half + 1) * padded] = part
        for columns in spans(2 * features, 512):
            at, size = features + columns.start, columns.stop - columns.start
            value = dot(normed[layer], w_qkv[layer, :, at : at + size])
            value = (value + vec(layer, at_qkv + at, size)).astype(BF16)
            for j in range(GROUP):
                kv[layer, j * keys : j * keys + padded, columns] = value[image[j]]

        def score(u):
            j, n = tasks[u]
            scores[u % 2] = dot_nt(queries[layer, j, n], key_of(layer, j, n))

        def soften(u):
            j, n = tasks[u]
            for at, size in row_chunks(2 * padded):
                real = lax.broadcasted_iota(jnp.int32, (size, keys), 1) < tokens
                s = jnp.where(real, scores[u % 2, at : at + size], -1e30)
                e = jnp.exp(s - jnp.max(s, axis=-1, keepdims=True))
                p = e * reciprocal(jnp.sum(e, axis=-1, keepdims=True))
                weights[layer, j, n, at : at + size] = p.astype(BF16)

        def attend(u):
            j, n = tasks[u]
            value = unstacked(dot(weights[layer, j, n], value_of(layer, j, n)))
            attended[layer, image[j], pairs[n]] = value.astype(BF16)

        def project(j):
            middle[layer, image[j]] = dot(attended[layer, image[j]], w_out[layer])

        def norm_two(j):
            for at, size in row_chunks(padded):
                at = j * padded + at
                value = middle[layer, at : at + size] + hidden[layer, at : at + size]
                value = value + vec(layer, at_bo)
                middle[layer, at : at + size] = value
                hat, _ = normalized(value)
                value = hat * vec(layer, at_g2) + vec(layer, at_b2)
                second[layer, at : at + size] = value.astype(BF16)

        score(0)
        for u in range(len(tasks)):
            if u + 1 < len(tasks):
                score(u + 1)
            if u:
                attend(u - 1)
                if tasks[u - 1][1] == heads // 2 - 1:
                    project(tasks[u - 1][0])
            soften(u)
            if u and tasks[u - 1][1] == heads // 2 - 1:
                norm_two(tasks[u - 1][0])
        attend(len(tasks) - 1)
        project(GROUP - 1)
        norm_two(GROUP - 1)

        def up(c):
            before[:, chunks[c]] = dot(second[layer], w_up[layer, :, chunks[c]])

        def curve(c):
            columns = chunks[c]
            for at, size in row_chunks(rows, 16):
                value, change = gelu_and_slope(
                    before[at : at + size, columns]
                    + vec(layer, at_up + columns.start, columns.stop - columns.start)
                )
                active[layer, at : at + size, columns] = value.astype(BF16)
                slope[layer, at : at + size, columns] = change.astype(BF16)

        def down(c):
            value = dot(active[layer, :, chunks[c]], w_down[layer, chunks[c]])
            if c:
                value = value + grad_norm[...]
            grad_norm[...] = value

        up(0)
        for c in range(len(chunks)):
            if c + 1 < len(chunks):
                up(c + 1)
            if c:
                down(c - 1)
            curve(c)
        down(len(chunks) - 1)
        for j in range(GROUP):
            keep = jnp.where(step * GROUP + j < count, 1.0, 0.0)
            result = grad_norm[image[j]] + middle[layer, image[j]]
            result = ((result + vec(layer, at_bd)) * keep).astype(BF16)
            leave(layer, 0, j, result[:tokens])
            hidden[layer + 1, image[j]] = result.astype(F32)

    def backward(layer):
        for at, size in row_chunks(rows):
            value = grad_out[at : at + size]
            grad_low[at : at + size] = value.astype(BF16)
            vec_one[layer, 0:8] += fold(value)

        def activation(c):
            before[:, chunks[c]] = dot_nt(grad_low[...], w_down[layer, chunks[c]])

        def multiply(c):
            columns = chunks[c]
            total = jnp.zeros((8, columns.stop - columns.start), F32)
            for at, size in row_chunks(rows, 16):
                lines = slice(at, at + size)
                piece = before[lines, columns] * slope[layer, lines, columns].astype(F32)
                piece = piece.astype(BF16)
                grad_before[lines, columns] = piece
                total = total + fold(piece.astype(F32))
            vec_up[layer, :, columns] += total

        activation(0)
        for c in range(len(chunks)):
            if c + 1 < len(chunks):
                activation(c + 1)
            sum_down[layer, :, chunks[c]] += dot_tn(grad_low[...], active[layer, :, chunks[c]])
            multiply(c)

        def norm_two(j):
            one, two, three = (jnp.zeros((8, features), F32) for _ in range(3))
            for at, size in row_chunks(padded):
                lines = slice(j * padded + at, j * padded + at + size)
                grad = grad_norm[lines]
                dx, by_hat = norm_backward(middle[layer, lines], grad, vec(layer, at_g2))
                one = one + fold(by_hat)
                two = two + fold(grad)
                value = grad_out[lines] + dx
                grad_out[lines] = value
                value = value.astype(BF16)
                out_low[lines] = value
                three = three + fold(value.astype(F32))
            vec_one[layer, 8:16] += one
            vec_one[layer, 16:24] += two
            vec_one[layer, 24:32] += three

        for j in range(GROUP):
            grad_norm[image[j]] = dot_nt(grad_before[image[j]], w_up[layer])
        for c in range(len(chunks)):
            sum_up[layer, :, chunks[c]] += dot_tn(second[layer], grad_before[:, chunks[c]])
            if c < GROUP:
                norm_two(c)
        for j in range(GROUP):
            value = dot_nt(out_low[image[j]], w_out[layer]).astype(BF16)
            for n in range(heads // 2):
                for half, part in enumerate(stacked(value[:, pairs[n]])):
                    grad_heads[j, n, half * padded : (half + 1) * padded] = part

        def grad_weights(u):
            j, n = tasks[u]
            scores[u % 2] = dot_nt(grad_heads[j, n], value_of(layer, j, n))

        def soften_back(u):
            j, n = tasks[u]
            for at, size in row_chunks(2 * padded):
                p = weights[layer, j, n, at : at + size].astype(F32)
                by = p * scores[u % 2, at : at + size]
                by = by - p * jnp.sum(by, axis=-1, keepdims=True)
                grad_scores[u % 2, at : at + size] = by.astype(BF16)

        def into(layer, j, column, part):
            part = part.astype(BF16)
            grad_joined[image[j], column : column + couple] = part
            vec_qkv[layer, :, column : column + couple] += fold(part.astype(F32))

        def attention_value(u):
            j, n = tasks[u]
            part = dot_tn(weights[layer, j, n], grad_heads[j, n])[:padded]
            into(layer, j, 2 * features + n * couple, part)

        def attention_rest(u):
            j, n = tasks[u]
            part = unstacked(dot(grad_scores[u % 2], key_of(layer, j, n))) * HEAD**-0.5
            into(layer, j, n * couple, part)
            part = dot_tn(grad_scores[u % 2], queries[layer, j, n])[:padded]
            into(layer, j, features + n * couple, part)

        grad_weights(0)
        for u in range(len(tasks)):
            if u + 1 < len(tasks):
                grad_weights(u + 1)
            if u:
                attention_rest(u - 1)
            else:
                sum_att[layer, :, 3 * features :] += dot_tn(attended[layer], out_low[...])
            attention_value(u)
            soften_back(u)
        attention_rest(len(tasks) - 1)

        def norm_one(j):
            one, two = (jnp.zeros((8, features), F32) for _ in range(2))
            for at, size in row_chunks(padded):
                lines = slice(j * padded + at, j * padded + at + size)
                grad = grad_norm[lines]
                dx, by_hat = norm_backward(hidden[layer, lines], grad, vec(layer, at_g1))
                one = one + fold(by_hat)
                two = two + fold(grad)
                value = grad_out[lines] + dx
                grad_out[lines] = value.astype(BF16).astype(F32)
            vec_one[layer, 32:40] += one
            vec_one[layer, 40:48] += two

        for j in range(GROUP):
            grad_norm[image[j]] = dot_nt(grad_joined[image[j]], w_qkv[layer])
        for c, columns in enumerate(spans(3 * features, 512)):
            sum_att[layer, :, columns] += dot_tn(normed[layer], grad_joined[:, columns])
            if c < GROUP:
                norm_one(c)
        for j in range(GROUP):
            leave(layer, 1, j, grad_out[j * padded : j * padded + tokens].astype(BF16))

    def store(layer, kind, target):
        stage = (wide, tall)[kind].at[layer]
        return pltpu.make_async_copy(stage, target, store_sem.at[layer, kind])

    def finish(layer):
        wide[layer, :, :units] = sum_up[layer].astype(BF16)
        wide[layer, :, units : units + 4 * features] = sum_att[layer].astype(BF16)
        line = lax.broadcasted_iota(jnp.int32, (128, features), 0)
        plain = jnp.zeros((128, features), F32)
        for n, group in enumerate((4, 5, 3, 1, 2, 0)):
            total = jnp.sum(vec_one[layer, 8 * group : 8 * group + 8], axis=0, keepdims=True)
            plain = plain + jnp.where(line == n, total, 0.0)
        qkv = jnp.sum(vec_qkv[layer], axis=0, keepdims=True)
        qv = jnp.concatenate([qkv[:, :features], qkv[:, 2 * features :]], axis=1)
        total_up = jnp.sum(vec_up[layer], axis=0, keepdims=True)
        columns = jnp.zeros((features, 128), F32)
        for first_line, total in ((0, plain), (6, qv), (8, total_up)):
            size = total.shape[1]
            each = size // features
            position = lax.broadcasted_iota(jnp.int32, (128, size), 1)
            row = lax.broadcasted_iota(jnp.int32, (128, size), 0)
            if each > 1:
                total = jnp.where(row - first_line == (position & (each - 1)), total, 0.0)
            target = lax.broadcasted_iota(jnp.int32, (features, size), 0)
            source = lax.broadcasted_iota(jnp.int32, (features, size), 1)
            inside = (source >= target * each) & (source < target * each + each)
            pick = jnp.where(inside, 1.0, 0.0).astype(BF16)
            columns = columns + dot_nt(pick, total.astype(BF16))
        wide[layer, :, units + 4 * features :] = columns.astype(BF16)

        def send(kind, mine, away):
            @pl.when(core == layer)
            def _():
                store(layer, kind, mine).start()

            @pl.when(core != layer)
            def _():
                store(layer, kind, away).start()

        send(0, mine_wide, away_wide)
        for columns in spans(units, features):
            tall[layer, columns, :] = sum_down[layer, :, columns].astype(BF16).T
        send(1, mine_tall, away_tall)

    @pl.when(jnp.logical_not(running))
    def _():
        mine_ref[...] = jnp.zeros_like(mine_ref)
        away_ref[...] = jnp.zeros_like(away_ref)

    @pl.when(running)
    def _():
        for j in range(GROUP):
            tail = slice(j * padded + padded - 16, (j + 1) * padded)
            hidden[0, tail] = jnp.zeros((16, features), F32)
            hidden[0, j * padded : j * padded + tokens] = h_ref[0, j].astype(F32)
        lax.fori_loop(0, 2, lambda layer, carry: (forward(layer), carry)[1], 0)
        for j in range(GROUP):
            keep = jnp.where(step * GROUP + j < count, 1.0, 0.0)
            tail = slice(j * padded + padded - 16, (j + 1) * padded)
            grad_out[tail] = jnp.zeros((16, features), F32)
            grad_out[j * padded : j * padded + tokens] = cot_ref[0, j].astype(F32) * keep

    def second_half(at, carry):
        layer = 1 - at

        @pl.when(running)
        def _():
            backward(layer)

        @pl.when(step == last)
        def _():
            finish(layer)

        return carry

    lax.fori_loop(0, 2, second_half, 0)

    @pl.when(step == last)
    def _():
        for layer in range(2):
            for kind, mine in enumerate((mine_wide, mine_tall)):
                store(layer, kind, mine).wait()


def run_layers(counts, which, inputs, cotangent, vectors, weights):
    slots, tokens, features = inputs.shape[1:]
    padded = -(-tokens // 16) * 16
    keys = -(-tokens // 128) * 128
    heads = features // HEAD
    steps = slots // GROUP
    block = GROUP * padded
    units = weights[0][2].shape[2]
    packed = vectors[0].shape[1]
    wide = units + 4 * features + 128
    images = pl.BlockSpec((1, GROUP, tokens, features), lambda i, counts, which: (which[0], i, 0, 0))
    kinds = pl.BlockSpec((2, GROUP, tokens, features), lambda i, counts, which: (0, i, 0, 0))
    vector = pl.BlockSpec((1, packed), lambda i, counts, which: (0, 0))
    anywhere = pl.BlockSpec(memory_space=pl.ANY)
    both = (
        ((features, 3 * features), BF16),
        ((features, features), BF16),
        ((features, units), BF16),
        ((units, features), BF16),
        ((packed,), F32),
    )
    saved = (
        ((block, features), BF16),
        ((GROUP, heads // 2, 2 * padded, 2 * HEAD), BF16),
        ((GROUP * keys, 2 * features), BF16),
        ((GROUP, heads // 2, 2 * padded, keys), BF16),
        ((block, features), BF16),
        ((block, features), F32),
        ((block, features), BF16),
        ((block, units), BF16),
        ((block, units), BF16),
    )
    sums = (
        ((features, units), F32),
        ((features, units), F32),
        ((features, 4 * features), F32),
        ((48, features), F32),
        ((8, units), F32),
        ((8, 3 * features), F32),
        ((features, wide), BF16),
        ((units, features), BF16),
    )

    def two(shapes):
        return [pltpu.VMEM((2,) + shape, kind) for shape, kind in shapes]

    scratch = (
        two(both)
        + [pltpu.VMEM((3, block, features), F32)]
        + two(saved)
        + [
            pltpu.VMEM((block, units), F32),
            pltpu.VMEM((block, features), F32),
            pltpu.VMEM((block, features), BF16),
            pltpu.VMEM((block, features), BF16),
            pltpu.VMEM((GROUP, heads // 2, 2 * padded, 2 * HEAD), BF16),
            pltpu.VMEM((block, units), BF16),
            pltpu.VMEM((block, 3 * features), BF16),
            pltpu.VMEM((block, features), F32),
            pltpu.VMEM((2, 2 * padded, keys), F32),
            pltpu.VMEM((2, 2 * padded, keys), BF16),
        ]
        + two(sums)
        + [pltpu.SemaphoreType.DMA((2, 4)), pltpu.SemaphoreType.DMA((2, 2))]
    )
    return pl.pallas_call(
        lambda *refs: layers_kernel(padded, keys, *refs),
        grid_spec=pltpu.PrefetchScalarGridSpec(
            num_scalar_prefetch=2,
            grid=(steps,),
            in_specs=[images, images, vector, vector] + [anywhere] * 8,
            out_specs=[kinds, kinds] + [anywhere] * 4,
            scratch_shapes=scratch,
        ),
        out_shape=[jax.ShapeDtypeStruct((2, slots, tokens, features), BF16)] * 2
        + [jax.ShapeDtypeStruct((features, wide), BF16)] * 2
        + [jax.ShapeDtypeStruct((units, features), BF16)] * 2,
        compiler_params=pltpu.CompilerParams(
            vmem_limit_bytes=VMEM_LIMIT, dimension_semantics=("arbitrary",)
        ),
        cost_estimate=pl.CostEstimate(
            flops=80_000_000_000, bytes_accessed=30_000_000, transcendentals=0
        ),
    )(counts, which, inputs, cotangent, *vectors, *weights[0], *weights[1])


def pack_vectors(g1, b1, b_qv, *rest):
    features = g1.shape[1]
    arrays = (g1, b1, b_qv) + rest
    total = sum(a.shape[1] for a in arrays) + features

    def body(*refs):
        out = refs[-1]
        at = 0
        for n, ref in enumerate(refs[:-1]):
            if n == 2:
                out[:, at : at + features] = ref[:, :features]
                out[:, at + features : at + 2 * features] = jnp.zeros((1, features), F32)
                out[:, at + 2 * features : at + 3 * features] = ref[:, features:]
                at += 3 * features
            else:
                out[:, at : at + ref.shape[1]] = ref[...]
                at += ref.shape[1]

    return pl.pallas_call(body, out_shape=jax.ShapeDtypeStruct((1, total), F32))(*arrays)


def swap_cores(block):
    return lax.ppermute(block, "segment", [(0, 1), (1, 0)])


def reduce_shards(mine, got, orders, first, after=None):
    dp = lax.axis_size("dp")
    me = lax.axis_index("dp")
    bits = dp.bit_length() - 1
    rest = (mine.shape[0] // dp, mine.shape[1])
    terms = (mine, got)
    held = [list(range(bits)) for _ in orders]
    first_send = None
    for n in range(bits):
        below = [left.index(order[n]) for order, left in zip(orders, held)]
        bit = [(me >> order[n]) & 1 for order in orders]
        for order, left in zip(orders, held):
            left.remove(order[n])

        def slices(terms, at, index):
            taken = []
            for term in terms:
                view = term.reshape((-1, 2, 1 << at) + rest)
                part = lax.dynamic_index_in_dim(view, index, 1, keepdims=False)
                taken.append(part.reshape((-1,) + rest))
            return taken

        def half(terms, other):
            if below[0] == below[1]:
                index = jnp.where(first, bit[0], bit[1])
                taken = slices(terms, below[0], 1 - index if other else index)
            else:
                index = [1 - b if other else b for b in bit]
                sides = zip(slices(terms, below[0], index[0]), slices(terms, below[1], index[1]))
                taken = [jnp.where(first, a, b) for a, b in sides]
            total = sum(part.astype(F32) for part in taken)
            return total.astype(BF16)

        send = half(terms, True)
        if n == 0:
            first_send = send
            if after is not None:
                terms = lax.optimization_barrier(terms + (after,))[:2]
        keep = half(terms, False)
        route = [
            (core * dp + i, core * dp + (i ^ (1 << order[n])))
            for core, order in enumerate(orders)
            for i in range(dp)
        ]
        arrived = lax.ppermute(send, ("segment", "dp"), route)
        terms = (keep, arrived)
    return tuple(t.reshape(rest) for t in terms), first_send


def split_wide(terms, features, units):
    share = terms[0].shape[0]
    plain = 6

    def body(one, two, up, qkv, out, qv, bias_up, *vectors):
        total = one[...].astype(F32) + two[...].astype(F32)
        up[0] = total[:, :units]
        qkv[0] = total[:, units : units + 3 * features]
        out[0] = total[:, units + 3 * features : units + 4 * features]
        columns = total[:, units + 4 * features :]

        def spread(ref, first_column):
            size = ref.shape[1]
            width = size // share
            lane = lax.broadcasted_iota(jnp.int32, (share, size), 1)
            row = lax.broadcasted_iota(jnp.int32, (share, size), 0)
            value = jnp.zeros((share, size), F32)
            for n in range(width):
                column = columns[:, first_column + n : first_column + n + 1]
                value = value + jnp.where(lane == row * width + n, column, 0.0)
            ref[...] = jnp.sum(value, axis=0, keepdims=True)

        for n, ref in enumerate(vectors):
            spread(ref, n)
        spread(qv, plain)
        spread(bias_up, plain + 2)

    shapes = [(1, share, units), (1, share, 3 * features), (1, share, features)]
    shapes += [(1, 2 * share), (1, units // features * share)] + [(1, share)] * plain
    return pl.pallas_call(
        body, out_shape=[jax.ShapeDtypeStruct(shape, F32) for shape in shapes]
    )(*terms)


def on_device(inputs, image_count, cotangent, *params):
    dp = lax.axis_size("dp")
    core = lax.axis_index("segment")
    first = core == 0
    features = inputs.shape[3]
    g1, b1, w_qkv, b_qv, w_out, b_out, g2, b2, w_up, b_up, w_down, b_down = params
    units = w_up.shape[2]
    own_weights = (w_qkv, w_out, w_up, w_down)
    got_weights = tuple(swap_cores(w) for w in own_weights)
    own_vec = pack_vectors(g1, b1, b_qv, b_out, g2, b2, b_down, b_up)
    got_vec = swap_cores(own_vec)
    counts, which = image_count.reshape(-1), core.astype(jnp.int32).reshape(1)
    mine, away, mine_wide, away_wide, mine_tall, away_tall = run_layers(
        counts, which, inputs, cotangent, (own_vec, got_vec), (own_weights, got_weights)
    )
    got_wide = swap_cores(away_wide)
    away_tall, got_wide = lax.optimization_barrier((away_tall, got_wide))
    got_tall = swap_cores(away_tall)
    got = swap_cores(away)
    bits = list(range(dp.bit_length() - 1))
    near, far = bits[:3], bits[3:]
    plain, turned, crossed = near + far, near[2:] + near[:2] + far, near[1:] + far + near[:1]
    tall, tall_sent = reduce_shards(mine_tall, got_tall, (crossed, crossed), first)
    wide, _ = reduce_shards(mine_wide, got_wide, (plain, turned), first, after=tall_sent)
    got, _ = lax.optimization_barrier((got, tall_sent))
    both = jnp.stack([jnp.where(first, mine, got), jnp.where(first, got, mine)], axis=1)
    g_up, g_qkv, g_out, g_bqv, g_bup, *vectors = split_wide(wide, features, units)
    ln1_gain, ln1_bias, g_bo, ln2_gain, ln2_bias, g_bd = vectors
    g_down = (tall[0].astype(F32) + tall[1].astype(F32))[None]
    outs = (ln1_gain, ln1_bias, g_qkv, g_bqv, g_out, g_bo, ln2_gain, ln2_bias, g_up, g_bup)
    return (both[0][None], both[1][None]) + outs + (g_down, g_bd)


def solution(mesh):
    in_specs = (
        P(None, "dp", None, None),
        P(None, "dp"),
        P(None, "dp", None, None),
        P("segment", None),
        P("segment", None),
        P("segment", None, None),
        P("segment", None),
        P("segment", None, None),
        P("segment", None),
        P("segment", None),
        P("segment", None),
        P("segment", None, None),
        P("segment", None),
        P("segment", None, None),
        P("segment", None),
    )
    out_specs = (
        P("segment", None, "dp", None, None),
        P("segment", None, "dp", None, None),
        P("segment", "dp"),
        P("segment", "dp"),
        P("segment", "dp", None),
        P("segment", "dp"),
        P("segment", "dp", None),
        P("segment", "dp"),
        P("segment", "dp"),
        P("segment", "dp"),
        P("segment", "dp", None),
        P("segment", "dp"),
        P("segment", "dp", None),
        P("segment", "dp"),
    )
    return jax.shard_map(
        on_device, mesh=mesh, in_specs=in_specs, out_specs=out_specs, check_vma=False
    )
```

```python
import jax
import jax.numpy as jnp
from jax import lax
from jax.experimental.layout import Layout, with_layout_constraint
from jax.experimental import pallas as pl
from jax.experimental.pallas import tpu as pltpu
from jax.sharding import PartitionSpec as P

HEAD = 64
EPSILON = 1e-06
BF16 = jnp.bfloat16
F32 = jnp.float32
GROUP = 2
VMEM_LIMIT = 62 * 1024 * 1024


def dot(a, b):
    return lax.dot_general(a, b, (((1,), (0,)), ((), ())), preferred_element_type=F32)


def dot_nt(a, b):
    return lax.dot_general(a, b, (((1,), (1,)), ((), ())), preferred_element_type=F32)


def dot_tn(a, b):
    return lax.dot_general(a, b, (((0,), (0,)), ((), ())), preferred_element_type=F32)


def normalized(rows):
    centered = rows - jnp.mean(rows, axis=-1, keepdims=True)
    spread = jnp.mean(centered * centered, axis=-1, keepdims=True)
    inverse = lax.rsqrt(spread + EPSILON)
    return centered * inverse, inverse


def norm_backward(rows, grad, gain):
    hat, inverse = normalized(rows)
    scaled = grad * gain
    inner = jnp.mean(scaled * hat, axis=-1, keepdims=True)
    dx = inverse * (scaled - jnp.mean(scaled, axis=-1, keepdims=True) - hat * inner)
    return dx, grad * hat


def reciprocal(x):
    guess = pl.reciprocal(x, approx=True)
    return guess * (2.0 - x * guess)


def gelu_and_slope(x):
    bell = jnp.exp(x * x * -0.5)
    t = reciprocal(1.0 + jnp.abs(x) * (0.3275911 * 0.7071067811865476))
    poly = t * (
        0.5 * 0.254829592
        + t
        * (
            0.5 * -0.284496736
            + t * (0.5 * 1.421413741 + t * (0.5 * -1.453152027 + t * (0.5 * 1.061405429)))
        )
    )
    tail = poly * bell
    cdf = jnp.where(x >= 0.0, 1.0 - tail, tail)
    return x * cdf, cdf + x * (bell * 0.3989422804014327)


def fold(rows):
    total = rows[0:8]
    for at in range(8, rows.shape[0], 8):
        total = total + rows[at : at + 8]
    return total


def row_chunks(total, size=64):
    return [(at, min(size, total - at)) for at in range(0, total, size)]


def spans(total, width):
    return [slice(at, min(at + width, total)) for at in range(0, total, width)]


def layers_kernel(
    padded,
    keys,
    counts,
    which,
    h_ref,
    cot_ref,
    own_vec,
    got_vec,
    own_qkv,
    own_out,
    own_up,
    own_down,
    got_qkv,
    got_out,
    got_up,
    got_down,
    mine_ref,
    away_ref,
    mine_wide,
    away_wide,
    mine_tall,
    away_tall,
    w_qkv,
    w_out,
    w_up,
    w_down,
    vecs,
    hidden,
    normed,
    queries,
    kv,
    weights,
    attended,
    middle,
    second,
    active,
    slope,
    before,
    grad_out,
    grad_low,
    out_low,
    grad_heads,
    grad_before,
    grad_joined,
    grad_norm,
    scores,
    grad_scores,
    sum_up,
    sum_down,
    sum_att,
    vec_one,
    vec_up,
    vec_qkv,
    wide,
    tall,
    load_sem,
    store_sem,
):
    step = pl.program_id(0)
    last = pl.num_programs(0) - 1
    core = which[0]
    count = counts[core]
    running = step * GROUP < count
    tokens, features = h_ref.shape[2:]
    heads = features // HEAD
    rows = GROUP * padded
    units = w_up.shape[2]
    couple = 2 * HEAD
    own = (own_qkv, own_out, own_up, own_down)
    got = (got_qkv, got_out, got_up, got_down)
    held = (w_qkv, w_out, w_up, w_down)
    at_g1, at_b1, at_qkv = 0, features, 2 * features
    at_bo, at_g2, at_b2, at_bd, at_up = (n * features for n in (5, 6, 7, 8, 9))

    def vec(layer, at, size=features):
        return vecs[pl.ds(layer, 1), at : at + size]

    def load(source, n, layer):
        return pltpu.make_async_copy(source[n].at[0], held[n].at[layer], load_sem.at[layer, n])

    def fetch(layer):
        for n in range(4):

            @pl.when(core == layer)
            def _():
                load(own, n, layer).start()

            @pl.when(core != layer)
            def _():
                load(got, n, layer).start()

    @pl.when(step == 0)
    def _():
        fetch(0)
        for layer in range(2):
            mine = jnp.full(own_vec.shape, core == layer)
            vecs[layer : layer + 1] = jnp.where(mine, own_vec[...], got_vec[...])
        for ref in (sum_up, sum_down, sum_att, vec_one, vec_up, vec_qkv):
            for layer in range(2):
                ref[layer] = jnp.zeros(ref.shape[1:], F32)
        for layer in range(2):
            for j in range(GROUP):
                kv[layer, j * keys + padded : (j + 1) * keys] = jnp.zeros(
                    (keys - padded, 2 * features), BF16
                )

    def leave(layer, kind, j, value):
        @pl.when(core == layer)
        def _():
            mine_ref[kind, j] = value

        @pl.when(core != layer)
        def _():
            away_ref[kind, j] = value

    lane = lax.broadcasted_iota(jnp.int32, (padded, couple), 1)
    left = lane < HEAD
    image = [slice(j * padded, (j + 1) * padded) for j in range(GROUP)]
    images_keys = [slice(j * keys, (j + 1) * keys) for j in range(GROUP)]
    pairs = [slice(n * couple, (n + 1) * couple) for n in range(heads // 2)]
    tasks = [(j, n) for j in range(GROUP) for n in range(heads // 2)]
    chunks = spans(units, 512)

    def stacked(value):
        nothing = jnp.zeros_like(value)
        return jnp.where(left, value, nothing), jnp.where(left, nothing, value)

    def key_of(layer, j, n):
        return kv[layer, images_keys[j], pairs[n]]

    def value_of(layer, j, n):
        at = features + n * couple
        return kv[layer, images_keys[j], at : at + couple]

    def unstacked(value):
        return jnp.where(left, value[:padded], value[padded:])

    def forward(layer):
        @pl.when(step == 0)
        def _():
            for n in range(4):
                load(own, n, layer).wait()

            @pl.when(layer == 0)
            def _():
                fetch(1)

        for at, size in row_chunks(rows):
            hat, _ = normalized(hidden[layer, at : at + size])
            value = hat * vec(layer, at_g1) + vec(layer, at_b1)
            normed[layer, at : at + size] = value.astype(BF16)
        value = dot(normed[layer], w_qkv[layer, :, :features]) + vec(layer, at_qkv)
        value = value.astype(BF16) * jnp.asarray(HEAD**-0.5, BF16)
        for j, n in tasks:
            for half, part in enumerate(stacked(value[image[j], pairs[n]])):
                queries[layer, j, n, half * padded : (half + 1) * padded] = part
        for columns in spans(2 * features, 512):
            at, size = features + columns.start, columns.stop - columns.start
            value = dot(normed[layer], w_qkv[layer, :, at : at + size])
            value = (value + vec(layer, at_qkv + at, size)).astype(BF16)
            for j in range(GROUP):
                kv[layer, j * keys : j * keys + padded, columns] = value[image[j]]

        def score(u):
            j, n = tasks[u]
            scores[u % 2] = dot_nt(queries[layer, j, n], key_of(layer, j, n))

        def soften(u):
            j, n = tasks[u]
            for at, size in row_chunks(2 * padded):
                real = lax.broadcasted_iota(jnp.int32, (size, keys), 1) < tokens
                s = jnp.where(real, scores[u % 2, at : at + size], -1e30)
                e = jnp.exp(s - jnp.max(s, axis=-1, keepdims=True))
                p = e * reciprocal(jnp.sum(e, axis=-1, keepdims=True))
                weights[layer, j, n, at : at + size] = p.astype(BF16)

        def attend(u):
            j, n = tasks[u]
            value = unstacked(dot(weights[layer, j, n], value_of(layer, j, n)))
            attended[layer, image[j], pairs[n]] = value.astype(BF16)

        def project(j):
            middle[layer, image[j]] = dot(attended[layer, image[j]], w_out[layer])

        def norm_two(j):
            for at, size in row_chunks(padded):
                at = j * padded + at
                value = middle[layer, at : at + size] + hidden[layer, at : at + size]
                value = value + vec(layer, at_bo)
                middle[layer, at : at + size] = value
                hat, _ = normalized(value)
                value = hat * vec(layer, at_g2) + vec(layer, at_b2)
                second[layer, at : at + size] = value.astype(BF16)

        score(0)
        for u in range(len(tasks)):
            if u + 1 < len(tasks):
                score(u + 1)
            if u:
                attend(u - 1)
                if tasks[u - 1][1] == heads // 2 - 1:
                    project(tasks[u - 1][0])
            soften(u)
            if u and tasks[u - 1][1] == heads // 2 - 1:
                norm_two(tasks[u - 1][0])
        attend(len(tasks) - 1)
        project(GROUP - 1)
        norm_two(GROUP - 1)

        def up(c):
            before[:, chunks[c]] = dot(second[layer], w_up[layer, :, chunks[c]])

        def curve(c):
            columns = chunks[c]
            for at, size in row_chunks(rows, 16):
                value, change = gelu_and_slope(
                    before[at : at + size, columns]
                    + vec(layer, at_up + columns.start, columns.stop - columns.start)
                )
                active[layer, at : at + size, columns] = value.astype(BF16)
                slope[layer, at : at + size, columns] = change.astype(BF16)

        def down(c):
            value = dot(active[layer, :, chunks[c]], w_down[layer, chunks[c]])
            if c:
                value = value + grad_norm[...]
            grad_norm[...] = value

        up(0)
        for c in range(len(chunks)):
            if c + 1 < len(chunks):
                up(c + 1)
            if c:
                down(c - 1)
            curve(c)
        down(len(chunks) - 1)
        for j in range(GROUP):
            keep = jnp.where(step * GROUP + j < count, 1.0, 0.0)
            result = grad_norm[image[j]] + middle[layer, image[j]]
            result = ((result + vec(layer, at_bd)) * keep).astype(BF16)
            leave(layer, 0, j, result[:tokens])
            hidden[layer + 1, image[j]] = result.astype(F32)

    def backward_mlp(layer):
        for at, size in row_chunks(rows):
            value = grad_out[at : at + size]
            grad_low[at : at + size] = value.astype(BF16)
            vec_one[layer, 0:8] += fold(value)

        def activation(c):
            before[:, chunks[c]] = dot_nt(grad_low[...], w_down[layer, chunks[c]])

        def multiply(c):
            columns = chunks[c]
            total = jnp.zeros((8, columns.stop - columns.start), F32)
            for at, size in row_chunks(rows, 16):
                lines = slice(at, at + size)
                piece = before[lines, columns] * slope[layer, lines, columns].astype(F32)
                piece = piece.astype(BF16)
                grad_before[lines, columns] = piece
                total = total + fold(piece.astype(F32))
            vec_up[layer, :, columns] += total

        activation(0)
        for c in range(len(chunks)):
            if c + 1 < len(chunks):
                activation(c + 1)
            sum_down[layer, :, chunks[c]] += dot_tn(grad_low[...], active[layer, :, chunks[c]])
            multiply(c)

        def norm_two(j):
            one, two, three = (jnp.zeros((8, features), F32) for _ in range(3))
            for at, size in row_chunks(padded):
                lines = slice(j * padded + at, j * padded + at + size)
                grad = grad_norm[lines]
                dx, by_hat = norm_backward(middle[layer, lines], grad, vec(layer, at_g2))
                one = one + fold(by_hat)
                two = two + fold(grad)
                value = grad_out[lines] + dx
                grad_out[lines] = value
                value = value.astype(BF16)
                out_low[lines] = value
                three = three + fold(value.astype(F32))
            vec_one[layer, 8:16] += one
            vec_one[layer, 16:24] += two
            vec_one[layer, 24:32] += three

        for j in range(GROUP):
            grad_norm[image[j]] = dot_nt(grad_before[image[j]], w_up[layer])
        for c in range(len(chunks)):
            sum_up[layer, :, chunks[c]] += dot_tn(second[layer], grad_before[:, chunks[c]])
            if c < GROUP:
                norm_two(c)
    def backward_attention(layer):
        for j in range(GROUP):
            value = dot_nt(out_low[image[j]], w_out[layer]).astype(BF16)
            for n in range(heads // 2):
                for half, part in enumerate(stacked(value[:, pairs[n]])):
                    grad_heads[j, n, half * padded : (half + 1) * padded] = part

        def grad_weights(u):
            j, n = tasks[u]
            scores[u % 2] = dot_nt(grad_heads[j, n], value_of(layer, j, n))

        def soften_back(u):
            j, n = tasks[u]
            for at, size in row_chunks(2 * padded):
                p = weights[layer, j, n, at : at + size].astype(F32)
                by = p * scores[u % 2, at : at + size]
                by = by - p * jnp.sum(by, axis=-1, keepdims=True)
                grad_scores[u % 2, at : at + size] = by.astype(BF16)

        def into(layer, j, column, part):
            part = part.astype(BF16)
            grad_joined[image[j], column : column + couple] = part
            vec_qkv[layer, :, column : column + couple] += fold(part.astype(F32))

        def attention_value(u):
            j, n = tasks[u]
            part = dot_tn(weights[layer, j, n], grad_heads[j, n])[:padded]
            into(layer, j, 2 * features + n * couple, part)

        def attention_rest(u):
            j, n = tasks[u]
            part = unstacked(dot(grad_scores[u % 2], key_of(layer, j, n))) * HEAD**-0.5
            into(layer, j, n * couple, part)
            part = dot_tn(grad_scores[u % 2], queries[layer, j, n])[:padded]
            into(layer, j, features + n * couple, part)

        grad_weights(0)
        for u in range(len(tasks)):
            if u + 1 < len(tasks):
                grad_weights(u + 1)
            if u:
                attention_rest(u - 1)
            else:
                sum_att[layer, :, 3 * features :] += dot_tn(attended[layer], out_low[...])
            attention_value(u)
            soften_back(u)
        attention_rest(len(tasks) - 1)

        def norm_one(j):
            one, two = (jnp.zeros((8, features), F32) for _ in range(2))
            for at, size in row_chunks(padded):
                lines = slice(j * padded + at, j * padded + at + size)
                grad = grad_norm[lines]
                dx, by_hat = norm_backward(hidden[layer, lines], grad, vec(layer, at_g1))
                one = one + fold(by_hat)
                two = two + fold(grad)
                value = grad_out[lines] + dx
                grad_out[lines] = value.astype(BF16).astype(F32)
            vec_one[layer, 32:40] += one
            vec_one[layer, 40:48] += two

        for j in range(GROUP):
            grad_norm[image[j]] = dot_nt(grad_joined[image[j]], w_qkv[layer])
        for c, columns in enumerate(spans(3 * features, 512)):
            sum_att[layer, :, columns] += dot_tn(normed[layer], grad_joined[:, columns])
            if c < GROUP:
                norm_one(c)
        for j in range(GROUP):
            leave(layer, 1, j, grad_out[j * padded : j * padded + tokens].astype(BF16))

    left_columns, right_columns = pl.ds(0, units), pl.ds(units, 4 * features + 128)
    parts = (
        (wide, mine_wide, away_wide, left_columns),
        (tall, mine_tall, away_tall, pl.ds(0, features)),
        (wide, mine_wide, away_wide, right_columns),
    )

    def store(layer, kind, away=False):
        stage, mine, other, columns = parts[kind]
        target = (other if away else mine).at[:, columns]
        return pltpu.make_async_copy(
            stage.at[layer, :, columns], target, store_sem.at[layer, kind]
        )

    def send(layer, kind):
        @pl.when(core == layer)
        def _():
            store(layer, kind).start()

        @pl.when(core != layer)
        def _():
            store(layer, kind, away=True).start()

    def finish_mlp(layer):
        wide[layer, :, :units] = sum_up[layer].astype(BF16)
        send(layer, 0)
        for columns in spans(units, features):
            tall[layer, columns, :] = sum_down[layer, :, columns].astype(BF16).T
        send(layer, 1)

    def finish_attention(layer):
        wide[layer, :, units : units + 4 * features] = sum_att[layer].astype(BF16)
        line = lax.broadcasted_iota(jnp.int32, (128, features), 0)
        plain = jnp.zeros((128, features), F32)
        for n, group in enumerate((4, 5, 3, 1, 2, 0)):
            total = jnp.sum(vec_one[layer, 8 * group : 8 * group + 8], axis=0, keepdims=True)
            plain = plain + jnp.where(line == n, total, 0.0)
        qkv = jnp.sum(vec_qkv[layer], axis=0, keepdims=True)
        qv = jnp.concatenate([qkv[:, :features], qkv[:, 2 * features :]], axis=1)
        total_up = jnp.sum(vec_up[layer], axis=0, keepdims=True)
        columns = jnp.zeros((features, 128), F32)
        for first_line, total in ((0, plain), (6, qv), (8, total_up)):
            size = total.shape[1]
            each = size // features
            position = lax.broadcasted_iota(jnp.int32, (128, size), 1)
            row = lax.broadcasted_iota(jnp.int32, (128, size), 0)
            if each > 1:
                total = jnp.where(row - first_line == (position & (each - 1)), total, 0.0)
            target = lax.broadcasted_iota(jnp.int32, (features, size), 0)
            source = lax.broadcasted_iota(jnp.int32, (features, size), 1)
            inside = (source >= target * each) & (source < target * each + each)
            pick = jnp.where(inside, 1.0, 0.0).astype(BF16)
            columns = columns + dot_nt(pick, total.astype(BF16))
        wide[layer, :, units + 4 * features :] = columns.astype(BF16)

        send(layer, 2)

    @pl.when(jnp.logical_not(running))
    def _():
        mine_ref[...] = jnp.zeros_like(mine_ref)
        away_ref[...] = jnp.zeros_like(away_ref)

    @pl.when(running)
    def _():
        for j in range(GROUP):
            tail = slice(j * padded + padded - 16, (j + 1) * padded)
            hidden[0, tail] = jnp.zeros((16, features), F32)
            hidden[0, j * padded : j * padded + tokens] = h_ref[0, j].astype(F32)
        lax.fori_loop(0, 2, lambda layer, carry: (forward(layer), carry)[1], 0)
        for j in range(GROUP):
            keep = jnp.where(step * GROUP + j < count, 1.0, 0.0)
            tail = slice(j * padded + padded - 16, (j + 1) * padded)
            grad_out[tail] = jnp.zeros((16, features), F32)
            grad_out[j * padded : j * padded + tokens] = cot_ref[0, j].astype(F32) * keep

    def second_half(at, carry):
        layer = 1 - at

        for compute, finish in (
            (backward_mlp, finish_mlp),
            (backward_attention, finish_attention),
        ):

            @pl.when(running)
            def _():
                compute(layer)

            @pl.when(step == last)
            def _():
                finish(layer)

        return carry

    lax.fori_loop(0, 2, second_half, 0)

    @pl.when(step == last)
    def _():
        for layer in range(2):
            for kind in range(3):
                store(layer, kind).wait()


def run_layers(counts, which, inputs, cotangent, vectors, weights):
    slots, tokens, features = inputs.shape[1:]
    padded = -(-tokens // 16) * 16
    keys = -(-tokens // 128) * 128
    heads = features // HEAD
    steps = slots // GROUP
    block = GROUP * padded
    units = weights[0][2].shape[2]
    packed = vectors[0].shape[1]
    wide = units + 4 * features + 128
    images = pl.BlockSpec((1, GROUP, tokens, features), lambda i, counts, which: (which[0], i, 0, 0))
    kinds = pl.BlockSpec((2, GROUP, tokens, features), lambda i, counts, which: (0, i, 0, 0))
    vector = pl.BlockSpec((1, packed), lambda i, counts, which: (0, 0))
    anywhere = pl.BlockSpec(memory_space=pl.ANY)
    both = (
        ((features, 3 * features), BF16),
        ((features, features), BF16),
        ((features, units), BF16),
        ((units, features), BF16),
        ((packed,), F32),
    )
    saved = (
        ((block, features), BF16),
        ((GROUP, heads // 2, 2 * padded, 2 * HEAD), BF16),
        ((GROUP * keys, 2 * features), BF16),
        ((GROUP, heads // 2, 2 * padded, keys), BF16),
        ((block, features), BF16),
        ((block, features), F32),
        ((block, features), BF16),
        ((block, units), BF16),
        ((block, units), BF16),
    )
    sums = (
        ((features, units), F32),
        ((features, units), F32),
        ((features, 4 * features), F32),
        ((48, features), F32),
        ((8, units), F32),
        ((8, 3 * features), F32),
        ((features, wide), BF16),
        ((units, features), BF16),
    )

    def two(shapes):
        return [pltpu.VMEM((2,) + shape, kind) for shape, kind in shapes]

    scratch = (
        two(both)
        + [pltpu.VMEM((3, block, features), F32)]
        + two(saved)
        + [
            pltpu.VMEM((block, units), F32),
            pltpu.VMEM((block, features), F32),
            pltpu.VMEM((block, features), BF16),
            pltpu.VMEM((block, features), BF16),
            pltpu.VMEM((GROUP, heads // 2, 2 * padded, 2 * HEAD), BF16),
            pltpu.VMEM((block, units), BF16),
            pltpu.VMEM((block, 3 * features), BF16),
            pltpu.VMEM((block, features), F32),
            pltpu.VMEM((2, 2 * padded, keys), F32),
            pltpu.VMEM((2, 2 * padded, keys), BF16),
        ]
        + two(sums)
        + [pltpu.SemaphoreType.DMA((2, 4)), pltpu.SemaphoreType.DMA((2, 3))]
    )
    return pl.pallas_call(
        lambda *refs: layers_kernel(padded, keys, *refs),
        grid_spec=pltpu.PrefetchScalarGridSpec(
            num_scalar_prefetch=2,
            grid=(steps,),
            in_specs=[images, images, vector, vector] + [anywhere] * 8,
            out_specs=[kinds, kinds] + [anywhere] * 4,
            scratch_shapes=scratch,
        ),
        out_shape=[jax.ShapeDtypeStruct((2, slots, tokens, features), BF16)] * 2
        + [jax.ShapeDtypeStruct((features, wide), BF16)] * 2
        + [jax.ShapeDtypeStruct((units, features), BF16)] * 2,
        compiler_params=pltpu.CompilerParams(
            vmem_limit_bytes=VMEM_LIMIT, dimension_semantics=("arbitrary",)
        ),
        cost_estimate=pl.CostEstimate(
            flops=80_000_000_000, bytes_accessed=30_000_000, transcendentals=0
        ),
    )(counts, which, inputs, cotangent, *vectors, *weights[0], *weights[1])


def pack_vectors(g1, b1, b_qv, *rest):
    features = g1.shape[1]
    arrays = (g1, b1, b_qv) + rest
    total = sum(a.shape[1] for a in arrays) + features

    def body(*refs):
        out = refs[-1]
        at = 0
        for n, ref in enumerate(refs[:-1]):
            if n == 2:
                out[:, at : at + features] = ref[:, :features]
                out[:, at + features : at + 2 * features] = jnp.zeros((1, features), F32)
                out[:, at + 2 * features : at + 3 * features] = ref[:, features:]
                at += 3 * features
            else:
                out[:, at : at + ref.shape[1]] = ref[...]
                at += ref.shape[1]

    return pl.pallas_call(body, out_shape=jax.ShapeDtypeStruct((1, total), F32))(*arrays)


def swap_cores(block):
    return lax.ppermute(block, "segment", [(0, 1), (1, 0)])


def reduce_shards(mine, got, orders, first, after=None, beside=()):
    dp = lax.axis_size("dp")
    me = lax.axis_index("dp")
    bits = dp.bit_length() - 1
    rest = (mine.shape[0] // dp, mine.shape[1])
    terms = (mine, got)
    held = [list(range(bits)) for _ in orders]
    first_send = None
    for n in range(bits):
        below = [left.index(order[n]) for order, left in zip(orders, held)]
        bit = [(me >> order[n]) & 1 for order in orders]
        for order, left in zip(orders, held):
            left.remove(order[n])

        def slices(terms, at, index):
            taken = []
            for term in terms:
                view = term.reshape((-1, 2, 1 << at) + rest)
                part = lax.dynamic_index_in_dim(view, index, 1, keepdims=False)
                taken.append(part.reshape((-1,) + rest))
            return taken

        def half(terms, other):
            if below[0] == below[1]:
                index = jnp.where(first, bit[0], bit[1])
                taken = slices(terms, below[0], 1 - index if other else index)
            else:
                index = [1 - b if other else b for b in bit]
                sides = zip(slices(terms, below[0], index[0]), slices(terms, below[1], index[1]))
                taken = [jnp.where(first, a, b) for a, b in sides]
            total = sum(part.astype(F32) for part in taken)
            return total.astype(BF16)

        send = half(terms, True)
        if n == 0:
            first_send = send
            if after is not None:
                terms = lax.optimization_barrier(terms + (after,))[:2]
        keep = half(terms, False)
        route = [
            (core * dp + i, core * dp + (i ^ (1 << order[n])))
            for core, order in enumerate(orders)
            for i in range(dp)
        ]
        arrived = lax.ppermute(send, ("segment", "dp"), route)
        if n == 0 and beside:
            arrived, *beside = lax.optimization_barrier((arrived, *beside))
        terms = (keep, arrived)
    return tuple(t.reshape(rest) for t in terms), first_send, beside


def split_wide(terms, features, units):
    share = terms[0].shape[0]
    plain = 6

    def body(one, two, up, qkv, out, qv, bias_up, *vectors):
        total = one[...].astype(F32) + two[...].astype(F32)
        up[0] = total[:, :units]
        qkv[0] = total[:, units : units + 3 * features]
        out[0] = total[:, units + 3 * features : units + 4 * features]
        columns = total[:, units + 4 * features :]

        def spread(ref, first_column):
            size = ref.shape[1]
            width = size // share
            lane = lax.broadcasted_iota(jnp.int32, (share, size), 1)
            row = lax.broadcasted_iota(jnp.int32, (share, size), 0)
            value = jnp.zeros((share, size), F32)
            for n in range(width):
                column = columns[:, first_column + n : first_column + n + 1]
                value = value + jnp.where(lane == row * width + n, column, 0.0)
            ref[...] = jnp.sum(value, axis=0, keepdims=True)

        for n, ref in enumerate(vectors):
            spread(ref, n)
        spread(qv, plain)
        spread(bias_up, plain + 2)

    shapes = [(1, share, units), (1, share, 3 * features), (1, share, features)]
    shapes += [(1, 2 * share), (1, units // features * share)] + [(1, share)] * plain
    return pl.pallas_call(
        body, out_shape=[jax.ShapeDtypeStruct(shape, F32) for shape in shapes]
    )(*terms)


def on_device(inputs, image_count, cotangent, *params):
    dp = lax.axis_size("dp")
    core = lax.axis_index("segment")
    first = core == 0
    features = inputs.shape[3]
    g1, b1, w_qkv, b_qv, w_out, b_out, g2, b2, w_up, b_up, w_down, b_down = params
    units = w_up.shape[2]
    own_weights = (w_qkv, w_out, w_up, w_down)
    got_weights = tuple(swap_cores(w) for w in own_weights)
    own_vec = pack_vectors(g1, b1, b_qv, b_out, g2, b2, b_down, b_up)
    got_vec = swap_cores(own_vec)
    counts, which = image_count.reshape(-1), core.astype(jnp.int32).reshape(1)
    mine, away, mine_wide, away_wide, mine_tall, away_tall = run_layers(
        counts, which, inputs, cotangent, (own_vec, got_vec), (own_weights, got_weights)
    )
    got_wide = swap_cores(away_wide)
    away_tall, got_wide = lax.optimization_barrier((away_tall, got_wide))
    got_tall = swap_cores(away_tall)
    got = swap_cores(away)
    bits = list(range(dp.bit_length() - 1))
    near, far = bits[:3], bits[3:]
    plain, turned, crossed = near + far, near[2:] + near[:2] + far, near[1:] + far + near[:1]
    tall, tall_sent, _ = reduce_shards(mine_tall, got_tall, (crossed, crossed), first)
    got, _ = lax.optimization_barrier((got, tall_sent))
    both = [
        jnp.stack([jnp.where(first, a, b), jnp.where(first, b, a)], axis=2)
        for a, b in zip(mine, got)
    ]
    both = [with_layout_constraint(b, Layout(major_to_minor=(0, 1, 2, 3))) for b in both]
    wide, _, both = reduce_shards(
        mine_wide, got_wide, (plain, turned), first, after=tall_sent, beside=both
    )
    activations, input_grads = (b.transpose(2, 0, 1, 3)[None] for b in both)
    g_up, g_qkv, g_out, g_bqv, g_bup, *vectors = split_wide(wide, features, units)
    ln1_gain, ln1_bias, g_bo, ln2_gain, ln2_bias, g_bd = vectors
    g_down = (tall[0].astype(F32) + tall[1].astype(F32))[None]
    outs = (ln1_gain, ln1_bias, g_qkv, g_bqv, g_out, g_bo, ln2_gain, ln2_bias, g_up, g_bup)
    return (activations, input_grads) + outs + (g_down, g_bd)


def solution(mesh):
    in_specs = (
        P(None, "dp", None, None),
        P(None, "dp"),
        P(None, "dp", None, None),
        P("segment", None),
        P("segment", None),
        P("segment", None, None),
        P("segment", None),
        P("segment", None, None),
        P("segment", None),
        P("segment", None),
        P("segment", None),
        P("segment", None, None),
        P("segment", None),
        P("segment", None, None),
        P("segment", None),
    )
    out_specs = (
        P("segment", None, "dp", None, None),
        P("segment", None, "dp", None, None),
        P("segment", "dp"),
        P("segment", "dp"),
        P("segment", "dp", None),
        P("segment", "dp"),
        P("segment", "dp", None),
        P("segment", "dp"),
        P("segment", "dp"),
        P("segment", "dp"),
        P("segment", "dp", None),
        P("segment", "dp"),
        P("segment", "dp", None),
        P("segment", "dp"),
    )
    return jax.shard_map(
        on_device, mesh=mesh, in_specs=in_specs, out_specs=out_specs, check_vma=False
    )
```

```python
import jax
import jax.numpy as jnp
from jax import lax
from jax.experimental import pallas as pl
from jax.experimental.pallas import tpu as pltpu
from jax.sharding import PartitionSpec as P

HEAD = 64
EPSILON = 1e-06
BF16 = jnp.bfloat16
F32 = jnp.float32
GROUP = 2
VMEM_LIMIT = 62 * 1024 * 1024


def dot(a, b):
    return lax.dot_general(a, b, (((1,), (0,)), ((), ())), preferred_element_type=F32)


def dot_nt(a, b):
    return lax.dot_general(a, b, (((1,), (1,)), ((), ())), preferred_element_type=F32)


def dot_tn(a, b):
    return lax.dot_general(a, b, (((0,), (0,)), ((), ())), preferred_element_type=F32)


def normalized(rows):
    centered = rows - jnp.mean(rows, axis=-1, keepdims=True)
    spread = jnp.mean(centered * centered, axis=-1, keepdims=True)
    inverse = lax.rsqrt(spread + EPSILON)
    return centered * inverse, inverse


def norm_backward(rows, grad, gain):
    hat, inverse = normalized(rows)
    scaled = grad * gain
    inner = jnp.mean(scaled * hat, axis=-1, keepdims=True)
    dx = inverse * (scaled - jnp.mean(scaled, axis=-1, keepdims=True) - hat * inner)
    return dx, grad * hat


def reciprocal(x):
    guess = pl.reciprocal(x, approx=True)
    return guess * (2.0 - x * guess)


def gelu_and_slope(x):
    bell = jnp.exp(x * x * -0.5)
    t = reciprocal(1.0 + jnp.abs(x) * (0.3275911 * 0.7071067811865476))
    poly = t * (
        0.5 * 0.254829592
        + t
        * (
            0.5 * -0.284496736
            + t * (0.5 * 1.421413741 + t * (0.5 * -1.453152027 + t * (0.5 * 1.061405429)))
        )
    )
    tail = poly * bell
    cdf = jnp.where(x >= 0.0, 1.0 - tail, tail)
    return x * cdf, cdf + x * (bell * 0.3989422804014327)


def fold(rows):
    total = rows[0:8]
    for at in range(8, rows.shape[0], 8):
        total = total + rows[at : at + 8]
    return total


def row_chunks(total, size=64):
    return [(at, min(size, total - at)) for at in range(0, total, size)]


def spans(total, width):
    return [slice(at, min(at + width, total)) for at in range(0, total, width)]


def layers_kernel(
    padded,
    keys,
    counts,
    which,
    h_ref,
    cot_ref,
    own_vec,
    got_vec,
    own_qkv,
    own_out,
    own_up,
    own_down,
    got_qkv,
    got_out,
    got_up,
    got_down,
    mine_ref,
    away_ref,
    mine_wide,
    away_wide,
    mine_tall,
    away_tall,
    w_qkv,
    w_out,
    w_up,
    w_down,
    vecs,
    hidden,
    normed,
    queries,
    kv,
    weights,
    attended,
    middle,
    second,
    active,
    slope,
    before,
    grad_out,
    grad_low,
    out_low,
    grad_heads,
    grad_before,
    grad_joined,
    grad_norm,
    scores,
    grad_scores,
    sum_up,
    sum_down,
    sum_att,
    vec_one,
    vec_up,
    vec_qkv,
    wide,
    tall,
    load_sem,
    store_sem,
):
    step = pl.program_id(0)
    last = pl.num_programs(0) - 1
    core = which[0]
    count = counts[core]
    running = step * GROUP < count
    tokens, features = h_ref.shape[2:]
    heads = features // HEAD
    rows = GROUP * padded
    units = w_up.shape[2]
    couple = 2 * HEAD
    own = (own_qkv, own_out, own_up, own_down)
    got = (got_qkv, got_out, got_up, got_down)
    held = (w_qkv, w_out, w_up, w_down)
    at_g1, at_b1, at_qkv = 0, features, 2 * features
    at_bo, at_g2, at_b2, at_bd, at_up = (n * features for n in (5, 6, 7, 8, 9))

    def vec(layer, at, size=features):
        return vecs[pl.ds(layer, 1), at : at + size]

    def load(source, n, layer):
        return pltpu.make_async_copy(source[n].at[0], held[n].at[layer], load_sem.at[layer, n])

    @pl.when(step == 0)
    def _():
        for layer in range(2):
            for n in range(4):

                @pl.when(core == layer)
                def _():
                    load(own, n, layer).start()

                @pl.when(core != layer)
                def _():
                    load(got, n, layer).start()

        for layer in range(2):
            mine = jnp.full(own_vec.shape, core == layer)
            vecs[layer : layer + 1] = jnp.where(mine, own_vec[...], got_vec[...])
        for ref in (sum_up, sum_down, sum_att, vec_one, vec_up, vec_qkv):
            for layer in range(2):
                ref[layer] = jnp.zeros(ref.shape[1:], F32)
        for layer in range(2):
            for j in range(GROUP):
                kv[layer, j * keys + padded : (j + 1) * keys] = jnp.zeros(
                    (keys - padded, 2 * features), BF16
                )

    def leave(layer, kind, j, value):
        @pl.when(core == layer)
        def _():
            mine_ref[kind, j] = value

        @pl.when(core != layer)
        def _():
            away_ref[kind, j] = value

    lane = lax.broadcasted_iota(jnp.int32, (padded, couple), 1)
    left = lane < HEAD
    image = [slice(j * padded, (j + 1) * padded) for j in range(GROUP)]
    images_keys = [slice(j * keys, (j + 1) * keys) for j in range(GROUP)]
    pairs = [slice(n * couple, (n + 1) * couple) for n in range(heads // 2)]
    tasks = [(j, n) for j in range(GROUP) for n in range(heads // 2)]
    chunks = spans(units, 512)

    def stacked(value):
        nothing = jnp.zeros_like(value)
        return jnp.where(left, value, nothing), jnp.where(left, nothing, value)

    def key_of(layer, j, n):
        return kv[layer, images_keys[j], pairs[n]]

    def value_of(layer, j, n):
        at = features + n * couple
        return kv[layer, images_keys[j], at : at + couple]

    def unstacked(value):
        return jnp.where(left, value[:padded], value[padded:])

    def forward(layer):
        @pl.when(step == 0)
        def _():
            for n in range(2):
                load(own, n, layer).wait()

        for at, size in row_chunks(rows):
            hat, _ = normalized(hidden[layer, at : at + size])
            value = hat * vec(layer, at_g1) + vec(layer, at_b1)
            normed[layer, at : at + size] = value.astype(BF16)
        value = dot(normed[layer], w_qkv[layer, :, :features]) + vec(layer, at_qkv)
        value = value.astype(BF16) * jnp.asarray(HEAD**-0.5, BF16)
        for j, n in tasks:
            for half, part in enumerate(stacked(value[image[j], pairs[n]])):
                queries[layer, j, n, half * padded : (half + 1) * padded] = part
        for columns in spans(2 * features, 512):
            at, size = features + columns.start, columns.stop - columns.start
            value = dot(normed[layer], w_qkv[layer, :, at : at + size])
            value = (value + vec(layer, at_qkv + at, size)).astype(BF16)
            for j in range(GROUP):
                kv[layer, j * keys : j * keys + padded, columns] = value[image[j]]

        def score(u):
            j, n = tasks[u]
            scores[u % 2] = dot_nt(queries[layer, j, n], key_of(layer, j, n))

        def soften(u):
            j, n = tasks[u]
            for at, size in row_chunks(2 * padded):
                real = lax.broadcasted_iota(jnp.int32, (size, keys), 1) < tokens
                s = jnp.where(real, scores[u % 2, at : at + size], -1e30)
                e = jnp.exp(s - jnp.max(s, axis=-1, keepdims=True))
                p = e * reciprocal(jnp.sum(e, axis=-1, keepdims=True))
                weights[layer, j, n, at : at + size] = p.astype(BF16)

        def attend(u):
            j, n = tasks[u]
            value = unstacked(dot(weights[layer, j, n], value_of(layer, j, n)))
            attended[layer, image[j], pairs[n]] = value.astype(BF16)

        def project(j):
            middle[layer, image[j]] = dot(attended[layer, image[j]], w_out[layer])

        def norm_two(j):
            for at, size in row_chunks(padded):
                at = j * padded + at
                value = middle[layer, at : at + size] + hidden[layer, at : at + size]
                value = value + vec(layer, at_bo)
                middle[layer, at : at + size] = value
                hat, _ = normalized(value)
                value = hat * vec(layer, at_g2) + vec(layer, at_b2)
                second[layer, at : at + size] = value.astype(BF16)

        score(0)
        for u in range(len(tasks)):
            if u + 1 < len(tasks):
                score(u + 1)
            if u:
                attend(u - 1)
                if tasks[u - 1][1] == heads // 2 - 1:
                    project(tasks[u - 1][0])
            soften(u)
            if u and tasks[u - 1][1] == heads // 2 - 1:
                norm_two(tasks[u - 1][0])
        attend(len(tasks) - 1)
        project(GROUP - 1)
        norm_two(GROUP - 1)

        @pl.when(step == 0)
        def _():
            for n in range(2, 4):
                load(own, n, layer).wait()

        def up(c):
            before[:, chunks[c]] = dot(second[layer], w_up[layer, :, chunks[c]])

        def curve(c):
            columns = chunks[c]
            for at, size in row_chunks(rows, 16):
                value, change = gelu_and_slope(
                    before[at : at + size, columns]
                    + vec(layer, at_up + columns.start, columns.stop - columns.start)
                )
                active[layer, at : at + size, columns] = value.astype(BF16)
                slope[layer, at : at + size, columns] = change.astype(BF16)

        def down(c):
            value = dot(active[layer, :, chunks[c]], w_down[layer, chunks[c]])
            if c:
                value = value + grad_norm[...]
            grad_norm[...] = value

        up(0)
        for c in range(len(chunks)):
            if c + 1 < len(chunks):
                up(c + 1)
            if c:
                down(c - 1)
            curve(c)
        down(len(chunks) - 1)
        for j in range(GROUP):
            keep = jnp.where(step * GROUP + j < count, 1.0, 0.0)
            result = grad_norm[image[j]] + middle[layer, image[j]]
            result = ((result + vec(layer, at_bd)) * keep).astype(BF16)
            leave(layer, 0, j, result[:tokens])
            hidden[layer + 1, image[j]] = result.astype(F32)

    def backward(layer):
        for at, size in row_chunks(rows):
            value = grad_out[at : at + size]
            grad_low[at : at + size] = value.astype(BF16)
            vec_one[layer, 0:8] += fold(value)

        def activation(c):
            before[:, chunks[c]] = dot_nt(grad_low[...], w_down[layer, chunks[c]])

        def multiply(c):
            columns = chunks[c]
            total = jnp.zeros((8, columns.stop - columns.start), F32)
            for at, size in row_chunks(rows, 16):
                lines = slice(at, at + size)
                piece = before[lines, columns] * slope[layer, lines, columns].astype(F32)
                piece = piece.astype(BF16)
                grad_before[lines, columns] = piece
                total = total + fold(piece.astype(F32))
            vec_up[layer, :, columns] += total

        activation(0)
        for c in range(len(chunks)):
            if c + 1 < len(chunks):
                activation(c + 1)
            sum_down[layer, :, chunks[c]] += dot_tn(grad_low[...], active[layer, :, chunks[c]])
            multiply(c)

        def norm_two(j):
            one, two, three = (jnp.zeros((8, features), F32) for _ in range(3))
            for at, size in row_chunks(padded):
                lines = slice(j * padded + at, j * padded + at + size)
                grad = grad_norm[lines]
                dx, by_hat = norm_backward(middle[layer, lines], grad, vec(layer, at_g2))
                one = one + fold(by_hat)
                two = two + fold(grad)
                value = grad_out[lines] + dx
                grad_out[lines] = value
                value = value.astype(BF16)
                out_low[lines] = value
                three = three + fold(value.astype(F32))
            vec_one[layer, 8:16] += one
            vec_one[layer, 16:24] += two
            vec_one[layer, 24:32] += three

        for j in range(GROUP):
            grad_norm[image[j]] = dot_nt(grad_before[image[j]], w_up[layer])
        for c in range(len(chunks)):
            sum_up[layer, :, chunks[c]] += dot_tn(second[layer], grad_before[:, chunks[c]])
            if c < GROUP:
                norm_two(c)
        for j in range(GROUP):
            value = dot_nt(out_low[image[j]], w_out[layer]).astype(BF16)
            for n in range(heads // 2):
                for half, part in enumerate(stacked(value[:, pairs[n]])):
                    grad_heads[j, n, half * padded : (half + 1) * padded] = part

        def grad_weights(u):
            j, n = tasks[u]
            scores[u % 2] = dot_nt(grad_heads[j, n], value_of(layer, j, n))

        def soften_back(u):
            j, n = tasks[u]
            for at, size in row_chunks(2 * padded):
                p = weights[layer, j, n, at : at + size].astype(F32)
                by = p * scores[u % 2, at : at + size]
                by = by - p * jnp.sum(by, axis=-1, keepdims=True)
                grad_scores[u % 2, at : at + size] = by.astype(BF16)

        def into(layer, j, column, part):
            part = part.astype(BF16)
            grad_joined[image[j], column : column + couple] = part
            vec_qkv[layer, :, column : column + couple] += fold(part.astype(F32))

        def attention_value(u):
            j, n = tasks[u]
            part = dot_tn(weights[layer, j, n], grad_heads[j, n])[:padded]
            into(layer, j, 2 * features + n * couple, part)

        def attention_rest(u):
            j, n = tasks[u]
            part = unstacked(dot(grad_scores[u % 2], key_of(layer, j, n))) * HEAD**-0.5
            into(layer, j, n * couple, part)
            part = dot_tn(grad_scores[u % 2], queries[layer, j, n])[:padded]
            into(layer, j, features + n * couple, part)

        grad_weights(0)
        for u in range(len(tasks)):
            if u + 1 < len(tasks):
                grad_weights(u + 1)
            if u:
                attention_rest(u - 1)
            else:
                sum_att[layer, :, 3 * features :] += dot_tn(attended[layer], out_low[...])
            attention_value(u)
            soften_back(u)
        attention_rest(len(tasks) - 1)

        def norm_one(j):
            one, two = (jnp.zeros((8, features), F32) for _ in range(2))
            for at, size in row_chunks(padded):
                lines = slice(j * padded + at, j * padded + at + size)
                grad = grad_norm[lines]
                dx, by_hat = norm_backward(hidden[layer, lines], grad, vec(layer, at_g1))
                one = one + fold(by_hat)
                two = two + fold(grad)
                value = grad_out[lines] + dx
                grad_out[lines] = value.astype(BF16).astype(F32)
            vec_one[layer, 32:40] += one
            vec_one[layer, 40:48] += two

        for j in range(GROUP):
            grad_norm[image[j]] = dot_nt(grad_joined[image[j]], w_qkv[layer])
        for c, columns in enumerate(spans(3 * features, 512)):
            sum_att[layer, :, columns] += dot_tn(normed[layer], grad_joined[:, columns])
            if c < GROUP:
                norm_one(c)
        for j in range(GROUP):
            leave(layer, 1, j, grad_out[j * padded : j * padded + tokens].astype(BF16))

    def store(layer, kind, target):
        stage = (wide, tall)[kind].at[layer]
        return pltpu.make_async_copy(stage, target, store_sem.at[layer, kind])

    def finish(layer):
        wide[layer, :, :units] = sum_up[layer].astype(BF16)
        wide[layer, :, units : units + 4 * features] = sum_att[layer].astype(BF16)
        line = lax.broadcasted_iota(jnp.int32, (128, features), 0)
        plain = jnp.zeros((128, features), F32)
        for n, group in enumerate((4, 5, 3, 1, 2, 0)):
            total = jnp.sum(vec_one[layer, 8 * group : 8 * group + 8], axis=0, keepdims=True)
            plain = plain + jnp.where(line == n, total, 0.0)
        qkv = jnp.sum(vec_qkv[layer], axis=0, keepdims=True)
        qv = jnp.concatenate([qkv[:, :features], qkv[:, 2 * features :]], axis=1)
        total_up = jnp.sum(vec_up[layer], axis=0, keepdims=True)
        columns = jnp.zeros((features, 128), F32)
        for first_line, total in ((0, plain), (6, qv), (8, total_up)):
            size = total.shape[1]
            each = size // features
            position = lax.broadcasted_iota(jnp.int32, (128, size), 1)
            row = lax.broadcasted_iota(jnp.int32, (128, size), 0)
            if each > 1:
                total = jnp.where(row - first_line == (position & (each - 1)), total, 0.0)
            target = lax.broadcasted_iota(jnp.int32, (features, size), 0)
            source = lax.broadcasted_iota(jnp.int32, (features, size), 1)
            inside = (source >= target * each) & (source < target * each + each)
            pick = jnp.where(inside, 1.0, 0.0).astype(BF16)
            columns = columns + dot_nt(pick, total.astype(BF16))
        wide[layer, :, units + 4 * features :] = columns.astype(BF16)

        def send(kind, mine, away):
            @pl.when(core == layer)
            def _():
                store(layer, kind, mine).start()

            @pl.when(core != layer)
            def _():
                store(layer, kind, away).start()

        send(0, mine_wide, away_wide)
        for columns in spans(units, features):
            tall[layer, columns, :] = sum_down[layer, :, columns].astype(BF16).T
        send(1, mine_tall, away_tall)

    @pl.when(jnp.logical_not(running))
    def _():
        mine_ref[...] = jnp.zeros_like(mine_ref)
        away_ref[...] = jnp.zeros_like(away_ref)

    @pl.when(running)
    def _():
        for j in range(GROUP):
            tail = slice(j * padded + padded - 16, (j + 1) * padded)
            hidden[0, tail] = jnp.zeros((16, features), F32)
            hidden[0, j * padded : j * padded + tokens] = h_ref[0, j].astype(F32)
        lax.fori_loop(0, 2, lambda layer, carry: (forward(layer), carry)[1], 0)
        for j in range(GROUP):
            keep = jnp.where(step * GROUP + j < count, 1.0, 0.0)
            tail = slice(j * padded + padded - 16, (j + 1) * padded)
            grad_out[tail] = jnp.zeros((16, features), F32)
            grad_out[j * padded : j * padded + tokens] = cot_ref[0, j].astype(F32) * keep

    def second_half(at, carry):
        layer = 1 - at

        @pl.when(running)
        def _():
            backward(layer)

        @pl.when(step == last)
        def _():
            finish(layer)

        return carry

    lax.fori_loop(0, 2, second_half, 0)

    @pl.when(step == last)
    def _():
        for layer in range(2):
            for kind, mine in enumerate((mine_wide, mine_tall)):
                store(layer, kind, mine).wait()


def run_layers(counts, which, inputs, cotangent, vectors, weights):
    slots, tokens, features = inputs.shape[1:]
    padded = -(-tokens // 16) * 16
    keys = -(-tokens // 128) * 128
    heads = features // HEAD
    steps = slots // GROUP
    block = GROUP * padded
    units = weights[0][2].shape[2]
    packed = vectors[0].shape[1]
    wide = units + 4 * features + 128
    images = pl.BlockSpec((1, GROUP, tokens, features), lambda i, counts, which: (which[0], i, 0, 0))
    kinds = pl.BlockSpec((2, GROUP, tokens, features), lambda i, counts, which: (0, i, 0, 0))
    vector = pl.BlockSpec((1, packed), lambda i, counts, which: (0, 0))
    anywhere = pl.BlockSpec(memory_space=pl.ANY)
    both = (
        ((features, 3 * features), BF16),
        ((features, features), BF16),
        ((features, units), BF16),
        ((units, features), BF16),
        ((packed,), F32),
    )
    saved = (
        ((block, features), BF16),
        ((GROUP, heads // 2, 2 * padded, 2 * HEAD), BF16),
        ((GROUP * keys, 2 * features), BF16),
        ((GROUP, heads // 2, 2 * padded, keys), BF16),
        ((block, features), BF16),
        ((block, features), F32),
        ((block, features), BF16),
        ((block, units), BF16),
        ((block, units), BF16),
    )
    sums = (
        ((features, units), F32),
        ((features, units), F32),
        ((features, 4 * features), F32),
        ((48, features), F32),
        ((8, units), F32),
        ((8, 3 * features), F32),
        ((features, wide), BF16),
        ((units, features), BF16),
    )

    def two(shapes):
        return [pltpu.VMEM((2,) + shape, kind) for shape, kind in shapes]

    scratch = (
        two(both)
        + [pltpu.VMEM((3, block, features), F32)]
        + two(saved)
        + [
            pltpu.VMEM((block, units), F32),
            pltpu.VMEM((block, features), F32),
            pltpu.VMEM((block, features), BF16),
            pltpu.VMEM((block, features), BF16),
            pltpu.VMEM((GROUP, heads // 2, 2 * padded, 2 * HEAD), BF16),
            pltpu.VMEM((block, units), BF16),
            pltpu.VMEM((block, 3 * features), BF16),
            pltpu.VMEM((block, features), F32),
            pltpu.VMEM((2, 2 * padded, keys), F32),
            pltpu.VMEM((2, 2 * padded, keys), BF16),
        ]
        + two(sums)
        + [pltpu.SemaphoreType.DMA((2, 4)), pltpu.SemaphoreType.DMA((2, 2))]
    )
    return pl.pallas_call(
        lambda *refs: layers_kernel(padded, keys, *refs),
        grid_spec=pltpu.PrefetchScalarGridSpec(
            num_scalar_prefetch=2,
            grid=(steps,),
            in_specs=[images, images, vector, vector] + [anywhere] * 8,
            out_specs=[kinds, kinds] + [anywhere] * 4,
            scratch_shapes=scratch,
        ),
        out_shape=[jax.ShapeDtypeStruct((2, slots, tokens, features), BF16)] * 2
        + [jax.ShapeDtypeStruct((features, wide), BF16)] * 2
        + [jax.ShapeDtypeStruct((units, features), BF16)] * 2,
        compiler_params=pltpu.CompilerParams(
            vmem_limit_bytes=VMEM_LIMIT, dimension_semantics=("arbitrary",)
        ),
        cost_estimate=pl.CostEstimate(
            flops=80_000_000_000, bytes_accessed=30_000_000, transcendentals=0
        ),
    )(counts, which, inputs, cotangent, *vectors, *weights[0], *weights[1])


def pack_vectors(g1, b1, b_qv, *rest):
    features = g1.shape[1]
    arrays = (g1, b1, b_qv) + rest
    total = sum(a.shape[1] for a in arrays) + features

    def body(*refs):
        out = refs[-1]
        at = 0
        for n, ref in enumerate(refs[:-1]):
            if n == 2:
                out[:, at : at + features] = ref[:, :features]
                out[:, at + features : at + 2 * features] = jnp.zeros((1, features), F32)
                out[:, at + 2 * features : at + 3 * features] = ref[:, features:]
                at += 3 * features
            else:
                out[:, at : at + ref.shape[1]] = ref[...]
                at += ref.shape[1]

    return pl.pallas_call(body, out_shape=jax.ShapeDtypeStruct((1, total), F32))(*arrays)


def swap_cores(block):
    return lax.ppermute(block, "segment", [(0, 1), (1, 0)])


class Shards:
    def __init__(self, mine, got, orders, first):
        self.dp = lax.axis_size("dp")
        self.bits = self.dp.bit_length() - 1
        self.rest = (mine.shape[0] // self.dp, mine.shape[1])
        self.terms = (mine, got)
        self.orders, self.first = orders, first
        self.held = [list(range(self.bits)) for _ in orders]

    def wait_for(self, *others):
        self.terms = lax.optimization_barrier(self.terms + others)[:2]

    def begin(self, n):
        me = lax.axis_index("dp")
        self.below = [left.index(order[n]) for order, left in zip(self.orders, self.held)]
        self.bit = [(me >> order[n]) & 1 for order in self.orders]
        for order, left in zip(self.orders, self.held):
            left.remove(order[n])

    def slices(self, at, index):
        taken = []
        for term in self.terms:
            view = term.reshape((-1, 2, 1 << at) + self.rest)
            part = lax.dynamic_index_in_dim(view, index, 1, keepdims=False)
            taken.append(part.reshape((-1,) + self.rest))
        return taken

    def half(self, other):
        index = [1 - b if other else b for b in self.bit]
        below, first = self.below, self.first
        if below[0] == below[1]:
            taken = self.slices(below[0], jnp.where(first, index[0], index[1]))
        else:
            sides = zip(self.slices(below[0], index[0]), self.slices(below[1], index[1]))
            taken = [jnp.where(first, a, b) for a, b in sides]
        return sum(part.astype(F32) for part in taken).astype(BF16)

    def exchange(self, n, send):
        keep = self.half(False)
        route = [
            (core * self.dp + i, core * self.dp + (i ^ (1 << order[n])))
            for core, order in enumerate(self.orders)
            for i in range(self.dp)
        ]
        self.terms = (keep, lax.ppermute(send, ("segment", "dp"), route))

    def result(self):
        return tuple(t.reshape(self.rest) for t in self.terms)


def split_wide(terms, features, units):
    share = terms[0].shape[0]
    plain = 6

    def body(one, two, up, qkv, out, qv, bias_up, *vectors):
        total = one[...].astype(F32) + two[...].astype(F32)
        up[0] = total[:, :units]
        qkv[0] = total[:, units : units + 3 * features]
        out[0] = total[:, units + 3 * features : units + 4 * features]
        columns = total[:, units + 4 * features :]

        def spread(ref, first_column):
            size = ref.shape[1]
            width = size // share
            lane = lax.broadcasted_iota(jnp.int32, (share, size), 1)
            row = lax.broadcasted_iota(jnp.int32, (share, size), 0)
            value = jnp.zeros((share, size), F32)
            for n in range(width):
                column = columns[:, first_column + n : first_column + n + 1]
                value = value + jnp.where(lane == row * width + n, column, 0.0)
            ref[...] = jnp.sum(value, axis=0, keepdims=True)

        for n, ref in enumerate(vectors):
            spread(ref, n)
        spread(qv, plain)
        spread(bias_up, plain + 2)

    shapes = [(1, share, units), (1, share, 3 * features), (1, share, features)]
    shapes += [(1, 2 * share), (1, units // features * share)] + [(1, share)] * plain
    return pl.pallas_call(
        body, out_shape=[jax.ShapeDtypeStruct(shape, F32) for shape in shapes]
    )(*terms)


def on_device(inputs, image_count, cotangent, *params):
    dp = lax.axis_size("dp")
    core = lax.axis_index("segment")
    first = core == 0
    features = inputs.shape[3]
    g1, b1, w_qkv, b_qv, w_out, b_out, g2, b2, w_up, b_up, w_down, b_down = params
    units = w_up.shape[2]
    own_weights = (w_qkv, w_out, w_up, w_down)
    got_weights = tuple(swap_cores(w) for w in own_weights)
    own_vec = pack_vectors(g1, b1, b_qv, b_out, g2, b2, b_down, b_up)
    got_vec = swap_cores(own_vec)
    counts, which = image_count.reshape(-1), core.astype(jnp.int32).reshape(1)
    mine, away, mine_wide, away_wide, mine_tall, away_tall = run_layers(
        counts, which, inputs, cotangent, (own_vec, got_vec), (own_weights, got_weights)
    )
    got_wide = swap_cores(away_wide)
    away_tall, got_wide = lax.optimization_barrier((away_tall, got_wide))
    got_tall = swap_cores(away_tall)
    bits = list(range(dp.bit_length() - 1))
    near, far = bits[:3], bits[3:]
    plain, turned, crossed = near + far, near[2:] + near[:2] + far, near[1:] + far + near[:1]
    wide = Shards(mine_wide, got_wide, (plain, turned), first)
    tall = Shards(mine_tall, got_tall, (crossed, crossed), first)
    for n in bits:
        wide.begin(n)
        tall.begin(n)
        wide_send = wide.half(True)
        if n in (0, bits[-1]):
            tall.wait_for(wide_send)
        tall_send = tall.half(True)
        if n == 0:
            wide.wait_for(tall_send)
            away, _ = lax.optimization_barrier((away, tall_send))
            got = swap_cores(away)
            both = [
                jnp.stack([jnp.where(first, a, b), jnp.where(first, b, a)])
                for a, b in zip(mine, got)
            ]
        wide.exchange(n, wide_send)
        tall.exchange(n, tall_send)
        if n == 0:
            keep, arrived, *both = lax.optimization_barrier(wide.terms + tuple(both))
            wide.terms = (keep, arrived)
    *both, _ = lax.optimization_barrier((*both, tall_send))
    wide, tall = wide.result(), tall.result()
    g_up, g_qkv, g_out, g_bqv, g_bup, *vectors = split_wide(wide, features, units)
    ln1_gain, ln1_bias, g_bo, ln2_gain, ln2_bias, g_bd = vectors
    g_down = (tall[0].astype(F32) + tall[1].astype(F32))[None]
    outs = (ln1_gain, ln1_bias, g_qkv, g_bqv, g_out, g_bo, ln2_gain, ln2_bias, g_up, g_bup)
    return (both[0][None], both[1][None]) + outs + (g_down, g_bd)


def solution(mesh):
    in_specs = (
        P(None, "dp", None, None),
        P(None, "dp"),
        P(None, "dp", None, None),
        P("segment", None),
        P("segment", None),
        P("segment", None, None),
        P("segment", None),
        P("segment", None, None),
        P("segment", None),
        P("segment", None),
        P("segment", None),
        P("segment", None, None),
        P("segment", None),
        P("segment", None, None),
        P("segment", None),
    )
    out_specs = (
        P("segment", None, "dp", None, None),
        P("segment", None, "dp", None, None),
        P("segment", "dp"),
        P("segment", "dp"),
        P("segment", "dp", None),
        P("segment", "dp"),
        P("segment", "dp", None),
        P("segment", "dp"),
        P("segment", "dp"),
        P("segment", "dp"),
        P("segment", "dp", None),
        P("segment", "dp"),
        P("segment", "dp", None),
        P("segment", "dp"),
    )
    return jax.shard_map(
        on_device, mesh=mesh, in_specs=in_specs, out_specs=out_specs, check_vma=False
    )
```

```python
import jax
import jax.numpy as jnp
from jax import lax
from jax.experimental.layout import Layout, with_layout_constraint
from jax.experimental import pallas as pl
from jax.experimental.pallas import tpu as pltpu
from jax.sharding import PartitionSpec as P

HEAD = 64
EPSILON = 1e-06
BF16 = jnp.bfloat16
F32 = jnp.float32
GROUP = 2
VMEM_LIMIT = 62 * 1024 * 1024


def dot(a, b):
    return lax.dot_general(a, b, (((1,), (0,)), ((), ())), preferred_element_type=F32)


def dot_nt(a, b):
    return lax.dot_general(a, b, (((1,), (1,)), ((), ())), preferred_element_type=F32)


def dot_tn(a, b):
    return lax.dot_general(a, b, (((0,), (0,)), ((), ())), preferred_element_type=F32)


def normalized(rows):
    centered = rows - jnp.mean(rows, axis=-1, keepdims=True)
    spread = jnp.mean(centered * centered, axis=-1, keepdims=True)
    inverse = lax.rsqrt(spread + EPSILON)
    return centered * inverse, inverse


def norm_backward(rows, grad, gain):
    hat, inverse = normalized(rows)
    scaled = grad * gain
    inner = jnp.mean(scaled * hat, axis=-1, keepdims=True)
    dx = inverse * (scaled - jnp.mean(scaled, axis=-1, keepdims=True) - hat * inner)
    return dx, grad * hat


def reciprocal(x):
    guess = pl.reciprocal(x, approx=True)
    return guess * (2.0 - x * guess)


def gelu_and_slope(x):
    bell = jnp.exp(x * x * -0.5)
    t = reciprocal(1.0 + jnp.abs(x) * (0.3275911 * 0.7071067811865476))
    poly = t * (
        0.5 * 0.254829592
        + t
        * (
            0.5 * -0.284496736
            + t * (0.5 * 1.421413741 + t * (0.5 * -1.453152027 + t * (0.5 * 1.061405429)))
        )
    )
    tail = poly * bell
    cdf = jnp.where(x >= 0.0, 1.0 - tail, tail)
    return x * cdf, cdf + x * (bell * 0.3989422804014327)


def fold(rows):
    total = rows[0:8]
    for at in range(8, rows.shape[0], 8):
        total = total + rows[at : at + 8]
    return total


def row_chunks(total, size=64):
    return [(at, min(size, total - at)) for at in range(0, total, size)]


def spans(total, width):
    return [slice(at, min(at + width, total)) for at in range(0, total, width)]


def layers_kernel(
    padded,
    keys,
    counts,
    which,
    h_ref,
    cot_ref,
    own_vec,
    got_vec,
    own_qkv,
    own_out,
    own_up,
    own_down,
    got_qkv,
    got_out,
    got_up,
    got_down,
    mine_ref,
    away_ref,
    mine_wide,
    away_wide,
    mine_tall,
    away_tall,
    w_qkv,
    w_out,
    w_up,
    w_down,
    vecs,
    hidden,
    normed,
    queries,
    kv,
    weights,
    attended,
    middle,
    second,
    active,
    slope,
    before,
    grad_out,
    grad_low,
    out_low,
    grad_heads,
    grad_before,
    grad_joined,
    grad_norm,
    scores,
    grad_scores,
    sum_up,
    sum_down,
    sum_att,
    vec_one,
    vec_up,
    vec_qkv,
    wide,
    tall,
    load_sem,
    store_sem,
    clear_sem,
):
    step = pl.program_id(0)
    last = pl.num_programs(0) - 1
    core = which[0]
    count = counts[core]
    running = step * GROUP < count
    tokens, features = h_ref.shape[2:]
    heads = features // HEAD
    rows = GROUP * padded
    units = w_up.shape[2]
    couple = 2 * HEAD
    own = (own_qkv, own_out, own_up, own_down)
    got = (got_qkv, got_out, got_up, got_down)
    held = (w_qkv, w_out, w_up, w_down)
    at_g1, at_b1, at_qkv = 0, features, 2 * features
    at_bo, at_g2, at_b2, at_bd, at_up = (n * features for n in (5, 6, 7, 8, 9))

    def vec(layer, at, size=features):
        return vecs[pl.ds(layer, 1), at : at + size]

    def load(source, n, layer):
        return pltpu.make_async_copy(source[n].at[0], held[n].at[layer], load_sem.at[layer, n])

    blank = [sum_up.at[1]] + [ref.at[layer] for ref in (sum_down, sum_att) for layer in range(2)]

    def clear(n):
        return pltpu.make_async_copy(sum_up.at[0], blank[n], clear_sem.at[n])

    @pl.when(step == 0)
    def _():
        for layer in range(2):
            for n in range(4):

                @pl.when(core == layer)
                def _():
                    load(own, n, layer).start()

                @pl.when(core != layer)
                def _():
                    load(got, n, layer).start()

        for layer in range(2):
            mine = jnp.full(own_vec.shape, core == layer)
            vecs[layer : layer + 1] = jnp.where(mine, own_vec[...], got_vec[...])
        sum_up[0] = jnp.zeros(sum_up.shape[1:], F32)
        for n in range(len(blank)):
            clear(n).start()
        for ref in (vec_one, vec_up, vec_qkv):
            for layer in range(2):
                ref[layer] = jnp.zeros(ref.shape[1:], F32)
        for layer in range(2):
            for j in range(GROUP):
                kv[layer, j * keys + padded : (j + 1) * keys] = jnp.zeros(
                    (keys - padded, 2 * features), BF16
                )

    def leave(layer, kind, j, value):
        @pl.when(core == layer)
        def _():
            mine_ref[kind, j] = value

        @pl.when(core != layer)
        def _():
            away_ref[kind, j] = value

    lane = lax.broadcasted_iota(jnp.int32, (padded, couple), 1)
    left = lane < HEAD
    image = [slice(j * padded, (j + 1) * padded) for j in range(GROUP)]
    images_keys = [slice(j * keys, (j + 1) * keys) for j in range(GROUP)]
    pairs = [slice(n * couple, (n + 1) * couple) for n in range(heads // 2)]
    tasks = [(j, n) for j in range(GROUP) for n in range(heads // 2)]
    chunks = spans(units, 512)

    def stacked(value):
        nothing = jnp.zeros_like(value)
        return jnp.where(left, value, nothing), jnp.where(left, nothing, value)

    def key_of(layer, j, n):
        return kv[layer, images_keys[j], pairs[n]]

    def value_of(layer, j, n):
        at = features + n * couple
        return kv[layer, images_keys[j], at : at + couple]

    def unstacked(value):
        return jnp.where(left, value[:padded], value[padded:])

    def forward(layer):
        @pl.when(step == 0)
        def _():
            for n in range(2):
                load(own, n, layer).wait()

        for at, size in row_chunks(rows):
            hat, _ = normalized(hidden[layer, at : at + size])
            value = hat * vec(layer, at_g1) + vec(layer, at_b1)
            normed[layer, at : at + size] = value.astype(BF16)
        value = dot(normed[layer], w_qkv[layer, :, :features]) + vec(layer, at_qkv)
        value = value.astype(BF16) * jnp.asarray(HEAD**-0.5, BF16)
        for j, n in tasks:
            for half, part in enumerate(stacked(value[image[j], pairs[n]])):
                queries[layer, j, n, half * padded : (half + 1) * padded] = part
        for columns in spans(2 * features, 512):
            at, size = features + columns.start, columns.stop - columns.start
            value = dot(normed[layer], w_qkv[layer, :, at : at + size])
            value = (value + vec(layer, at_qkv + at, size)).astype(BF16)
            for j in range(GROUP):
                kv[layer, j * keys : j * keys + padded, columns] = value[image[j]]

        def score(u):
            j, n = tasks[u]
            scores[u % 2] = dot_nt(queries[layer, j, n], key_of(layer, j, n))

        def soften(u):
            j, n = tasks[u]
            for at, size in row_chunks(2 * padded):
                real = lax.broadcasted_iota(jnp.int32, (size, keys), 1) < tokens
                s = jnp.where(real, scores[u % 2, at : at + size], -1e30)
                e = jnp.exp(s - jnp.max(s, axis=-1, keepdims=True))
                p = e * reciprocal(jnp.sum(e, axis=-1, keepdims=True))
                weights[layer, j, n, at : at + size] = p.astype(BF16)

        def attend(u):
            j, n = tasks[u]
            value = unstacked(dot(weights[layer, j, n], value_of(layer, j, n)))
            attended[layer, image[j], pairs[n]] = value.astype(BF16)

        def project(j):
            middle[layer, image[j]] = dot(attended[layer, image[j]], w_out[layer])

        def norm_two(j):
            for at, size in row_chunks(padded):
                at = j * padded + at
                value = middle[layer, at : at + size] + hidden[layer, at : at + size]
                value = value + vec(layer, at_bo)
                middle[layer, at : at + size] = value
                hat, _ = normalized(value)
                value = hat * vec(layer, at_g2) + vec(layer, at_b2)
                second[layer, at : at + size] = value.astype(BF16)

        score(0)
        for u in range(len(tasks)):
            if u + 1 < len(tasks):
                score(u + 1)
            if u:
                attend(u - 1)
                if tasks[u - 1][1] == heads // 2 - 1:
                    project(tasks[u - 1][0])
            soften(u)
            if u and tasks[u - 1][1] == heads // 2 - 1:
                norm_two(tasks[u - 1][0])
        attend(len(tasks) - 1)
        project(GROUP - 1)
        norm_two(GROUP - 1)

        @pl.when(step == 0)
        def _():
            for n in range(2, 4):
                load(own, n, layer).wait()

        def up(c):
            before[:, chunks[c]] = dot(second[layer], w_up[layer, :, chunks[c]])

        def curve(c):
            columns = chunks[c]
            for at, size in row_chunks(rows, 16):
                value, change = gelu_and_slope(
                    before[at : at + size, columns]
                    + vec(layer, at_up + columns.start, columns.stop - columns.start)
                )
                active[layer, at : at + size, columns] = value.astype(BF16)
                slope[layer, at : at + size, columns] = change.astype(BF16)

        def down(c):
            value = dot(active[layer, :, chunks[c]], w_down[layer, chunks[c]])
            if c:
                value = value + grad_norm[...]
            grad_norm[...] = value

        up(0)
        for c in range(len(chunks)):
            if c + 1 < len(chunks):
                up(c + 1)
            if c:
                down(c - 1)
            curve(c)
        down(len(chunks) - 1)
        for j in range(GROUP):
            keep = jnp.where(step * GROUP + j < count, 1.0, 0.0)
            result = grad_norm[image[j]] + middle[layer, image[j]]
            result = ((result + vec(layer, at_bd)) * keep).astype(BF16)
            leave(layer, 0, j, result[:tokens])
            hidden[layer + 1, image[j]] = result.astype(F32)

    def backward(layer):
        for at, size in row_chunks(rows):
            value = grad_out[at : at + size]
            grad_low[at : at + size] = value.astype(BF16)
            vec_one[layer, 0:8] += fold(value)

        def activation(c):
            before[:, chunks[c]] = dot_nt(grad_low[...], w_down[layer, chunks[c]])

        def multiply(c):
            columns = chunks[c]
            total = jnp.zeros((8, columns.stop - columns.start), F32)
            for at, size in row_chunks(rows, 16):
                lines = slice(at, at + size)
                piece = before[lines, columns] * slope[layer, lines, columns].astype(F32)
                piece = piece.astype(BF16)
                grad_before[lines, columns] = piece
                total = total + fold(piece.astype(F32))
            vec_up[layer, :, columns] += total

        activation(0)
        for c in range(len(chunks)):
            if c + 1 < len(chunks):
                activation(c + 1)
            sum_down[layer, :, chunks[c]] += dot_tn(grad_low[...], active[layer, :, chunks[c]])
            multiply(c)

        def norm_two(j):
            one, two, three = (jnp.zeros((8, features), F32) for _ in range(3))
            for at, size in row_chunks(padded):
                lines = slice(j * padded + at, j * padded + at + size)
                grad = grad_norm[lines]
                dx, by_hat = norm_backward(middle[layer, lines], grad, vec(layer, at_g2))
                one = one + fold(by_hat)
                two = two + fold(grad)
                value = grad_out[lines] + dx
                grad_out[lines] = value
                value = value.astype(BF16)
                out_low[lines] = value
                three = three + fold(value.astype(F32))
            vec_one[layer, 8:16] += one
            vec_one[layer, 16:24] += two
            vec_one[layer, 24:32] += three

        for j in range(GROUP):
            grad_norm[image[j]] = dot_nt(grad_before[image[j]], w_up[layer])
        for c in range(len(chunks)):
            sum_up[layer, :, chunks[c]] += dot_tn(second[layer], grad_before[:, chunks[c]])
            if c < GROUP:
                norm_two(c)
        for j in range(GROUP):
            value = dot_nt(out_low[image[j]], w_out[layer]).astype(BF16)
            for n in range(heads // 2):
                for half, part in enumerate(stacked(value[:, pairs[n]])):
                    grad_heads[j, n, half * padded : (half + 1) * padded] = part

        def grad_weights(u):
            j, n = tasks[u]
            scores[u % 2] = dot_nt(grad_heads[j, n], value_of(layer, j, n))

        def soften_back(u):
            j, n = tasks[u]
            for at, size in row_chunks(2 * padded):
                p = weights[layer, j, n, at : at + size].astype(F32)
                by = p * scores[u % 2, at : at + size]
                by = by - p * jnp.sum(by, axis=-1, keepdims=True)
                grad_scores[u % 2, at : at + size] = by.astype(BF16)

        def into(layer, j, column, part):
            part = part.astype(BF16)
            grad_joined[image[j], column : column + couple] = part
            vec_qkv[layer, :, column : column + couple] += fold(part.astype(F32))

        def attention_value(u):
            j, n = tasks[u]
            part = dot_tn(weights[layer, j, n], grad_heads[j, n])[:padded]
            into(layer, j, 2 * features + n * couple, part)

        def attention_rest(u):
            j, n = tasks[u]
            part = unstacked(dot(grad_scores[u % 2], key_of(layer, j, n))) * HEAD**-0.5
            into(layer, j, n * couple, part)
            part = dot_tn(grad_scores[u % 2], queries[layer, j, n])[:padded]
            into(layer, j, features + n * couple, part)

        grad_weights(0)
        for u in range(len(tasks)):
            if u + 1 < len(tasks):
                grad_weights(u + 1)
            if u:
                attention_rest(u - 1)
            else:
                sum_att[layer, :, 3 * features :] += dot_tn(attended[layer], out_low[...])
            attention_value(u)
            soften_back(u)
        attention_rest(len(tasks) - 1)

        def norm_one(j):
            one, two = (jnp.zeros((8, features), F32) for _ in range(2))
            for at, size in row_chunks(padded):
                lines = slice(j * padded + at, j * padded + at + size)
                grad = grad_norm[lines]
                dx, by_hat = norm_backward(hidden[layer, lines], grad, vec(layer, at_g1))
                one = one + fold(by_hat)
                two = two + fold(grad)
                value = grad_out[lines] + dx
                grad_out[lines] = value.astype(BF16).astype(F32)
            vec_one[layer, 32:40] += one
            vec_one[layer, 40:48] += two

        for j in range(GROUP):
            grad_norm[image[j]] = dot_nt(grad_joined[image[j]], w_qkv[layer])
        for c, columns in enumerate(spans(3 * features, 512)):
            sum_att[layer, :, columns] += dot_tn(normed[layer], grad_joined[:, columns])
            if c < GROUP:
                norm_one(c)
        for j in range(GROUP):
            leave(layer, 1, j, grad_out[j * padded : j * padded + tokens].astype(BF16))

    def store(layer, kind, target):
        stage = (wide, tall)[kind].at[layer]
        return pltpu.make_async_copy(stage, target, store_sem.at[layer, kind])

    def finish(layer):
        wide[layer, :, :units] = sum_up[layer].astype(BF16)
        wide[layer, :, units : units + 4 * features] = sum_att[layer].astype(BF16)
        line = lax.broadcasted_iota(jnp.int32, (128, features), 0)
        plain = jnp.zeros((128, features), F32)
        for n, group in enumerate((4, 5, 3, 1, 2, 0)):
            total = jnp.sum(vec_one[layer, 8 * group : 8 * group + 8], axis=0, keepdims=True)
            plain = plain + jnp.where(line == n, total, 0.0)
        qkv = jnp.sum(vec_qkv[layer], axis=0, keepdims=True)
        qv = jnp.concatenate([qkv[:, :features], qkv[:, 2 * features :]], axis=1)
        total_up = jnp.sum(vec_up[layer], axis=0, keepdims=True)
        columns = jnp.zeros((features, 128), F32)
        for first_line, total in ((0, plain), (6, qv), (8, total_up)):
            size = total.shape[1]
            each = size // features
            position = lax.broadcasted_iota(jnp.int32, (128, size), 1)
            row = lax.broadcasted_iota(jnp.int32, (128, size), 0)
            if each > 1:
                total = jnp.where(row - first_line == (position & (each - 1)), total, 0.0)
            target = lax.broadcasted_iota(jnp.int32, (features, size), 0)
            source = lax.broadcasted_iota(jnp.int32, (features, size), 1)
            inside = (source >= target * each) & (source < target * each + each)
            pick = jnp.where(inside, 1.0, 0.0).astype(BF16)
            columns = columns + dot_nt(pick, total.astype(BF16))
        wide[layer, :, units + 4 * features :] = columns.astype(BF16)

        def send(kind, mine, away):
            @pl.when(core == layer)
            def _():
                store(layer, kind, mine).start()

            @pl.when(core != layer)
            def _():
                store(layer, kind, away).start()

        send(0, mine_wide, away_wide)
        for columns in spans(units, features):
            tall[layer, columns, :] = sum_down[layer, :, columns].astype(BF16).T
        send(1, mine_tall, away_tall)

    @pl.when(jnp.logical_not(running))
    def _():
        mine_ref[...] = jnp.zeros_like(mine_ref)
        away_ref[...] = jnp.zeros_like(away_ref)

    @pl.when(running)
    def _():
        for j in range(GROUP):
            tail = slice(j * padded + padded - 16, (j + 1) * padded)
            hidden[0, tail] = jnp.zeros((16, features), F32)
            hidden[0, j * padded : j * padded + tokens] = h_ref[0, j].astype(F32)
        lax.fori_loop(0, 2, lambda layer, carry: (forward(layer), carry)[1], 0)
        for j in range(GROUP):
            keep = jnp.where(step * GROUP + j < count, 1.0, 0.0)
            tail = slice(j * padded + padded - 16, (j + 1) * padded)
            grad_out[tail] = jnp.zeros((16, features), F32)
            grad_out[j * padded : j * padded + tokens] = cot_ref[0, j].astype(F32) * keep

    @pl.when(step == 0)
    def _():
        for n in range(len(blank)):
            clear(n).wait()

    def second_half(at, carry):
        layer = 1 - at

        @pl.when(running)
        def _():
            backward(layer)

        @pl.when(step == last)
        def _():
            finish(layer)

        return carry

    lax.fori_loop(0, 2, second_half, 0)

    @pl.when(step == last)
    def _():
        for layer in range(2):
            for kind, mine in enumerate((mine_wide, mine_tall)):
                store(layer, kind, mine).wait()


def run_layers(counts, which, inputs, cotangent, vectors, weights):
    slots, tokens, features = inputs.shape[1:]
    padded = -(-tokens // 16) * 16
    keys = -(-tokens // 128) * 128
    heads = features // HEAD
    steps = slots // GROUP
    block = GROUP * padded
    units = weights[0][2].shape[2]
    packed = vectors[0].shape[1]
    wide = units + 4 * features + 128
    images = pl.BlockSpec((1, GROUP, tokens, features), lambda i, counts, which: (which[0], i, 0, 0))
    kinds = pl.BlockSpec((2, GROUP, tokens, features), lambda i, counts, which: (0, i, 0, 0))
    vector = pl.BlockSpec((1, packed), lambda i, counts, which: (0, 0))
    anywhere = pl.BlockSpec(memory_space=pl.ANY)
    both = (
        ((features, 3 * features), BF16),
        ((features, features), BF16),
        ((features, units), BF16),
        ((units, features), BF16),
        ((packed,), F32),
    )
    saved = (
        ((block, features), BF16),
        ((GROUP, heads // 2, 2 * padded, 2 * HEAD), BF16),
        ((GROUP * keys, 2 * features), BF16),
        ((GROUP, heads // 2, 2 * padded, keys), BF16),
        ((block, features), BF16),
        ((block, features), F32),
        ((block, features), BF16),
        ((block, units), BF16),
        ((block, units), BF16),
    )
    sums = (
        ((features, units), F32),
        ((features, units), F32),
        ((features, 4 * features), F32),
        ((48, features), F32),
        ((8, units), F32),
        ((8, 3 * features), F32),
        ((features, wide), BF16),
        ((units, features), BF16),
    )

    def two(shapes):
        return [pltpu.VMEM((2,) + shape, kind) for shape, kind in shapes]

    scratch = (
        two(both)
        + [pltpu.VMEM((3, block, features), F32)]
        + two(saved)
        + [
            pltpu.VMEM((block, units), F32),
            pltpu.VMEM((block, features), F32),
            pltpu.VMEM((block, features), BF16),
            pltpu.VMEM((block, features), BF16),
            pltpu.VMEM((GROUP, heads // 2, 2 * padded, 2 * HEAD), BF16),
            pltpu.VMEM((block, units), BF16),
            pltpu.VMEM((block, 3 * features), BF16),
            pltpu.VMEM((block, features), F32),
            pltpu.VMEM((2, 2 * padded, keys), F32),
            pltpu.VMEM((2, 2 * padded, keys), BF16),
        ]
        + two(sums)
        + [pltpu.SemaphoreType.DMA((2, 4)), pltpu.SemaphoreType.DMA((2, 2))]
        + [pltpu.SemaphoreType.DMA((5,))]
    )
    return pl.pallas_call(
        lambda *refs: layers_kernel(padded, keys, *refs),
        grid_spec=pltpu.PrefetchScalarGridSpec(
            num_scalar_prefetch=2,
            grid=(steps,),
            in_specs=[images, images, vector, vector] + [anywhere] * 8,
            out_specs=[kinds, kinds] + [anywhere] * 4,
            scratch_shapes=scratch,
        ),
        out_shape=[jax.ShapeDtypeStruct((2, slots, tokens, features), BF16)] * 2
        + [jax.ShapeDtypeStruct((features, wide), BF16)] * 2
        + [jax.ShapeDtypeStruct((units, features), BF16)] * 2,
        compiler_params=pltpu.CompilerParams(
            vmem_limit_bytes=VMEM_LIMIT, dimension_semantics=("arbitrary",)
        ),
        cost_estimate=pl.CostEstimate(
            flops=80_000_000_000, bytes_accessed=30_000_000, transcendentals=0
        ),
    )(counts, which, inputs, cotangent, *vectors, *weights[0], *weights[1])


def pack_vectors(g1, b1, b_qv, *rest):
    features = g1.shape[1]
    arrays = (g1, b1, b_qv) + rest
    total = sum(a.shape[1] for a in arrays) + features

    def body(*refs):
        out = refs[-1]
        at = 0
        for n, ref in enumerate(refs[:-1]):
            if n == 2:
                out[:, at : at + features] = ref[:, :features]
                out[:, at + features : at + 2 * features] = jnp.zeros((1, features), F32)
                out[:, at + 2 * features : at + 3 * features] = ref[:, features:]
                at += 3 * features
            else:
                out[:, at : at + ref.shape[1]] = ref[...]
                at += ref.shape[1]

    return pl.pallas_call(body, out_shape=jax.ShapeDtypeStruct((1, total), F32))(*arrays)


def swap_cores(block):
    return lax.ppermute(block, "segment", [(0, 1), (1, 0)])


class Shards:
    def __init__(self, mine, got, orders, first):
        self.dp = lax.axis_size("dp")
        self.bits = self.dp.bit_length() - 1
        self.rest = (mine.shape[0] // self.dp, mine.shape[1])
        self.terms = (mine, got)
        self.orders, self.first = orders, first
        self.held = [list(range(self.bits)) for _ in orders]

    def wait_for(self, *others):
        self.terms = lax.optimization_barrier(self.terms + others)[:2]

    def begin(self, n):
        me = lax.axis_index("dp")
        self.below = [left.index(order[n]) for order, left in zip(self.orders, self.held)]
        self.bit = [(me >> order[n]) & 1 for order in self.orders]
        for order, left in zip(self.orders, self.held):
            left.remove(order[n])

    def slices(self, at, index):
        taken = []
        for term in self.terms:
            view = term.reshape((-1, 2, 1 << at) + self.rest)
            part = lax.dynamic_index_in_dim(view, index, 1, keepdims=False)
            taken.append(part.reshape((-1,) + self.rest))
        return taken

    def half(self, other):
        index = [1 - b if other else b for b in self.bit]
        below, first = self.below, self.first
        if below[0] == below[1]:
            taken = self.slices(below[0], jnp.where(first, index[0], index[1]))
        else:
            sides = zip(self.slices(below[0], index[0]), self.slices(below[1], index[1]))
            taken = [jnp.where(first, a, b) for a, b in sides]
        return sum(part.astype(F32) for part in taken).astype(BF16)

    def exchange(self, n, send):
        keep = self.half(False)
        route = [
            (core * self.dp + i, core * self.dp + (i ^ (1 << order[n])))
            for core, order in enumerate(self.orders)
            for i in range(self.dp)
        ]
        self.terms = (keep, lax.ppermute(send, ("segment", "dp"), route))

    def result(self):
        return tuple(t.reshape(self.rest) for t in self.terms)


def split_wide(terms, features, units):
    share = terms[0].shape[0]
    plain = 6

    def body(one, two, up, qkv, out, qv, bias_up, *vectors):
        total = one[...].astype(F32) + two[...].astype(F32)
        up[0] = total[:, :units]
        qkv[0] = total[:, units : units + 3 * features]
        out[0] = total[:, units + 3 * features : units + 4 * features]
        columns = total[:, units + 4 * features :]

        def spread(ref, first_column):
            size = ref.shape[1]
            width = size // share
            lane = lax.broadcasted_iota(jnp.int32, (share, size), 1)
            row = lax.broadcasted_iota(jnp.int32, (share, size), 0)
            value = jnp.zeros((share, size), F32)
            for n in range(width):
                column = columns[:, first_column + n : first_column + n + 1]
                value = value + jnp.where(lane == row * width + n, column, 0.0)
            ref[...] = jnp.sum(value, axis=0, keepdims=True)

        for n, ref in enumerate(vectors):
            spread(ref, n)
        spread(qv, plain)
        spread(bias_up, plain + 2)

    shapes = [(1, share, units), (1, share, 3 * features), (1, share, features)]
    shapes += [(1, 2 * share), (1, units // features * share)] + [(1, share)] * plain
    return pl.pallas_call(
        body, out_shape=[jax.ShapeDtypeStruct(shape, F32) for shape in shapes]
    )(*terms)


def on_device(inputs, image_count, cotangent, *params):
    dp = lax.axis_size("dp")
    core = lax.axis_index("segment")
    first = core == 0
    features = inputs.shape[3]
    g1, b1, w_qkv, b_qv, w_out, b_out, g2, b2, w_up, b_up, w_down, b_down = params
    units = w_up.shape[2]
    own_weights = (w_qkv, w_out, w_up, w_down)
    got_weights = tuple(swap_cores(w) for w in own_weights)
    own_vec = pack_vectors(g1, b1, b_qv, b_out, g2, b2, b_down, b_up)
    got_vec = swap_cores(own_vec)
    counts, which = image_count.reshape(-1), core.astype(jnp.int32).reshape(1)
    mine, away, mine_wide, away_wide, mine_tall, away_tall = run_layers(
        counts, which, inputs, cotangent, (own_vec, got_vec), (own_weights, got_weights)
    )
    got_wide = swap_cores(away_wide)
    away_tall, got_wide = lax.optimization_barrier((away_tall, got_wide))
    got_tall = swap_cores(away_tall)
    bits = list(range(dp.bit_length() - 1))
    near, far = bits[:3], bits[3:]
    plain, turned, crossed = near + far, near[2:] + near[:2] + far, near[1:] + far + near[:1]
    wide = Shards(mine_wide, got_wide, (plain, turned), first)
    tall = Shards(mine_tall, got_tall, (crossed, crossed), first)
    for n in bits:
        wide.begin(n)
        tall.begin(n)
        wide_send = wide.half(True)
        if n in (0, bits[-1]):
            tall.wait_for(wide_send)
        tall_send = tall.half(True)
        if n == 0:
            wide.wait_for(tall_send)
            away, _ = lax.optimization_barrier((away, tall_send))
            got = swap_cores(away)
            here = (lax.iota(jnp.int32, 2) == core)[:, None, None, None]
            straight = Layout(major_to_minor=(0, 1, 2, 3))
            both = [
                with_layout_constraint(jnp.where(here, a[None], b[None]), straight)
                for a, b in zip(mine, got)
            ]
        wide.exchange(n, wide_send)
        tall.exchange(n, tall_send)
        if n == 1:
            both = [
                with_layout_constraint(b.transpose(1, 2, 0, 3), straight) for b in both
            ]
        if n < 2:
            keep, arrived, *both = lax.optimization_barrier(wide.terms + tuple(both))
            wide.terms = (keep, arrived)
    both = [b.transpose(2, 0, 1, 3) for b in both]
    wide, tall = wide.result(), tall.result()
    g_up, g_qkv, g_out, g_bqv, g_bup, *vectors = split_wide(wide, features, units)
    ln1_gain, ln1_bias, g_bo, ln2_gain, ln2_bias, g_bd = vectors
    g_down = (tall[0].astype(F32) + tall[1].astype(F32))[None]
    outs = (ln1_gain, ln1_bias, g_qkv, g_bqv, g_out, g_bo, ln2_gain, ln2_bias, g_up, g_bup)
    return (both[0][None], both[1][None]) + outs + (g_down, g_bd)


def solution(mesh):
    in_specs = (
        P(None, "dp", None, None),
        P(None, "dp"),
        P(None, "dp", None, None),
        P("segment", None),
        P("segment", None),
        P("segment", None, None),
        P("segment", None),
        P("segment", None, None),
        P("segment", None),
        P("segment", None),
        P("segment", None),
        P("segment", None, None),
        P("segment", None),
        P("segment", None, None),
        P("segment", None),
    )
    out_specs = (
        P("segment", None, "dp", None, None),
        P("segment", None, "dp", None, None),
        P("segment", "dp"),
        P("segment", "dp"),
        P("segment", "dp", None),
        P("segment", "dp"),
        P("segment", "dp", None),
        P("segment", "dp"),
        P("segment", "dp"),
        P("segment", "dp"),
        P("segment", "dp", None),
        P("segment", "dp"),
        P("segment", "dp", None),
        P("segment", "dp"),
    )
    return jax.shard_map(
        on_device, mesh=mesh, in_specs=in_specs, out_specs=out_specs, check_vma=False
    )
```

```python
import jax
import jax.numpy as jnp
from jax import lax
from jax.experimental.layout import Layout, with_layout_constraint
from jax.experimental import pallas as pl
from jax.experimental.pallas import tpu as pltpu
from jax.sharding import PartitionSpec as P

HEAD = 64
EPSILON = 1e-06
BF16 = jnp.bfloat16
F32 = jnp.float32
GROUP = 2
VMEM_LIMIT = 62 * 1024 * 1024


def dot(a, b):
    return lax.dot_general(a, b, (((1,), (0,)), ((), ())), preferred_element_type=F32)


def dot_nt(a, b):
    return lax.dot_general(a, b, (((1,), (1,)), ((), ())), preferred_element_type=F32)


def dot_tn(a, b):
    return lax.dot_general(a, b, (((0,), (0,)), ((), ())), preferred_element_type=F32)


def normalized(rows):
    centered = rows - jnp.mean(rows, axis=-1, keepdims=True)
    spread = jnp.mean(centered * centered, axis=-1, keepdims=True)
    inverse = lax.rsqrt(spread + EPSILON)
    return centered * inverse, inverse


def norm_backward(rows, grad, gain):
    hat, inverse = normalized(rows)
    scaled = grad * gain
    inner = jnp.mean(scaled * hat, axis=-1, keepdims=True)
    dx = inverse * (scaled - jnp.mean(scaled, axis=-1, keepdims=True) - hat * inner)
    return dx, grad * hat


def reciprocal(x):
    guess = pl.reciprocal(x, approx=True)
    return guess * (2.0 - x * guess)


def gelu_and_slope(x):
    bell = jnp.exp(x * x * -0.5)
    t = reciprocal(1.0 + jnp.abs(x) * (0.3275911 * 0.7071067811865476))
    poly = t * (
        0.5 * 0.254829592
        + t
        * (
            0.5 * -0.284496736
            + t * (0.5 * 1.421413741 + t * (0.5 * -1.453152027 + t * (0.5 * 1.061405429)))
        )
    )
    tail = poly * bell
    cdf = jnp.where(x >= 0.0, 1.0 - tail, tail)
    return x * cdf, cdf + x * (bell * 0.3989422804014327)


def fold(rows):
    total = rows[0:8]
    for at in range(8, rows.shape[0], 8):
        total = total + rows[at : at + 8]
    return total


def row_chunks(total, size=64):
    return [(at, min(size, total - at)) for at in range(0, total, size)]


def spans(total, width):
    return [slice(at, min(at + width, total)) for at in range(0, total, width)]


def layers_kernel(
    padded,
    keys,
    counts,
    which,
    h_ref,
    cot_ref,
    own_vec,
    got_vec,
    own_qkv,
    own_out,
    own_up,
    own_down,
    got_qkv,
    got_out,
    got_up,
    got_down,
    mine_ref,
    away_ref,
    mine_wide,
    away_wide,
    mine_tall,
    away_tall,
    w_qkv,
    w_out,
    w_up,
    w_down,
    vecs,
    hidden,
    normed,
    queries,
    kv,
    weights,
    attended,
    middle,
    second,
    active,
    slope,
    before,
    grad_out,
    grad_low,
    out_low,
    grad_heads,
    grad_before,
    grad_joined,
    grad_norm,
    scores,
    grad_scores,
    sum_up,
    sum_down,
    sum_att,
    vec_one,
    vec_up,
    vec_qkv,
    wide,
    tall,
    load_sem,
    store_sem,
):
    step = pl.program_id(0)
    last = pl.num_programs(0) - 1
    core = which[0]
    count = counts[core]
    running = step * GROUP < count
    tokens, features = h_ref.shape[2:]
    heads = features // HEAD
    rows = GROUP * padded
    units = w_up.shape[2]
    couple = 2 * HEAD
    own = (own_qkv, own_out, own_up, own_down)
    got = (got_qkv, got_out, got_up, got_down)
    held = (w_qkv, w_out, w_up, w_down)
    at_g1, at_b1, at_qkv = 0, features, 2 * features
    at_bo, at_g2, at_b2, at_bd, at_up = (n * features for n in (5, 6, 7, 8, 9))

    def vec(layer, at, size=features):
        return vecs[pl.ds(layer, 1), at : at + size]

    def load(source, n, layer):
        return pltpu.make_async_copy(source[n].at[0], held[n].at[layer], load_sem.at[layer, n])

    @pl.when(step == 0)
    def _():
        for layer in range(2):
            for n in range(4):

                @pl.when(core == layer)
                def _():
                    load(own, n, layer).start()

                @pl.when(core != layer)
                def _():
                    load(got, n, layer).start()

        for layer in range(2):
            mine = jnp.full(own_vec.shape, core == layer)
            vecs[layer : layer + 1] = jnp.where(mine, own_vec[...], got_vec[...])
        for ref in (sum_up, sum_down, sum_att, vec_one, vec_up, vec_qkv):
            for layer in range(2):
                ref[layer] = jnp.zeros(ref.shape[1:], F32)
        for layer in range(2):
            for j in range(GROUP):
                kv[layer, j * keys + padded : (j + 1) * keys] = jnp.zeros(
                    (keys - padded, 2 * features), BF16
                )

    def leave(layer, kind, j, value):
        @pl.when(core == layer)
        def _():
            mine_ref[kind, j] = value

        @pl.when(core != layer)
        def _():
            away_ref[kind, j] = value

    lane = lax.broadcasted_iota(jnp.int32, (padded, couple), 1)
    left = lane < HEAD
    image = [slice(j * padded, (j + 1) * padded) for j in range(GROUP)]
    images_keys = [slice(j * keys, (j + 1) * keys) for j in range(GROUP)]
    pairs = [slice(n * couple, (n + 1) * couple) for n in range(heads // 2)]
    tasks = [(j, n) for j in range(GROUP) for n in range(heads // 2)]
    chunks = spans(units, 512)

    def stacked(value):
        nothing = jnp.zeros_like(value)
        return jnp.where(left, value, nothing), jnp.where(left, nothing, value)

    def key_of(layer, j, n):
        return kv[layer, images_keys[j], pairs[n]]

    def value_of(layer, j, n):
        at = features + n * couple
        return kv[layer, images_keys[j], at : at + couple]

    def unstacked(value):
        return jnp.where(left, value[:padded], value[padded:])

    def forward(layer):
        @pl.when(step == 0)
        def _():
            for n in range(2):
                load(own, n, layer).wait()

        for at, size in row_chunks(rows):
            hat, _ = normalized(hidden[layer, at : at + size])
            value = hat * vec(layer, at_g1) + vec(layer, at_b1)
            normed[layer, at : at + size] = value.astype(BF16)
        value = dot(normed[layer], w_qkv[layer, :, :features]) + vec(layer, at_qkv)
        value = value.astype(BF16) * jnp.asarray(HEAD**-0.5, BF16)
        for j, n in tasks:
            for half, part in enumerate(stacked(value[image[j], pairs[n]])):
                queries[layer, j, n, half * padded : (half + 1) * padded] = part
        for columns in spans(2 * features, 512):
            at, size = features + columns.start, columns.stop - columns.start
            value = dot(normed[layer], w_qkv[layer, :, at : at + size])
            value = (value + vec(layer, at_qkv + at, size)).astype(BF16)
            for j in range(GROUP):
                kv[layer, j * keys : j * keys + padded, columns] = value[image[j]]

        def score(u):
            j, n = tasks[u]
            scores[u % 2] = dot_nt(queries[layer, j, n], key_of(layer, j, n))

        def soften(u):
            j, n = tasks[u]
            for at, size in row_chunks(2 * padded):
                real = lax.broadcasted_iota(jnp.int32, (size, keys), 1) < tokens
                s = jnp.where(real, scores[u % 2, at : at + size], -1e30)
                e = jnp.exp(s - jnp.max(s, axis=-1, keepdims=True))
                p = e * reciprocal(jnp.sum(e, axis=-1, keepdims=True))
                weights[layer, j, n, at : at + size] = p.astype(BF16)

        def attend(u):
            j, n = tasks[u]
            value = unstacked(dot(weights[layer, j, n], value_of(layer, j, n)))
            attended[layer, image[j], pairs[n]] = value.astype(BF16)

        def project(j):
            middle[layer, image[j]] = dot(attended[layer, image[j]], w_out[layer])

        def norm_two(j):
            for at, size in row_chunks(padded):
                at = j * padded + at
                value = middle[layer, at : at + size] + hidden[layer, at : at + size]
                value = value + vec(layer, at_bo)
                middle[layer, at : at + size] = value
                hat, _ = normalized(value)
                value = hat * vec(layer, at_g2) + vec(layer, at_b2)
                second[layer, at : at + size] = value.astype(BF16)

        score(0)
        for u in range(len(tasks)):
            if u + 1 < len(tasks):
                score(u + 1)
            if u:
                attend(u - 1)
                if tasks[u - 1][1] == heads // 2 - 1:
                    project(tasks[u - 1][0])
            soften(u)
            if u and tasks[u - 1][1] == heads // 2 - 1:
                norm_two(tasks[u - 1][0])
        attend(len(tasks) - 1)
        project(GROUP - 1)
        norm_two(GROUP - 1)

        @pl.when(step == 0)
        def _():
            for n in range(2, 4):
                load(own, n, layer).wait()

        def up(c):
            before[:, chunks[c]] = dot(second[layer], w_up[layer, :, chunks[c]])

        def curve(c):
            columns = chunks[c]
            for at, size in row_chunks(rows, 16):
                value, change = gelu_and_slope(
                    before[at : at + size, columns]
                    + vec(layer, at_up + columns.start, columns.stop - columns.start)
                )
                active[layer, at : at + size, columns] = value.astype(BF16)
                slope[layer, at : at + size, columns] = change.astype(BF16)

        def down(c):
            value = dot(active[layer, :, chunks[c]], w_down[layer, chunks[c]])
            if c:
                value = value + grad_norm[...]
            grad_norm[...] = value

        up(0)
        for c in range(len(chunks)):
            if c + 1 < len(chunks):
                up(c + 1)
            if c:
                down(c - 1)
            curve(c)
        down(len(chunks) - 1)
        for j in range(GROUP):
            keep = jnp.where(step * GROUP + j < count, 1.0, 0.0)
            result = grad_norm[image[j]] + middle[layer, image[j]]
            result = ((result + vec(layer, at_bd)) * keep).astype(BF16)
            leave(layer, 0, j, result[:tokens])
            hidden[layer + 1, image[j]] = result.astype(F32)

    def backward(layer):
        for at, size in row_chunks(rows):
            value = grad_out[at : at + size]
            grad_low[at : at + size] = value.astype(BF16)
            vec_one[layer, 0:8] += fold(value)

        def activation(c):
            before[:, chunks[c]] = dot_nt(grad_low[...], w_down[layer, chunks[c]])

        def multiply(c):
            columns = chunks[c]
            total = jnp.zeros((8, columns.stop - columns.start), F32)
            for at, size in row_chunks(rows, 16):
                lines = slice(at, at + size)
                piece = before[lines, columns] * slope[layer, lines, columns].astype(F32)
                piece = piece.astype(BF16)
                grad_before[lines, columns] = piece
                total = total + fold(piece.astype(F32))
            vec_up[layer, :, columns] += total

        activation(0)
        for c in range(len(chunks)):
            if c + 1 < len(chunks):
                activation(c + 1)
            sum_down[layer, :, chunks[c]] += dot_tn(grad_low[...], active[layer, :, chunks[c]])
            multiply(c)

        def norm_two(j):
            one, two, three = (jnp.zeros((8, features), F32) for _ in range(3))
            for at, size in row_chunks(padded):
                lines = slice(j * padded + at, j * padded + at + size)
                grad = grad_norm[lines]
                dx, by_hat = norm_backward(middle[layer, lines], grad, vec(layer, at_g2))
                one = one + fold(by_hat)
                two = two + fold(grad)
                value = grad_out[lines] + dx
                grad_out[lines] = value
                value = value.astype(BF16)
                out_low[lines] = value
                three = three + fold(value.astype(F32))
            vec_one[layer, 8:16] += one
            vec_one[layer, 16:24] += two
            vec_one[layer, 24:32] += three

        for j in range(GROUP):
            grad_norm[image[j]] = dot_nt(grad_before[image[j]], w_up[layer])
        for c in range(len(chunks)):
            sum_up[layer, :, chunks[c]] += dot_tn(second[layer], grad_before[:, chunks[c]])
            if c < GROUP:
                norm_two(c)
        for j in range(GROUP):
            value = dot_nt(out_low[image[j]], w_out[layer]).astype(BF16)
            for n in range(heads // 2):
                for half, part in enumerate(stacked(value[:, pairs[n]])):
                    grad_heads[j, n, half * padded : (half + 1) * padded] = part

        def grad_weights(u):
            j, n = tasks[u]
            scores[u % 2] = dot_nt(grad_heads[j, n], value_of(layer, j, n))

        def soften_back(u):
            j, n = tasks[u]
            for at, size in row_chunks(2 * padded):
                p = weights[layer, j, n, at : at + size].astype(F32)
                by = p * scores[u % 2, at : at + size]
                by = by - p * jnp.sum(by, axis=-1, keepdims=True)
                grad_scores[u % 2, at : at + size] = by.astype(BF16)

        def into(layer, j, column, part):
            part = part.astype(BF16)
            grad_joined[image[j], column : column + couple] = part
            vec_qkv[layer, :, column : column + couple] += fold(part.astype(F32))

        def attention_value(u):
            j, n = tasks[u]
            part = dot_tn(weights[layer, j, n], grad_heads[j, n])[:padded]
            into(layer, j, 2 * features + n * couple, part)

        def attention_rest(u):
            j, n = tasks[u]
            part = unstacked(dot(grad_scores[u % 2], key_of(layer, j, n))) * HEAD**-0.5
            into(layer, j, n * couple, part)
            part = dot_tn(grad_scores[u % 2], queries[layer, j, n])[:padded]
            into(layer, j, features + n * couple, part)

        grad_weights(0)
        for u in range(len(tasks)):
            if u + 1 < len(tasks):
                grad_weights(u + 1)
            if u:
                attention_rest(u - 1)
            else:
                sum_att[layer, :, 3 * features :] += dot_tn(attended[layer], out_low[...])
            attention_value(u)
            soften_back(u)
        attention_rest(len(tasks) - 1)

        def norm_one(j):
            one, two = (jnp.zeros((8, features), F32) for _ in range(2))
            for at, size in row_chunks(padded):
                lines = slice(j * padded + at, j * padded + at + size)
                grad = grad_norm[lines]
                dx, by_hat = norm_backward(hidden[layer, lines], grad, vec(layer, at_g1))
                one = one + fold(by_hat)
                two = two + fold(grad)
                value = grad_out[lines] + dx
                grad_out[lines] = value.astype(BF16).astype(F32)
            vec_one[layer, 32:40] += one
            vec_one[layer, 40:48] += two

        for j in range(GROUP):
            grad_norm[image[j]] = dot_nt(grad_joined[image[j]], w_qkv[layer])
        for c, columns in enumerate(spans(3 * features, 512)):
            sum_att[layer, :, columns] += dot_tn(normed[layer], grad_joined[:, columns])
            if c < GROUP:
                norm_one(c)
        for j in range(GROUP):
            leave(layer, 1, j, grad_out[j * padded : j * padded + tokens].astype(BF16))

    def store(layer, kind, target):
        stage = (wide, tall)[kind].at[layer]
        return pltpu.make_async_copy(stage, target, store_sem.at[layer, kind])

    def finish(layer):
        wide[layer, :, :units] = sum_up[layer].astype(BF16)
        wide[layer, :, units : units + 4 * features] = sum_att[layer].astype(BF16)
        line = lax.broadcasted_iota(jnp.int32, (128, features), 0)
        plain = jnp.zeros((128, features), F32)
        for n, group in enumerate((4, 5, 3, 1, 2, 0)):
            total = jnp.sum(vec_one[layer, 8 * group : 8 * group + 8], axis=0, keepdims=True)
            plain = plain + jnp.where(line == n, total, 0.0)
        qkv = jnp.sum(vec_qkv[layer], axis=0, keepdims=True)
        qv = jnp.concatenate([qkv[:, :features], qkv[:, 2 * features :]], axis=1)
        total_up = jnp.sum(vec_up[layer], axis=0, keepdims=True)
        columns = jnp.zeros((features, 128), F32)
        for first_line, total in ((0, plain), (6, qv), (8, total_up)):
            size = total.shape[1]
            each = size // features
            position = lax.broadcasted_iota(jnp.int32, (128, size), 1)
            row = lax.broadcasted_iota(jnp.int32, (128, size), 0)
            if each > 1:
                total = jnp.where(row - first_line == (position & (each - 1)), total, 0.0)
            target = lax.broadcasted_iota(jnp.int32, (features, size), 0)
            source = lax.broadcasted_iota(jnp.int32, (features, size), 1)
            inside = (source >= target * each) & (source < target * each + each)
            pick = jnp.where(inside, 1.0, 0.0).astype(BF16)
            columns = columns + dot_nt(pick, total.astype(BF16))
        wide[layer, :, units + 4 * features :] = columns.astype(BF16)

        def send(kind, mine, away):
            @pl.when(core == layer)
            def _():
                store(layer, kind, mine).start()

            @pl.when(core != layer)
            def _():
                store(layer, kind, away).start()

        send(0, mine_wide, away_wide)
        for columns in spans(units, features):
            tall[layer, columns, :] = sum_down[layer, :, columns].astype(BF16).T
        send(1, mine_tall, away_tall)

    @pl.when(jnp.logical_not(running))
    def _():
        mine_ref[...] = jnp.zeros_like(mine_ref)
        away_ref[...] = jnp.zeros_like(away_ref)

    @pl.when(running)
    def _():
        for j in range(GROUP):
            tail = slice(j * padded + padded - 16, (j + 1) * padded)
            hidden[0, tail] = jnp.zeros((16, features), F32)
            hidden[0, j * padded : j * padded + tokens] = h_ref[0, j].astype(F32)
        lax.fori_loop(0, 2, lambda layer, carry: (forward(layer), carry)[1], 0)
        for j in range(GROUP):
            keep = jnp.where(step * GROUP + j < count, 1.0, 0.0)
            tail = slice(j * padded + padded - 16, (j + 1) * padded)
            grad_out[tail] = jnp.zeros((16, features), F32)
            grad_out[j * padded : j * padded + tokens] = cot_ref[0, j].astype(F32) * keep

    def second_half(at, carry):
        layer = 1 - at

        @pl.when(running)
        def _():
            backward(layer)

        @pl.when(step == last)
        def _():
            finish(layer)

        return carry

    lax.fori_loop(0, 2, second_half, 0)

    @pl.when(step == last)
    def _():
        for layer in range(2):
            for kind, mine in enumerate((mine_wide, mine_tall)):
                store(layer, kind, mine).wait()


def run_layers(counts, which, inputs, cotangent, vectors, weights):
    slots, tokens, features = inputs.shape[1:]
    padded = -(-tokens // 16) * 16
    keys = -(-tokens // 128) * 128
    heads = features // HEAD
    steps = slots // GROUP
    block = GROUP * padded
    units = weights[0][2].shape[2]
    packed = vectors[0].shape[1]
    wide = units + 4 * features + 128
    images = pl.BlockSpec((1, GROUP, tokens, features), lambda i, counts, which: (which[0], i, 0, 0))
    kinds = pl.BlockSpec((2, GROUP, tokens, features), lambda i, counts, which: (0, i, 0, 0))
    vector = pl.BlockSpec((1, packed), lambda i, counts, which: (0, 0))
    anywhere = pl.BlockSpec(memory_space=pl.ANY)
    both = (
        ((features, 3 * features), BF16),
        ((features, features), BF16),
        ((features, units), BF16),
        ((units, features), BF16),
        ((packed,), F32),
    )
    saved = (
        ((block, features), BF16),
        ((GROUP, heads // 2, 2 * padded, 2 * HEAD), BF16),
        ((GROUP * keys, 2 * features), BF16),
        ((GROUP, heads // 2, 2 * padded, keys), BF16),
        ((block, features), BF16),
        ((block, features), F32),
        ((block, features), BF16),
        ((block, units), BF16),
        ((block, units), BF16),
    )
    sums = (
        ((features, units), F32),
        ((features, units), F32),
        ((features, 4 * features), F32),
        ((48, features), F32),
        ((8, units), F32),
        ((8, 3 * features), F32),
        ((features, wide), BF16),
        ((units, features), BF16),
    )

    def two(shapes):
        return [pltpu.VMEM((2,) + shape, kind) for shape, kind in shapes]

    scratch = (
        two(both)
        + [pltpu.VMEM((3, block, features), F32)]
        + two(saved)
        + [
            pltpu.VMEM((block, units), F32),
            pltpu.VMEM((block, features), F32),
            pltpu.VMEM((block, features), BF16),
            pltpu.VMEM((block, features), BF16),
            pltpu.VMEM((GROUP, heads // 2, 2 * padded, 2 * HEAD), BF16),
            pltpu.VMEM((block, units), BF16),
            pltpu.VMEM((block, 3 * features), BF16),
            pltpu.VMEM((block, features), F32),
            pltpu.VMEM((2, 2 * padded, keys), F32),
            pltpu.VMEM((2, 2 * padded, keys), BF16),
        ]
        + two(sums)
        + [pltpu.SemaphoreType.DMA((2, 4)), pltpu.SemaphoreType.DMA((2, 2))]
    )
    return pl.pallas_call(
        lambda *refs: layers_kernel(padded, keys, *refs),
        grid_spec=pltpu.PrefetchScalarGridSpec(
            num_scalar_prefetch=2,
            grid=(steps,),
            in_specs=[images, images, vector, vector] + [anywhere] * 8,
            out_specs=[kinds, kinds] + [anywhere] * 4,
            scratch_shapes=scratch,
        ),
        out_shape=[jax.ShapeDtypeStruct((2, slots, tokens, features), BF16)] * 2
        + [jax.ShapeDtypeStruct((features, wide), BF16)] * 2
        + [jax.ShapeDtypeStruct((units, features), BF16)] * 2,
        compiler_params=pltpu.CompilerParams(
            vmem_limit_bytes=VMEM_LIMIT, dimension_semantics=("arbitrary",)
        ),
        cost_estimate=pl.CostEstimate(
            flops=80_000_000_000, bytes_accessed=30_000_000, transcendentals=0
        ),
    )(counts, which, inputs, cotangent, *vectors, *weights[0], *weights[1])


def pack_vectors(g1, b1, b_qv, *rest):
    features = g1.shape[1]
    arrays = (g1, b1, b_qv) + rest
    total = sum(a.shape[1] for a in arrays) + features

    def body(*refs):
        out = refs[-1]
        at = 0
        for n, ref in enumerate(refs[:-1]):
            if n == 2:
                out[:, at : at + features] = ref[:, :features]
                out[:, at + features : at + 2 * features] = jnp.zeros((1, features), F32)
                out[:, at + 2 * features : at + 3 * features] = ref[:, features:]
                at += 3 * features
            else:
                out[:, at : at + ref.shape[1]] = ref[...]
                at += ref.shape[1]

    return pl.pallas_call(body, out_shape=jax.ShapeDtypeStruct((1, total), F32))(*arrays)


def swap_cores(block):
    return lax.ppermute(block, "segment", [(0, 1), (1, 0)])


class Shards:
    def __init__(self, mine, got, orders, first):
        self.dp = lax.axis_size("dp")
        self.bits = self.dp.bit_length() - 1
        self.rest = (mine.shape[0] // self.dp, mine.shape[1])
        self.terms = (mine, got)
        self.orders, self.first = orders, first
        self.held = [list(range(self.bits)) for _ in orders]

    def wait_for(self, *others):
        self.terms = lax.optimization_barrier(self.terms + others)[:2]

    def begin(self, n):
        me = lax.axis_index("dp")
        self.below = [left.index(order[n]) for order, left in zip(self.orders, self.held)]
        self.bit = [(me >> order[n]) & 1 for order in self.orders]
        for order, left in zip(self.orders, self.held):
            left.remove(order[n])

    def slices(self, at, index):
        taken = []
        for term in self.terms:
            view = term.reshape((-1, 2, 1 << at) + self.rest)
            part = lax.dynamic_index_in_dim(view, index, 1, keepdims=False)
            taken.append(part.reshape((-1,) + self.rest))
        return taken

    def half(self, other):
        index = [1 - b if other else b for b in self.bit]
        below, first = self.below, self.first
        if below[0] == below[1]:
            taken = self.slices(below[0], jnp.where(first, index[0], index[1]))
        else:
            sides = zip(self.slices(below[0], index[0]), self.slices(below[1], index[1]))
            taken = [jnp.where(first, a, b) for a, b in sides]
        return sum(part.astype(F32) for part in taken).astype(BF16)

    def exchange(self, n, send):
        keep = self.half(False)
        route = [
            (core * self.dp + i, core * self.dp + (i ^ (1 << order[n])))
            for core, order in enumerate(self.orders)
            for i in range(self.dp)
        ]
        self.terms = (keep, lax.ppermute(send, ("segment", "dp"), route))

    def result(self):
        return tuple(t.reshape(self.rest) for t in self.terms)


def split_wide(terms, features, units):
    share = terms[0].shape[0]
    plain = 6

    def body(one, two, up, qkv, out, qv, bias_up, *vectors):
        total = one[...].astype(F32) + two[...].astype(F32)
        up[0] = total[:, :units]
        qkv[0] = total[:, units : units + 3 * features]
        out[0] = total[:, units + 3 * features : units + 4 * features]
        columns = total[:, units + 4 * features :]

        def spread(ref, first_column):
            size = ref.shape[1]
            width = size // share
            lane = lax.broadcasted_iota(jnp.int32, (share, size), 1)
            row = lax.broadcasted_iota(jnp.int32, (share, size), 0)
            value = jnp.zeros((share, size), F32)
            for n in range(width):
                column = columns[:, first_column + n : first_column + n + 1]
                value = value + jnp.where(lane == row * width + n, column, 0.0)
            ref[...] = jnp.sum(value, axis=0, keepdims=True)

        for n, ref in enumerate(vectors):
            spread(ref, n)
        spread(qv, plain)
        spread(bias_up, plain + 2)

    shapes = [(1, share, units), (1, share, 3 * features), (1, share, features)]
    shapes += [(1, 2 * share), (1, units // features * share)] + [(1, share)] * plain
    return pl.pallas_call(
        body, out_shape=[jax.ShapeDtypeStruct(shape, F32) for shape in shapes]
    )(*terms)


def on_device(inputs, image_count, cotangent, *params):
    dp = lax.axis_size("dp")
    core = lax.axis_index("segment")
    first = core == 0
    features = inputs.shape[3]
    g1, b1, w_qkv, b_qv, w_out, b_out, g2, b2, w_up, b_up, w_down, b_down = params
    units = w_up.shape[2]
    own_weights = (w_qkv, w_out, w_up, w_down)
    got_weights = tuple(swap_cores(w) for w in own_weights)
    own_vec = pack_vectors(g1, b1, b_qv, b_out, g2, b2, b_down, b_up)
    got_vec = swap_cores(own_vec)
    counts, which = image_count.reshape(-1), core.astype(jnp.int32).reshape(1)
    mine, away, mine_wide, away_wide, mine_tall, away_tall = run_layers(
        counts, which, inputs, cotangent, (own_vec, got_vec), (own_weights, got_weights)
    )
    got_wide = swap_cores(away_wide)
    away_tall, got_wide = lax.optimization_barrier((away_tall, got_wide))
    got_tall = swap_cores(away_tall)
    bits = list(range(dp.bit_length() - 1))
    near, far = bits[:3], bits[3:]
    plain = near[:1] + near[2:] + near[1:2] + far
    turned = near[2:] + near[1:2] + near[:1] + far
    crossed = near[1:2] + near[:1] + far + near[2:]
    wide = Shards(mine_wide, got_wide, (plain, turned), first)
    tall = Shards(mine_tall, got_tall, (crossed, crossed), first)
    for n in bits:
        wide.begin(n)
        tall.begin(n)
        wide_send = wide.half(True)
        if n in (0, bits[-1]):
            tall.wait_for(wide_send)
        tall_send = tall.half(True)
        if n == 0:
            wide.wait_for(tall_send)
            away, _ = lax.optimization_barrier((away, tall_send))
            got = swap_cores(away)
            here = (lax.iota(jnp.int32, 2) == core)[:, None, None, None]
            straight = Layout(major_to_minor=(0, 1, 2, 3))
            both = [
                with_layout_constraint(jnp.where(here, a[None], b[None]), straight)
                for a, b in zip(mine, got)
            ]
        wide.exchange(n, wide_send)
        tall.exchange(n, tall_send)
        if n == 1:
            both = [
                with_layout_constraint(b.transpose(1, 2, 0, 3), straight) for b in both
            ]
        if n < 2:
            keep, arrived, *both = lax.optimization_barrier(wide.terms + tuple(both))
            wide.terms = (keep, arrived)
    both = [b.transpose(2, 0, 1, 3) for b in both]
    wide, tall = wide.result(), tall.result()
    g_up, g_qkv, g_out, g_bqv, g_bup, *vectors = split_wide(wide, features, units)
    ln1_gain, ln1_bias, g_bo, ln2_gain, ln2_bias, g_bd = vectors
    g_down = (tall[0].astype(F32) + tall[1].astype(F32))[None]
    outs = (ln1_gain, ln1_bias, g_qkv, g_bqv, g_out, g_bo, ln2_gain, ln2_bias, g_up, g_bup)
    return (both[0][None], both[1][None]) + outs + (g_down, g_bd)


def solution(mesh):
    in_specs = (
        P(None, "dp", None, None),
        P(None, "dp"),
        P(None, "dp", None, None),
        P("segment", None),
        P("segment", None),
        P("segment", None, None),
        P("segment", None),
        P("segment", None, None),
        P("segment", None),
        P("segment", None),
        P("segment", None),
        P("segment", None, None),
        P("segment", None),
        P("segment", None, None),
        P("segment", None),
    )
    out_specs = (
        P("segment", None, "dp", None, None),
        P("segment", None, "dp", None, None),
        P("segment", "dp"),
        P("segment", "dp"),
        P("segment", "dp", None),
        P("segment", "dp"),
        P("segment", "dp", None),
        P("segment", "dp"),
        P("segment", "dp"),
        P("segment", "dp"),
        P("segment", "dp", None),
        P("segment", "dp"),
        P("segment", "dp", None),
        P("segment", "dp"),
    )
    return jax.shard_map(
        on_device, mesh=mesh, in_specs=in_specs, out_specs=out_specs, check_vma=False
    )
```
